256 devices in a mesh: rx: 128 (over y, x_lo, z, core), win: 2 (over x_hi).
Axes of the slice: x: 4 (x_hi: 2, x_lo: 2; x = x_hi * 2 + x_lo), y: 4, z: 8, core: 2. Of those that a mesh axis runs over, the one named last changes fastest.
Arguments:
- spectra: bfloat16 [16, 16384, 512], P('win', 'rx'), may hold values from -6 to 6
- plan: int32 [2], replicated, may hold values from 0 to 127
- mask: int32 [2, 128, 16384], P(None, 'win', 'rx'), may hold values 0 or 1
Outputs:
- stacks: bfloat16 [2, 128, 16384, 256], P(None, 'win', 'rx')
The draws below stay inside these ranges and needn't reach their ends.
Inputs may be any that keep to these rules, and one draw needn't show every extreme that they name: plan holds rx indices.
All inputs are finite; a program needn't handle non-finite values. No bound on the sum of `mask` on one device may be relied on, other than what follows from the above.
Results may differ from the reference program's by a relative error of at most 0.0054.
Values may be sent and summed in bfloat16 or wider, within the bound.
A program may use at most 192 MiB of HBM per device.

```python
import math
import jax
import jax.numpy as jnp
from jax import lax

CH_DEV = 128
NF = 256
LAGS = 256
SAMPLES = 15000
BIN0 = 12
STEPS = 2
WINDOWS = 16
C = 16384
N_RX = 128


def with_ends(values, rng, smallest, largest):
    longest = values.shape.index(max(values.shape))
    spots = []
    for shift in (0, 1):
        where = [jax.random.randint(jax.random.fold_in(rng, axis), (), 0, length) for axis, length in enumerate(values.shape)]
        where[longest] = (where[longest] + shift) % values.shape[longest]
        spots.append(tuple(where))
    return values.at[spots[0]].set(smallest).at[spots[1]].set(largest)


def steps_of(stream_key, extent, split, least, high):
    gain = 1.0
    for dim, blocks in split:
        heights = jax.random.uniform(jax.random.fold_in(jax.random.fold_in(stream_key, 6), dim), (blocks,), jnp.float32, least / len(split), high / len(split))
        gain = gain * jnp.repeat(jnp.exp(heights), extent[dim] // blocks).reshape((-1,) + (1,) * (len(extent) - 1 - dim))
    return gain


def noise(key, dims, width, reach, split=(), kind=jnp.bfloat16):
    entries = width * jax.random.normal(key, dims, jnp.float32)
    if split:
        entries = entries * steps_of(key, dims, split, -0.22, 0.18)
    return jnp.clip(entries, -reach, reach).astype(kind)


def setup_inputs(seed: int = 0) -> dict:
    arg_keys = jax.random.split(jax.random.key(seed), 4)
    return {
        "spectra": noise(arg_keys[0], (WINDOWS, C, 2 * NF), 1.0, 6.0, ((0, 2), (1, 128))),
        "plan": jax.random.randint(arg_keys[1], (STEPS,), 0, N_RX).astype(jnp.int32),
        "mask": with_ends((jax.random.randint(arg_keys[2], (STEPS, CH_DEV, C), 0, 4) < 3).astype(jnp.int32), jax.random.fold_in(arg_keys[2], 1), 0, 1),
    }


def lag_table(freq, lags):
    bins = BIN0 + jnp.arange(freq, dtype=jnp.int32)
    shifts = jnp.arange(lags, dtype=jnp.int32) - lags // 2
    product = jnp.mod(bins[:, None] * shifts[None, :], SAMPLES)
    theta = 2.0 * math.pi * product.astype(jnp.float32) / SAMPLES
    scale = 1.0 / math.sqrt(freq)
    return jnp.concatenate([jnp.cos(theta) * scale, -jnp.sin(theta) * scale], 0).astype(jnp.bfloat16)

def correlate(sources, block, table):
    freq = table.shape[0] // 2
    count = sources.shape[0]
    src = sources.astype(jnp.float32)
    rec = block.astype(jnp.float32)
    sr, si = (src[..., :freq], src[..., freq:])
    rr, ri = (rec[..., :freq], rec[..., freq:])
    real = (jnp.einsum('wsf,wrf->srf', sr, rr) + jnp.einsum('wsf,wrf->srf', si, ri)) / count
    imag = (jnp.einsum('wsf,wrf->srf', si, rr) - jnp.einsum('wsf,wrf->srf', sr, ri)) / count
    stacked = jnp.concatenate([real, imag], -1).astype(jnp.bfloat16)
    flat = stacked.reshape(-1, 2 * freq)
    return jnp.dot(flat, table, preferred_element_type=jnp.float32).reshape(stacked.shape[0], stacked.shape[1], -1)

def reference(spectra, plan, mask):
    table = lag_table(NF, LAGS)
    blocks = spectra.reshape(WINDOWS, N_RX, CH_DEV, 2 * NF).transpose(1, 0, 2, 3)
    results = []
    for step in range(STEPS):
        start = (plan[step] * CH_DEV).astype(jnp.int32)
        sources = lax.dynamic_slice_in_dim(spectra, start, CH_DEV, 1)
        masks = mask[step].reshape(CH_DEV, N_RX, CH_DEV).transpose(1, 0, 2)

        def one(pair):
            block, keep = pair
            lagged = correlate(sources, block, table)
            return (lagged * keep.astype(jnp.float32)[..., None]).astype(jnp.bfloat16)
        parts = lax.map(one, (blocks, masks))
        results.append(parts.transpose(1, 0, 2, 3).reshape(CH_DEV, C, LAGS))
    return jnp.stack(results, 0)
```

```python
import math

import jax
import jax.numpy as jnp
import numpy as np
from jax import lax
from jax.experimental import pallas as pl
from jax.experimental.pallas import tpu as pltpu
from jax.sharding import PartitionSpec as P

LAGS = 256
SAMPLES = 15000
BIN0 = 12
NF = 256
WINDOWS = 16
CH = 128
HALF = 64
GROUPS = 32
MESH = pl.DeviceIdType.MESH
NY, NZ = 4, 8
BATCH = 8
BUFFERS = 2 * BATCH


def table_transposed():
    bins = BIN0 + np.arange(NF)
    shifts = np.arange(LAGS) - LAGS // 2
    theta = 2.0 * math.pi * np.mod(bins[:, None] * shifts[None, :], SAMPLES) / SAMPLES
    scale = 1.0 / math.sqrt(NF)
    table = np.concatenate([np.cos(theta) * scale, -np.sin(theta) * scale], 0)
    table = table.astype(np.float32).astype(jnp.bfloat16).astype(np.float32)
    return np.ascontiguousarray((table / WINDOWS).T).astype(jnp.bfloat16)


def owner_of(plan_ref, block):
    rx = plan_ref[block]
    return rx // 32, (rx // 16) % 2, (rx // 2) % NZ, rx % 2


def spread_kernel(
    plan_ref, spec_ref, cross,
    near, far, from_y, relay_p, relay_m, to_core, from_core, to_z, from_z, relay_z, to_x, from_x,
    gathered, transit_p, transit_m, weights, sources,
    in_sem, y_send, y_recv, relay_sems, core_sems, z_send, z_recv, zr_sems, x_send, x_recv,
    gy_send, gy_recv, ring_send, ring_recv, gc_send, gc_recv,
    hop1_send, hop1_recv, hop2_send, hop2_recv,
):
    rx, win = lax.axis_index("rx"), lax.axis_index("win")
    core, z, x_lo, y = rx % 2, (rx // 2) % NZ, (rx // 16) % 2, rx // 32

    def at(y_=y, x_=x_lo, z_=z, core_=core, win_=win):
        return {"rx": ((y_ * 2 + x_) * NZ + z_) * 2 + core_, "win": win_}

    def remote(src, dst, send, recv, device):
        return pltpu.make_async_remote_copy(
            src_ref=src, dst_ref=dst, send_sem=send, recv_sem=recv, device_id=device, device_id_type=MESH
        )

    def arrived(ref, recv):
        remote(ref, ref, recv, recv, at()).wait_recv()

    load = pltpu.make_async_copy(spec_ref, near, in_sem)
    load.start()

    plus = at(x_=1 - x_lo, win_=(win + x_lo) % 2)
    minus = at(x_=1 - x_lo, win_=(win + 1 - x_lo) % 2)
    ys = [(y + d) % NY for d in range(1, NY)]
    zs = [(z + d) % NZ for d in range(1, NZ)]
    peers = [at(y_=v) for v in ys] + [at(z_=v) for v in zs] + [at(core_=1 - core)]
    peers += [plus, minus, at(win_=1 - win)]
    barrier = pltpu.get_barrier_semaphore()
    for peer in peers:
        pl.semaphore_signal(barrier, inc=1, device_id=peer, device_id_type=MESH)
    pl.semaphore_wait(barrier, len(peers))

    sent = []

    def go(copy):
        copy.start()
        sent.append(copy)

    next_y, across, last_y = ys
    go(remote(spec_ref.at[0:4, :, across], relay_p, relay_sems.at[0], relay_sems.at[1], at(y_=next_y)))
    go(remote(spec_ref.at[4:8, :, across], relay_m, relay_sems.at[2], relay_sems.at[3], at(y_=last_y)))
    go(remote(spec_ref.at[:, :, next_y], from_y.at[y], y_send.at[0], y_recv.at[0], at(y_=next_y)))
    go(remote(spec_ref.at[:, :, last_y], from_y.at[y], y_send.at[1], y_recv.at[1], at(y_=last_y)))
    for i in range(4):
        go(remote(spec_ref.at[i], transit_p.at[i], hop1_send.at[i], hop1_recv.at[i], plus))
        go(remote(spec_ref.at[4 + i], transit_m.at[i], hop1_send.at[4 + i], hop1_recv.at[4 + i], minus))

    def window_pair(ref, side):
        def body(i, carry):
            both = [
                ref[2 * i + k].reshape(CH, 2 * NF).astype(jnp.float32).T.reshape(2, GROUPS, 8, CH) for k in range(2)
            ]
            a = jnp.concatenate([both[0][0], both[1][0]], 1).astype(jnp.bfloat16)
            b = jnp.concatenate([both[0][1], both[1][1]], 1)
            minus_b = (-b).astype(jnp.bfloat16)
            b = b.astype(jnp.bfloat16)
            row = pl.multiple_of(side * CH + 16 * i, 16)
            weights[:, pl.ds(row, 16), :CH] = a
            weights[:, pl.ds(HALF + row, 16), :CH] = b
            weights[:, pl.ds(row, 16), CH:] = minus_b
            weights[:, pl.ds(HALF + row, 16), CH:] = a
            return carry

        lax.fori_loop(0, 4, body, 0)

    load.wait()
    from_y[y] = near[:, :, y]
    arrived(relay_p, relay_sems.at[1])
    go(remote(relay_p, from_y.at[last_y, 0:4], relay_sems.at[4], y_recv.at[2], at(y_=next_y)))
    arrived(relay_m, relay_sems.at[3])
    go(remote(relay_m, from_y.at[next_y, 4:8], relay_sems.at[5], y_recv.at[3], at(y_=last_y)))
    window_pair(near, win)

    arrived(from_y.at[last_y], y_recv.at[0])
    arrived(from_y.at[next_y], y_recv.at[1])
    arrived(from_y.at[across, 0:4], y_recv.at[2])
    arrived(from_y.at[across, 4:8], y_recv.at[3])
    for b in range(2):
        oy = owner_of(plan_ref, b)[0]
        to_core[b] = from_y[oy, :, 1 - core]
        from_core[core, b] = from_y[oy, :, core]

    go(remote(to_core, from_core.at[core], core_sems.at[0], core_sems.at[1], at(core_=1 - core)))
    for i in range(4):
        arrived(transit_p.at[i], hop1_recv.at[i])
        go(remote(transit_p.at[i], far.at[i], hop2_send.at[i], hop2_recv.at[i], plus))
        arrived(transit_m.at[i], hop1_recv.at[4 + i])
        go(remote(transit_m.at[i], far.at[4 + i], hop2_send.at[4 + i], hop2_recv.at[4 + i], minus))
    arrived(from_core.at[1 - core], core_sems.at[1])
    for b in range(2):
        picked = from_core[owner_of(plan_ref, b)[3], b].astype(jnp.float32)
        picked = jnp.transpose(picked, (1, 0, 2))
        picked = jnp.concatenate([picked[:, :, :NF], picked[:, :, NF:]], 1)
        to_z[:, b] = picked.astype(jnp.bfloat16).reshape(NZ, 2, 16, NF)

    opposite, three_down, one_down = zs[3], zs[4], zs[6]
    go(remote(to_z.at[opposite, :, 1], relay_z, zr_sems.at[0], zr_sems.at[1], at(z_=three_down)))
    go(remote(to_z.at[opposite, :, 0], from_z.at[z, :, 0], z_send.at[3], z_recv.at[z], at(z_=opposite)))
    for d, v in enumerate(zs):
        if d != 3:
            go(remote(to_z.at[v], from_z.at[z], z_send.at[d], z_recv.at[z], at(z_=v)))
    from_z[z] = to_z[z]

    shape = (GROUPS * 16, NF)
    pick_group = (lax.broadcasted_iota(jnp.int32, shape, 1) >> 3) == (lax.broadcasted_iota(jnp.int32, shape, 0) >> 4)
    shape = (GROUPS * 16, CH)
    pick_row = (lax.broadcasted_iota(jnp.int32, shape, 1) >> 3) == (lax.broadcasted_iota(jnp.int32, shape, 0) & 15)
    f = lax.broadcasted_iota(jnp.int32, (NF, CH), 0)
    n = lax.broadcasted_iota(jnp.int32, (NF, CH), 1)
    same_place = ((f & 7) == (n & 7)).astype(jnp.float32).astype(jnp.bfloat16)
    out_row = lax.broadcasted_iota(jnp.int32, (GROUPS, GROUPS * 16), 0)
    in_row = lax.broadcasted_iota(jnp.int32, (GROUPS, GROUPS * 16), 1)
    same_group = ((in_row >> 4) == out_row).astype(jnp.float32).astype(jnp.bfloat16)

    arrived(relay_z, zr_sems.at[1])
    go(remote(relay_z, from_z.at[zs[2], :, 1], zr_sems.at[2], zr_sems.at[3], at(z_=one_down)))
    for d, v in enumerate(zs):
        if d != 3:
            arrived(from_z.at[v], z_recv.at[v])
    arrived(from_z.at[opposite, :, 0], z_recv.at[opposite])
    arrived(from_z.at[opposite, :, 1], zr_sems.at[3])

    def regroup(i, carry):
        b, e = i // 2, i % 2
        rows = from_z[owner_of(plan_ref, b)[2], b, e].astype(jnp.float32).reshape(1, 16, NF)
        rows = jnp.broadcast_to(rows, (GROUPS, 16, NF)).reshape(GROUPS * 16, NF)
        rows = jnp.where(pick_group, rows, 0.0).astype(jnp.bfloat16)
        moved = jnp.dot(rows, same_place, preferred_element_type=jnp.float32)
        moved = jnp.where(pick_row, moved, 0.0).astype(jnp.bfloat16)
        done = jnp.dot(same_group, moved, preferred_element_type=jnp.float32)
        to_x[b, e] = done.astype(jnp.bfloat16)
        return carry

    lax.fori_loop(0, 4, regroup, 0, unroll=2)

    active = win == core
    there = from_x.at[x_lo, win]
    go(remote(to_x, there, x_send.at[0], x_recv.at[x_lo, win], at(x_=1 - x_lo, win_=core)))

    def over():
        return remote(to_x, there, x_send.at[1], x_recv.at[x_lo, win], at(win_=core))

    @pl.when(win != core)
    def _():
        over().start()

    own = gathered.at[z, y]

    def over_y():
        return [remote(own, own, gy_send.at[d], gy_recv.at[y], at(y_=v)) for d, v in enumerate(ys)]

    @pl.when(active)
    def _():
        from_x[x_lo, win] = to_x[...]
        arrived(from_x.at[1 - x_lo, win], x_recv.at[1 - x_lo, win])
        arrived(from_x.at[0, 1 - win], x_recv.at[0, 1 - win])
        arrived(from_x.at[1, 1 - win], x_recv.at[1, 1 - win])

        for b in range(2):
            ox = owner_of(plan_ref, b)[1]
            for w in range(2):
                gathered[z, y, b, :, :, w * CH : (w + 1) * CH] = from_x[ox, w, b]
        for copy in over_y():
            copy.start()

    for i in range(8):
        arrived(far.at[i], hop2_recv.at[i])
    window_pair(far, 1 - win)

    lane = lax.broadcasted_iota(jnp.int32, (1, 8, 2 * CH), 2)
    sub = lax.broadcasted_iota(jnp.int32, (1, 8, 2 * CH), 1)
    diagonal = (lane & 7) == sub

    def correlate(slots):
        count = len(slots)

        def unpack(v, carry):
            for i, slot in enumerate(slots):
                sources[i, v] = gathered[slot, v].astype(jnp.float32)
            return carry

        lax.fori_loop(0, NY, unpack, 0)

        def product(g):
            row = sources[:count, :, :, :, pl.ds(g, 1), :].reshape(count * 16, 1, 2 * CH)
            spread = jnp.where(diagonal, row, 0.0)
            spread = spread.reshape(count * 16 * 8, 2 * CH).astype(jnp.bfloat16)
            res = jnp.dot(spread, weights[g], preferred_element_type=jnp.float32)
            return res.reshape(count * 16, 8, 2 * CH)

        def bins(gg, carry):
            res = jnp.concatenate([product(2 * gg), product(2 * gg + 1)], 1)
            res = res.astype(jnp.bfloat16).reshape(count, NY, 2, 2, 16, 2 * CH)
            row = pl.multiple_of(gg * 16, 16)
            for i, slot in enumerate(slots):
                for b in range(2):
                    for c in range(2):
                        for s in range(2):
                            cross[b, :, slot, pl.ds(c * NF + row, 16), s * CH : (s + 1) * CH] = res[
                                i, :, b, s, :, c * CH : (c + 1) * CH
                            ]
            return carry

        lax.fori_loop(0, GROUPS // 2, bins, 0, unroll=2)

    def down(t):
        return (z + NZ - t) % NZ

    def up(t):
        return (z + t) % NZ

    def pieces(t):
        return [(0, 0), (1, 1)] if t == 3 else [(0, 0), (1, 0), (0, 1), (1, 1)]

    def ring_piece(t, way, half):
        ref = gathered.at[down(t) if way == 0 else up(t), 2 * half : 2 * half + 2]
        return remote(
            ref, ref, ring_send.at[way, t, half], ring_recv.at[way, t, half], at(z_=up(1) if way == 0 else down(1))
        )

    def ring_arrived(t, way, half):
        ref = gathered.at[down(t) if way == 0 else up(t), 2 * half : 2 * half + 2]
        arrived(ref, ring_recv.at[way, t - 1, half])

    def pass_on(slot):
        ref = gathered.at[slot]
        return remote(ref, ref, gc_send.at[slot], gc_recv.at[slot], at(core_=1 - core))

    slots = [[z], [down(1), up(1)], [down(2), up(2)], [down(3), up(3)], [up(4)]]
    done = []
    for t in range(5):

        @pl.when(active)
        def _():
            if t == 0:
                for v in ys:
                    arrived(gathered.at[z, v], gy_recv.at[v])
                for way, half in pieces(0):
                    ring_piece(0, way, half).start()
            else:
                for way, half in pieces(t - 1):
                    ring_arrived(t, way, half)
                    if t < 4 and (way, half) in pieces(t):
                        ring_piece(t, way, half).start()
            for slot in slots[t]:
                pass_on(slot).start()

        @pl.when(win != core)
        def _():
            for slot in slots[t]:
                arrived(gathered.at[slot], gc_recv.at[slot])

        correlate(slots[t])
        done.extend(slots[t])

    for copy in sent:
        copy.wait_send()

    @pl.when(win != core)
    def _():
        over().wait_send()

    @pl.when(active)
    def _():
        for copy in over_y() + [pass_on(slot) for slot in done]:
            copy.wait_send()
        for t in range(4):
            for way, half in pieces(t):
                ring_piece(t, way, half).wait_send()


def spread(plan, spectra):
    bf = jnp.bfloat16
    piece = (2, 16, NF)
    dma = pltpu.SemaphoreType.DMA
    natural = (2, NY, 16, 2 * NF)
    return pl.pallas_call(
        spread_kernel,
        out_shape=jax.ShapeDtypeStruct((2, NY, NZ, 2 * NF, 2 * CH), bf),
        in_specs=[pl.BlockSpec(memory_space=pltpu.SMEM), pl.BlockSpec(memory_space=pltpu.HBM)],
        out_specs=pl.BlockSpec(memory_space=pltpu.VMEM),
        scratch_shapes=[
            pltpu.VMEM((8,) + natural, bf),
            pltpu.VMEM((8,) + natural, bf),
            pltpu.VMEM((NY, 8, 2, 16, 2 * NF), bf),
            pltpu.VMEM((4, 2, 16, 2 * NF), bf),
            pltpu.VMEM((4, 2, 16, 2 * NF), bf),
            pltpu.VMEM((2, 8, 16, 2 * NF), bf),
            pltpu.VMEM((2, 2, 8, 16, 2 * NF), bf),
            pltpu.VMEM((NZ, 2) + piece, bf),
            pltpu.VMEM((NZ, 2) + piece, bf),
            pltpu.VMEM(piece, bf),
            pltpu.VMEM((2, 2, GROUPS, CH), bf),
            pltpu.VMEM((2, 2, 2, 2, GROUPS, CH), bf),
            pltpu.VMEM((NZ, NY, 2, 2, GROUPS, 2 * CH), bf),
            pltpu.VMEM((4,) + natural, bf),
            pltpu.VMEM((4,) + natural, bf),
            pltpu.VMEM((GROUPS, 2 * CH, 2 * CH), bf),
            pltpu.VMEM((2, NY, 2, 2, GROUPS, 2 * CH), jnp.float32),
            dma, dma((2,)), dma((4,)), dma((6,)), dma((2,)), dma((7,)), dma((NZ,)), dma((4,)), dma((2,)), dma((2, 2)),
            dma((3,)), dma((NY,)), dma((2, 4, 2)), dma((2, 4, 2)), dma((NZ,)), dma((NZ,)),
            dma((8,)), dma((8,)), dma((8,)), dma((8,)),
        ],
        compiler_params=pltpu.CompilerParams(
            collective_id=0, has_side_effects=True, vmem_limit_bytes=28 * 1024 * 1024
        ),
    )(plan, spectra.reshape((8,) + natural))


def lag_kernel(cross, mask_ref, table_ref, out_ref, stage, out_sems):
    half = HALF // 2

    def result(p):
        slot = lax.rem(p, BUFFERS)
        place = out_ref.at[p // half, pl.ds(2 * lax.rem(p, half), 2)]
        return pltpu.make_async_copy(stage.at[slot], place, out_sems.at[slot])

    def batch(i, drain):
        pairs = [BATCH * i + k for k in range(BATCH)]
        if drain:
            for p in pairs:
                result(p - BUFFERS).wait()
        for p in pairs:
            b, row = p // half, 2 * lax.rem(p, half)
            lagged = jnp.dot(table_ref[...], cross[b, lax.rem(p, half)], preferred_element_type=jnp.float32)
            for s in range(2):
                keep = mask_ref[b, pl.ds(row + s, 1), :].astype(jnp.float32)
                kept = (lagged[:, s * CH : (s + 1) * CH] * keep).astype(jnp.bfloat16)
                stage[lax.rem(p, BUFFERS), s] = kept.T
        for p in pairs:
            result(p).start()

    def first(i, carry):
        batch(i, False)
        return carry

    def rest(i, carry):
        batch(i, True)
        return carry

    lax.fori_loop(0, 2, first, 0)
    lax.fori_loop(2, HALF // BATCH, rest, 0)
    for k in range(BUFFERS):
        result(HALF - BUFFERS + k).wait()


def lags(cross, mask):
    vmem = pl.BlockSpec(memory_space=pltpu.VMEM)
    return pl.pallas_call(
        lag_kernel,
        out_shape=jax.ShapeDtypeStruct((2, HALF, CH, LAGS), jnp.bfloat16),
        in_specs=[vmem, vmem, vmem],
        out_specs=pl.BlockSpec(memory_space=pltpu.HBM),
        scratch_shapes=[
            pltpu.VMEM((BUFFERS, 2, CH, LAGS), jnp.bfloat16),
            pltpu.SemaphoreType.DMA((BUFFERS,)),
        ],
        compiler_params=pltpu.CompilerParams(vmem_limit_bytes=28 * 1024 * 1024),
    )(cross.reshape(2, HALF // 2, 2 * NF, 2 * CH), mask, jnp.asarray(table_transposed()))


def on_device(spectra, plan, mask):
    return lags(spread(plan, spectra), mask)


def solution(mesh):
    return jax.shard_map(
        on_device,
        mesh=mesh,
        in_specs=(P("win", "rx", None), P(), P(None, "win", "rx")),
        out_specs=P(None, "win", "rx", None),
        check_vma=False,
    )
```

```python
import math

import jax
import jax.numpy as jnp
import numpy as np
from jax import lax
from jax.experimental import pallas as pl
from jax.experimental.pallas import tpu as pltpu
from jax.sharding import PartitionSpec as P

LAGS = 256
SAMPLES = 15000
BIN0 = 12
NF = 256
WINDOWS = 16
CH = 128
HALF = 64
GROUPS = 32
MESH = pl.DeviceIdType.MESH
NY, NZ = 4, 8
BATCH = 16
BUFFERS = 2 * BATCH


def table_transposed():
    bins = BIN0 + np.arange(NF)
    shifts = np.arange(LAGS) - LAGS // 2
    theta = 2.0 * math.pi * np.mod(bins[:, None] * shifts[None, :], SAMPLES) / SAMPLES
    scale = 1.0 / math.sqrt(NF)
    table = np.concatenate([np.cos(theta) * scale, -np.sin(theta) * scale], 0)
    table = table.astype(np.float32).astype(jnp.bfloat16).astype(np.float32)
    return np.ascontiguousarray((table / WINDOWS).T).astype(jnp.bfloat16)


def owner_of(plan_ref, block):
    rx = plan_ref[block]
    return rx // 32, (rx // 16) % 2, (rx // 2) % NZ, rx % 2


def spread_kernel(
    plan_hbm, spec_ref, cross,
    plan_ref, near, far, from_y, relay_p, relay_m, to_core, from_core, to_z, from_z, relay_z, to_x, from_x,
    gathered, transit_p, transit_m, weights, sources,
    y_send, y_recv, relay_sems, core_sems, z_send, z_recv, zr_sems, x_send, x_recv,
    gy_send, gy_recv, ring_send, ring_recv, gc_send, gc_recv, last_send, last_recv, in_sems,
    hop1_send, hop1_recv, hop2_send, hop2_recv,
):
    rx, win = lax.axis_index("rx"), lax.axis_index("win")
    core, z, x_lo, y = rx % 2, (rx // 2) % NZ, (rx // 16) % 2, rx // 32

    def at(y_=y, x_=x_lo, z_=z, core_=core, win_=win):
        return {"rx": ((y_ * 2 + x_) * NZ + z_) * 2 + core_, "win": win_}

    def remote(src, dst, send, recv, device):
        return pltpu.make_async_remote_copy(
            src_ref=src, dst_ref=dst, send_sem=send, recv_sem=recv, device_id=device, device_id_type=MESH
        )

    def arrived(ref, recv):
        remote(ref, ref, recv, recv, at()).wait_recv()


    loads = [
        pltpu.make_async_copy(spec_ref, near, in_sems.at[0]),
        pltpu.make_async_copy(plan_hbm, plan_ref, in_sems.at[1]),
    ]
    for load in loads:
        load.start()

    plus = at(x_=1 - x_lo, win_=(win + x_lo) % 2)
    minus = at(x_=1 - x_lo, win_=(win + 1 - x_lo) % 2)
    ys = [(y + d) % NY for d in range(1, NY)]
    zs = [(z + d) % NZ for d in range(1, NZ)]
    peers = [at(y_=v) for v in ys] + [at(z_=v) for v in zs] + [at(core_=1 - core)]
    peers += [plus, minus, at(win_=1 - win)]
    barrier = pltpu.get_barrier_semaphore()
    for peer in peers:
        pl.semaphore_signal(barrier, inc=1, device_id=peer, device_id_type=MESH)
    pl.semaphore_wait(barrier, len(peers))

    sent = []

    def go(copy):
        copy.start()
        sent.append(copy)

    next_y, across, last_y = ys
    go(remote(spec_ref.at[0:4, :, across], relay_p, relay_sems.at[0], relay_sems.at[1], at(y_=next_y)))
    go(remote(spec_ref.at[4:8, :, across], relay_m, relay_sems.at[2], relay_sems.at[3], at(y_=last_y)))
    go(remote(spec_ref.at[:, :, next_y], from_y.at[y], y_send.at[0], y_recv.at[0], at(y_=next_y)))
    go(remote(spec_ref.at[:, :, last_y], from_y.at[y], y_send.at[1], y_recv.at[1], at(y_=last_y)))
    for i in range(4):
        go(remote(spec_ref.at[i], transit_p.at[i], hop1_send.at[i], hop1_recv.at[i], plus))
        go(remote(spec_ref.at[4 + i], transit_m.at[i], hop1_send.at[4 + i], hop1_recv.at[4 + i], minus))

    def window_pair(ref, side):
        def body(i, carry):
            both = [
                ref[2 * i + k].reshape(CH, 2 * NF).astype(jnp.float32).T.reshape(2, GROUPS, 8, CH) for k in range(2)
            ]
            a = jnp.concatenate([both[0][0], both[1][0]], 1).astype(jnp.bfloat16)
            b = jnp.concatenate([both[0][1], both[1][1]], 1)
            minus_b = (-b).astype(jnp.bfloat16)
            b = b.astype(jnp.bfloat16)
            row = pl.multiple_of(side * CH + 16 * i, 16)
            weights[:, pl.ds(row, 16), :CH] = a
            weights[:, pl.ds(HALF + row, 16), :CH] = b
            weights[:, pl.ds(row, 16), CH:] = minus_b
            weights[:, pl.ds(HALF + row, 16), CH:] = a
            return carry

        lax.fori_loop(0, 4, body, 0)

    for load in loads:
        load.wait()
    from_y[y] = near[:, :, y]
    arrived(relay_p, relay_sems.at[1])
    go(remote(relay_p, from_y.at[last_y, 0:4], relay_sems.at[4], y_recv.at[2], at(y_=next_y)))
    arrived(relay_m, relay_sems.at[3])
    go(remote(relay_m, from_y.at[next_y, 4:8], relay_sems.at[5], y_recv.at[3], at(y_=last_y)))
    window_pair(near, win)

    arrived(from_y.at[last_y], y_recv.at[0])
    arrived(from_y.at[next_y], y_recv.at[1])
    arrived(from_y.at[across, 0:4], y_recv.at[2])
    arrived(from_y.at[across, 4:8], y_recv.at[3])
    for b in range(2):
        oy = owner_of(plan_ref, b)[0]
        to_core[b] = from_y[oy, :, 1 - core]
        from_core[core, b] = from_y[oy, :, core]

    go(remote(to_core, from_core.at[core], core_sems.at[0], core_sems.at[1], at(core_=1 - core)))
    def forward(i):
        arrived(transit_p.at[i], hop1_recv.at[i])
        go(remote(transit_p.at[i], far.at[i], hop2_send.at[i], hop2_recv.at[i], plus))
        arrived(transit_m.at[i], hop1_recv.at[4 + i])
        go(remote(transit_m.at[i], far.at[4 + i], hop2_send.at[4 + i], hop2_recv.at[4 + i], minus))

    for i in range(3):
        forward(i)
    arrived(from_core.at[1 - core], core_sems.at[1])
    for b in range(2):
        picked = from_core[owner_of(plan_ref, b)[3], b].astype(jnp.float32)
        picked = jnp.transpose(picked, (1, 0, 2))
        picked = jnp.concatenate([picked[:, :, :NF], picked[:, :, NF:]], 1)
        to_z[:, b] = picked.astype(jnp.bfloat16).reshape(NZ, 2, 16, NF)

    opposite, three_down, one_down = zs[3], zs[4], zs[6]
    go(remote(to_z.at[opposite, :, 1], relay_z, zr_sems.at[0], zr_sems.at[1], at(z_=three_down)))
    go(remote(to_z.at[opposite, :, 0], from_z.at[z, :, 0], z_send.at[3], z_recv.at[z], at(z_=opposite)))
    for d, v in enumerate(zs):
        if d != 3:
            go(remote(to_z.at[v], from_z.at[z], z_send.at[d], z_recv.at[z], at(z_=v)))
    from_z[z] = to_z[z]
    forward(3)

    shape = (GROUPS * 16, NF)
    pick_group = (lax.broadcasted_iota(jnp.int32, shape, 1) >> 3) == (lax.broadcasted_iota(jnp.int32, shape, 0) >> 4)
    shape = (GROUPS * 16, CH)
    pick_row = (lax.broadcasted_iota(jnp.int32, shape, 1) >> 3) == (lax.broadcasted_iota(jnp.int32, shape, 0) & 15)
    f = lax.broadcasted_iota(jnp.int32, (NF, CH), 0)
    n = lax.broadcasted_iota(jnp.int32, (NF, CH), 1)
    same_place = ((f & 7) == (n & 7)).astype(jnp.float32).astype(jnp.bfloat16)
    out_row = lax.broadcasted_iota(jnp.int32, (GROUPS, GROUPS * 16), 0)
    in_row = lax.broadcasted_iota(jnp.int32, (GROUPS, GROUPS * 16), 1)
    same_group = ((in_row >> 4) == out_row).astype(jnp.float32).astype(jnp.bfloat16)

    arrived(relay_z, zr_sems.at[1])
    go(remote(relay_z, from_z.at[zs[2], :, 1], zr_sems.at[2], zr_sems.at[3], at(z_=one_down)))
    for d, v in enumerate(zs):
        if d != 3:
            arrived(from_z.at[v], z_recv.at[v])
    arrived(from_z.at[opposite, :, 0], z_recv.at[opposite])
    arrived(from_z.at[opposite, :, 1], zr_sems.at[3])

    def regroup(i, carry):
        b, e = i // 2, i % 2
        rows = from_z[owner_of(plan_ref, b)[2], b, e].astype(jnp.float32).reshape(1, 16, NF)
        rows = jnp.broadcast_to(rows, (GROUPS, 16, NF)).reshape(GROUPS * 16, NF)
        rows = jnp.where(pick_group, rows, 0.0).astype(jnp.bfloat16)
        moved = jnp.dot(rows, same_place, preferred_element_type=jnp.float32)
        moved = jnp.where(pick_row, moved, 0.0).astype(jnp.bfloat16)
        done = jnp.dot(same_group, moved, preferred_element_type=jnp.float32)
        to_x[b, e] = done.astype(jnp.bfloat16)
        return carry

    lax.fori_loop(0, 4, regroup, 0, unroll=2)

    active = win == core
    there = from_x.at[x_lo, win]
    go(remote(to_x, there, x_send.at[0], x_recv.at[x_lo, win], at(x_=1 - x_lo, win_=core)))

    def over():
        return remote(to_x, there, x_send.at[1], x_recv.at[x_lo, win], at(win_=core))

    @pl.when(win != core)
    def _():
        over().start()

    own = gathered.at[z, y]

    def over_y():
        return [remote(own, own, gy_send.at[d], gy_recv.at[y], at(y_=v)) for d, v in enumerate(ys)]

    @pl.when(active)
    def _():
        from_x[x_lo, win] = to_x[...]
        arrived(from_x.at[1 - x_lo, win], x_recv.at[1 - x_lo, win])
        arrived(from_x.at[0, 1 - win], x_recv.at[0, 1 - win])
        arrived(from_x.at[1, 1 - win], x_recv.at[1, 1 - win])

        for b in range(2):
            ox = owner_of(plan_ref, b)[1]
            for w in range(2):
                gathered[z, y, b, :, :, w * CH : (w + 1) * CH] = from_x[ox, w, b]
        for copy in over_y():
            copy.start()

    for i in range(8):
        arrived(far.at[i], hop2_recv.at[i])
    window_pair(far, 1 - win)

    lane = lax.broadcasted_iota(jnp.int32, (1, 8, 2 * CH), 2)
    sub = lax.broadcasted_iota(jnp.int32, (1, 8, 2 * CH), 1)
    diagonal = (lane & 7) == sub

    def correlate(slots, part=None):
        count = len(slots)

        def unpack(v, carry):
            for i, slot in enumerate(slots):
                sources[i, v] = gathered[slot, v].astype(jnp.float32)
            return carry

        if part != 1:
            lax.fori_loop(0, NY, unpack, 0)

        def product(g):
            row = sources[:count, :, :, :, pl.ds(g, 1), :].reshape(count * 16, 1, 2 * CH)
            spread = jnp.where(diagonal, row, 0.0)
            spread = spread.reshape(count * 16 * 8, 2 * CH).astype(jnp.bfloat16)
            res = jnp.dot(spread, weights[g], preferred_element_type=jnp.float32)
            return res.reshape(count * 16, 8, 2 * CH)

        def bins(gg, carry):
            res = jnp.concatenate([product(2 * gg), product(2 * gg + 1)], 1)
            res = res.astype(jnp.bfloat16).reshape(count, NY, 2, 2, 16, 2 * CH)
            row = pl.multiple_of(gg * 16, 16)
            for i, slot in enumerate(slots):
                for b in range(2):
                    for c in range(2):
                        for s in range(2):
                            cross[b, :, slot, pl.ds(c * NF + row, 16), s * CH : (s + 1) * CH] = res[
                                i, :, b, s, :, c * CH : (c + 1) * CH
                            ]
            return carry

        quarter = GROUPS // 4
        lax.fori_loop(quarter if part == 1 else 0, quarter if part == 0 else 2 * quarter, bins, 0, unroll=4)

    def down(t):
        return (z + NZ - t) % NZ

    def up(t):
        return (z + t) % NZ

    def pieces(t):
        return [(0, 0), (1, 1)] if t == 3 else [(0, 0), (1, 0), (0, 1), (1, 1)]

    def ring_piece(t, way, half):
        ref = gathered.at[down(t) if way == 0 else up(t), 2 * half : 2 * half + 2]
        return remote(
            ref, ref, ring_send.at[way, t, half], ring_recv.at[way, t, half], at(z_=up(1) if way == 0 else down(1))
        )

    def ring_arrived(t, way, half):
        ref = gathered.at[down(t) if way == 0 else up(t), 2 * half : 2 * half + 2]
        arrived(ref, ring_recv.at[way, t - 1, half])

    def pass_on(slot):
        ref = gathered.at[slot]
        return remote(ref, ref, gc_send.at[slot], gc_recv.at[slot], at(core_=1 - core))

    def pass_last(half):
        ref = gathered.at[up(4), 2 * half : 2 * half + 2]
        return remote(ref, ref, last_send.at[half], last_recv.at[half], at(core_=1 - core))

    def receive(t, late):
        ways = ([(0, 0)], [(1, 1)]) if t == 4 else ([(0, 0), (1, 0)], [(0, 1), (1, 1)])
        for way, half in ways[late]:
            ring_arrived(t, way, half)
            if t == 4:
                pass_last(half).start()
            elif (way, half) in pieces(t):
                ring_piece(t, way, half).start()

    slots = [[z], [down(1), up(1)], [down(2), up(2)], [down(3), up(3)], [up(4)]]
    done = sum(slots, [])
    for t in range(5):

        @pl.when(active)
        def _():
            if t == 0:
                for v in ys:
                    arrived(gathered.at[z, v], gy_recv.at[v])
                for way, half in pieces(0):
                    ring_piece(0, way, half).start()
            else:
                if t == 1:
                    receive(t, 0)
                receive(t, 1)
            if t < 4:
                for slot in slots[t]:
                    pass_on(slot).start()

        @pl.when(win != core)
        def _():
            if t < 4:
                for slot in slots[t]:
                    arrived(gathered.at[slot], gc_recv.at[slot])
            else:
                for half in range(2):
                    arrived(gathered.at[up(4), 2 * half : 2 * half + 2], last_recv.at[half])

        if 0 < t < 4:
            correlate(slots[t], 0)

            @pl.when(active)
            def _():
                receive(t + 1, 0)

            correlate(slots[t], 1)
        else:
            correlate(slots[t])

    for copy in sent:
        copy.wait_send()

    @pl.when(win != core)
    def _():
        over().wait_send()

    @pl.when(active)
    def _():
        for copy in over_y() + [pass_on(slot) for slot in done[:7]] + [pass_last(half) for half in range(2)]:
            copy.wait_send()
        for t in range(4):
            for way, half in pieces(t):
                ring_piece(t, way, half).wait_send()


def spread(plan, spectra):
    bf = jnp.bfloat16
    piece = (2, 16, NF)
    dma = pltpu.SemaphoreType.DMA
    natural = (2, NY, 16, 2 * NF)
    return pl.pallas_call(
        spread_kernel,
        out_shape=jax.ShapeDtypeStruct((2, NY, NZ, 2 * NF, 2 * CH), bf),
        in_specs=[pl.BlockSpec(memory_space=pltpu.HBM), pl.BlockSpec(memory_space=pltpu.HBM)],
        out_specs=pl.BlockSpec(memory_space=pltpu.VMEM),
        scratch_shapes=[
            pltpu.SMEM((2,), jnp.int32),
            pltpu.VMEM((8,) + natural, bf),
            pltpu.VMEM((8,) + natural, bf),
            pltpu.VMEM((NY, 8, 2, 16, 2 * NF), bf),
            pltpu.VMEM((4, 2, 16, 2 * NF), bf),
            pltpu.VMEM((4, 2, 16, 2 * NF), bf),
            pltpu.VMEM((2, 8, 16, 2 * NF), bf),
            pltpu.VMEM((2, 2, 8, 16, 2 * NF), bf),
            pltpu.VMEM((NZ, 2) + piece, bf),
            pltpu.VMEM((NZ, 2) + piece, bf),
            pltpu.VMEM(piece, bf),
            pltpu.VMEM((2, 2, GROUPS, CH), bf),
            pltpu.VMEM((2, 2, 2, 2, GROUPS, CH), bf),
            pltpu.VMEM((NZ, NY, 2, 2, GROUPS, 2 * CH), bf),
            pltpu.VMEM((4,) + natural, bf),
            pltpu.VMEM((4,) + natural, bf),
            pltpu.VMEM((GROUPS, 2 * CH, 2 * CH), bf),
            pltpu.VMEM((2, NY, 2, 2, GROUPS, 2 * CH), jnp.float32),
            dma((2,)), dma((4,)), dma((6,)), dma((2,)), dma((7,)), dma((NZ,)), dma((4,)), dma((2,)), dma((2, 2)),
            dma((3,)), dma((NY,)), dma((2, 4, 2)), dma((2, 4, 2)), dma((NZ,)), dma((NZ,)), dma((2,)), dma((2,)), dma((2,)),
            dma((8,)), dma((8,)), dma((8,)), dma((8,)),
        ],
        compiler_params=pltpu.CompilerParams(
            collective_id=0, has_side_effects=True, vmem_limit_bytes=28 * 1024 * 1024
        ),
    )(
        pltpu.with_memory_space_constraint(plan, pltpu.HBM),
        pltpu.with_memory_space_constraint(spectra.reshape((8,) + natural), pltpu.HBM),
    )


def lag_kernel(cross, mask_ref, table_ref, out_ref, stage, out_sems):
    half = HALF // 2

    def result(p):
        slot = lax.rem(p, BUFFERS)
        place = out_ref.at[p // half, pl.ds(2 * lax.rem(p, half), 2)]
        return pltpu.make_async_copy(stage.at[slot], place, out_sems.at[slot])

    def batch(i, drain):
        pairs = [BATCH * i + k for k in range(BATCH)]
        if drain:
            for p in pairs:
                result(p - BUFFERS).wait()
        for p in pairs:
            b, row = p // half, 2 * lax.rem(p, half)
            lagged = jnp.dot(table_ref[...], cross[b, lax.rem(p, half)], preferred_element_type=jnp.float32)
            for s in range(2):
                keep = mask_ref[b, pl.ds(row + s, 1), :].astype(jnp.float32)
                kept = (lagged[:, s * CH : (s + 1) * CH] * keep).astype(jnp.bfloat16)
                stage[lax.rem(p, BUFFERS), s] = kept.T
        for p in pairs:
            result(p).start()

    def first(i, carry):
        batch(i, False)
        return carry

    def rest(i, carry):
        batch(i, True)
        return carry

    lax.fori_loop(0, 2, first, 0)
    lax.fori_loop(2, HALF // BATCH, rest, 0)
    for k in range(BUFFERS):
        result(HALF - BUFFERS + k).wait()


def lags(cross, mask):
    vmem = pl.BlockSpec(memory_space=pltpu.VMEM)
    return pl.pallas_call(
        lag_kernel,
        out_shape=jax.ShapeDtypeStruct((2, HALF, CH, LAGS), jnp.bfloat16),
        in_specs=[vmem, vmem, vmem],
        out_specs=pl.BlockSpec(memory_space=pltpu.HBM),
        scratch_shapes=[
            pltpu.VMEM((BUFFERS, 2, CH, LAGS), jnp.bfloat16),
            pltpu.SemaphoreType.DMA((BUFFERS,)),
        ],
        compiler_params=pltpu.CompilerParams(vmem_limit_bytes=28 * 1024 * 1024),
    )(cross.reshape(2, HALF // 2, 2 * NF, 2 * CH), mask, jnp.asarray(table_transposed()))


def on_device(spectra, plan, mask):
    return lags(spread(plan, spectra), mask)


def solution(mesh):
    return jax.shard_map(
        on_device,
        mesh=mesh,
        in_specs=(P("win", "rx", None), P(), P(None, "win", "rx")),
        out_specs=P(None, "win", "rx", None),
        check_vma=False,
    )
```

```python
import math

import jax
import jax.numpy as jnp
import numpy as np
from jax import lax
from jax.experimental import pallas as pl
from jax.experimental.pallas import tpu as pltpu
from jax.sharding import PartitionSpec as P

LAGS = 256
SAMPLES = 15000
BIN0 = 12
NF = 256
WINDOWS = 16
CH = 128
HALF = 64
GROUPS = 32
MESH = pl.DeviceIdType.MESH
NY, NZ = 4, 8
BATCH = 16
BUFFERS = 2 * BATCH


def table_transposed():
    bins = BIN0 + np.arange(NF)
    shifts = np.arange(LAGS) - LAGS // 2
    theta = 2.0 * math.pi * np.mod(bins[:, None] * shifts[None, :], SAMPLES) / SAMPLES
    scale = 1.0 / math.sqrt(NF)
    table = np.concatenate([np.cos(theta) * scale, -np.sin(theta) * scale], 0)
    table = table.astype(np.float32).astype(jnp.bfloat16).astype(np.float32)
    return np.ascontiguousarray((table / WINDOWS).T).astype(jnp.bfloat16)


def owner_of(plan_ref, block):
    rx = plan_ref[block]
    return rx // 32, (rx // 16) % 2, (rx // 2) % NZ, rx % 2


def spread_kernel(
    plan_hbm, spec_ref, cross,
    plan_ref, near, far, from_y, relay_p, relay_m, to_core, from_core, to_z, from_z, relay_z, to_x, from_x,
    gathered, transit_p, transit_m, weights, sources,
    y_send, y_recv, relay_sems, core_sems, z_send, z_recv, zr_sems, x_send, x_recv,
    gy_send, gy_recv, ring_send, ring_recv, gc_send, gc_recv, last_send, last_recv, in_sems,
    hop1_send, hop1_recv, hop2_send, hop2_recv,
):
    rx, win = lax.axis_index("rx"), lax.axis_index("win")
    core, z, x_lo, y = rx % 2, (rx // 2) % NZ, (rx // 16) % 2, rx // 32

    def at(y_=y, x_=x_lo, z_=z, core_=core, win_=win):
        return {"rx": ((y_ * 2 + x_) * NZ + z_) * 2 + core_, "win": win_}

    def remote(src, dst, send, recv, device):
        return pltpu.make_async_remote_copy(
            src_ref=src, dst_ref=dst, send_sem=send, recv_sem=recv, device_id=device, device_id_type=MESH
        )

    def arrived(ref, recv):
        remote(ref, ref, recv, recv, at()).wait_recv()


    loads = [
        pltpu.make_async_copy(spec_ref, near, in_sems.at[0]),
        pltpu.make_async_copy(plan_hbm, plan_ref, in_sems.at[1]),
    ]
    for load in loads:
        load.start()

    plus = at(x_=1 - x_lo, win_=(win + x_lo) % 2)
    minus = at(x_=1 - x_lo, win_=(win + 1 - x_lo) % 2)
    ys = [(y + d) % NY for d in range(1, NY)]
    zs = [(z + d) % NZ for d in range(1, NZ)]
    peers = [at(y_=v) for v in ys] + [at(z_=v) for v in zs] + [at(core_=1 - core)]
    peers += [plus, minus, at(win_=1 - win)]
    barrier = pltpu.get_barrier_semaphore()
    for peer in peers:
        pl.semaphore_signal(barrier, inc=1, device_id=peer, device_id_type=MESH)
    pl.semaphore_wait(barrier, len(peers))

    sent = []

    def go(copy):
        copy.start()
        sent.append(copy)

    next_y, across, last_y = ys
    go(remote(spec_ref.at[0:4, :, across], relay_p, relay_sems.at[0], relay_sems.at[1], at(y_=next_y)))
    go(remote(spec_ref.at[4:8, :, across], relay_m, relay_sems.at[2], relay_sems.at[3], at(y_=last_y)))
    go(remote(spec_ref.at[:, :, next_y], from_y.at[y], y_send.at[0], y_recv.at[0], at(y_=next_y)))
    go(remote(spec_ref.at[:, :, last_y], from_y.at[y], y_send.at[1], y_recv.at[1], at(y_=last_y)))
    for i in range(4):
        go(remote(spec_ref.at[i], transit_p.at[i], hop1_send.at[i], hop1_recv.at[i], plus))
        go(remote(spec_ref.at[4 + i], transit_m.at[i], hop1_send.at[4 + i], hop1_recv.at[4 + i], minus))

    def window_pair(ref, side):
        def body(i, carry):
            both = [
                ref[2 * i + k].reshape(CH, 2 * NF).astype(jnp.float32).T.reshape(2, GROUPS, 8, CH) for k in range(2)
            ]
            a = jnp.concatenate([both[0][0], both[1][0]], 1).astype(jnp.bfloat16)
            b = jnp.concatenate([both[0][1], both[1][1]], 1)
            minus_b = (-b).astype(jnp.bfloat16)
            b = b.astype(jnp.bfloat16)
            row = pl.multiple_of(side * CH + 16 * i, 16)
            weights[:, pl.ds(row, 16), :CH] = a
            weights[:, pl.ds(HALF + row, 16), :CH] = b
            weights[:, pl.ds(row, 16), CH:] = minus_b
            weights[:, pl.ds(HALF + row, 16), CH:] = a
            return carry

        lax.fori_loop(0, 4, body, 0)

    for load in loads:
        load.wait()
    from_y[y] = near[:, :, y]
    arrived(relay_p, relay_sems.at[1])
    go(remote(relay_p, from_y.at[last_y, 0:4], relay_sems.at[4], y_recv.at[2], at(y_=next_y)))
    arrived(relay_m, relay_sems.at[3])
    go(remote(relay_m, from_y.at[next_y, 4:8], relay_sems.at[5], y_recv.at[3], at(y_=last_y)))
    window_pair(near, win)

    arrived(from_y.at[last_y], y_recv.at[0])
    arrived(from_y.at[next_y], y_recv.at[1])
    arrived(from_y.at[across, 0:4], y_recv.at[2])
    arrived(from_y.at[across, 4:8], y_recv.at[3])
    for b in range(2):
        oy = owner_of(plan_ref, b)[0]
        to_core[b] = from_y[oy, :, 1 - core]
        from_core[core, b] = from_y[oy, :, core]

    go(remote(to_core, from_core.at[core], core_sems.at[0], core_sems.at[1], at(core_=1 - core)))
    def forward(i):
        arrived(transit_p.at[i], hop1_recv.at[i])
        go(remote(transit_p.at[i], far.at[i], hop2_send.at[i], hop2_recv.at[i], plus))
        arrived(transit_m.at[i], hop1_recv.at[4 + i])
        go(remote(transit_m.at[i], far.at[4 + i], hop2_send.at[4 + i], hop2_recv.at[4 + i], minus))

    for i in range(3):
        forward(i)
    arrived(from_core.at[1 - core], core_sems.at[1])
    for b in range(2):
        picked = from_core[owner_of(plan_ref, b)[3], b].astype(jnp.float32)
        picked = jnp.transpose(picked, (1, 0, 2))
        picked = jnp.concatenate([picked[:, :, :NF], picked[:, :, NF:]], 1)
        to_z[:, b] = picked.astype(jnp.bfloat16).reshape(NZ, 2, 16, NF)

    opposite, three_down, one_down = zs[3], zs[4], zs[6]
    go(remote(to_z.at[opposite, :, 1], relay_z, zr_sems.at[0], zr_sems.at[1], at(z_=three_down)))
    go(remote(to_z.at[opposite, :, 0], from_z.at[z, :, 0], z_send.at[3], z_recv.at[z], at(z_=opposite)))
    for d, v in enumerate(zs):
        if d != 3:
            go(remote(to_z.at[v], from_z.at[z], z_send.at[d], z_recv.at[z], at(z_=v)))
    from_z[z] = to_z[z]
    forward(3)

    shape = (GROUPS * 16, NF)
    pick_group = (lax.broadcasted_iota(jnp.int32, shape, 1) >> 3) == (lax.broadcasted_iota(jnp.int32, shape, 0) >> 4)
    shape = (GROUPS * 16, CH)
    pick_row = (lax.broadcasted_iota(jnp.int32, shape, 1) >> 3) == (lax.broadcasted_iota(jnp.int32, shape, 0) & 15)
    f = lax.broadcasted_iota(jnp.int32, (NF, CH), 0)
    n = lax.broadcasted_iota(jnp.int32, (NF, CH), 1)
    same_place = ((f & 7) == (n & 7)).astype(jnp.float32).astype(jnp.bfloat16)
    out_row = lax.broadcasted_iota(jnp.int32, (GROUPS, GROUPS * 16), 0)
    in_row = lax.broadcasted_iota(jnp.int32, (GROUPS, GROUPS * 16), 1)
    same_group = ((in_row >> 4) == out_row).astype(jnp.float32).astype(jnp.bfloat16)

    arrived(relay_z, zr_sems.at[1])
    go(remote(relay_z, from_z.at[zs[2], :, 1], zr_sems.at[2], zr_sems.at[3], at(z_=one_down)))
    for d, v in enumerate(zs):
        if d != 3:
            arrived(from_z.at[v], z_recv.at[v])
    arrived(from_z.at[opposite, :, 0], z_recv.at[opposite])
    arrived(from_z.at[opposite, :, 1], zr_sems.at[3])

    def regroup(i, carry):
        b, e = i // 2, i % 2
        rows = from_z[owner_of(plan_ref, b)[2], b, e].astype(jnp.float32).reshape(1, 16, NF)
        rows = jnp.broadcast_to(rows, (GROUPS, 16, NF)).reshape(GROUPS * 16, NF)
        rows = jnp.where(pick_group, rows, 0.0).astype(jnp.bfloat16)
        moved = jnp.dot(rows, same_place, preferred_element_type=jnp.float32)
        moved = jnp.where(pick_row, moved, 0.0).astype(jnp.bfloat16)
        done = jnp.dot(same_group, moved, preferred_element_type=jnp.float32)
        to_x[b, e] = done.astype(jnp.bfloat16)
        return carry

    lax.fori_loop(0, 4, regroup, 0, unroll=2)

    active = win == core
    there = from_x.at[x_lo, win]
    go(remote(to_x, there, x_send.at[0], x_recv.at[x_lo, win], at(x_=1 - x_lo, win_=core)))

    def over():
        return remote(to_x, there, x_send.at[1], x_recv.at[x_lo, win], at(win_=core))

    @pl.when(win != core)
    def _():
        over().start()

    def down(t):
        return (z + NZ - t) % NZ

    def up(t):
        return (z + t) % NZ

    def pieces(t):
        return [(0, 0), (0, 1), (1, 2), (1, 3)] if t == 3 else [(way, d) for d in range(NY) for way in range(2)]

    def piece(t, way, d):
        return gathered.at[down(t) if way == 0 else up(t), (y + d) % NY]

    def ring_piece(t, way, d):
        ref = piece(t, way, d)
        return remote(ref, ref, ring_send.at[way, t, d], ring_recv.at[way, t, d], at(z_=up(1) if way == 0 else down(1)))

    def pass_on(slot):
        ref = gathered.at[slot]
        return remote(ref, ref, gc_send.at[slot], gc_recv.at[slot], at(core_=1 - core))

    def pass_last(d):
        ref = piece(4, 0, d)
        return remote(ref, ref, last_send.at[d], last_recv.at[d], at(core_=1 - core))

    own = gathered.at[z, y]

    def over_y():
        return [remote(own, own, gy_send.at[d], gy_recv.at[y], at(y_=v)) for d, v in enumerate(ys)]

    @pl.when(active)
    def _():
        from_x[x_lo, win] = to_x[...]
        arrived(from_x.at[1 - x_lo, win], x_recv.at[1 - x_lo, win])
        arrived(from_x.at[0, 1 - win], x_recv.at[0, 1 - win])
        arrived(from_x.at[1, 1 - win], x_recv.at[1, 1 - win])

        for b in range(2):
            ox = owner_of(plan_ref, b)[1]
            for w in range(2):
                gathered[z, y, b, :, :, w * CH : (w + 1) * CH] = from_x[ox, w, b]
        for copy in over_y():
            copy.start()
        for way in range(2):
            ring_piece(0, way, 0).start()

    for i in range(8):
        arrived(far.at[i], hop2_recv.at[i])
    window_pair(far, 1 - win)

    lane = lax.broadcasted_iota(jnp.int32, (1, 8, 2 * CH), 2)
    sub = lax.broadcasted_iota(jnp.int32, (1, 8, 2 * CH), 1)
    diagonal = (lane & 7) == sub

    def correlate(slots, part=None):
        count = len(slots)

        def unpack(v, carry):
            for i, slot in enumerate(slots):
                sources[i, v] = gathered[slot, v].astype(jnp.float32)
            return carry

        if part != 1:
            lax.fori_loop(0, NY, unpack, 0)

        def product(g):
            row = sources[:count, :, :, :, pl.ds(g, 1), :].reshape(count * 16, 1, 2 * CH)
            spread = jnp.where(diagonal, row, 0.0)
            spread = spread.reshape(count * 16 * 8, 2 * CH).astype(jnp.bfloat16)
            res = jnp.dot(spread, weights[g], preferred_element_type=jnp.float32)
            return res.reshape(count * 16, 8, 2 * CH)

        def bins(gg, carry):
            res = jnp.concatenate([product(2 * gg), product(2 * gg + 1)], 1)
            res = res.astype(jnp.bfloat16).reshape(count, NY, 2, 2, 16, 2 * CH)
            row = pl.multiple_of(gg * 16, 16)
            for i, slot in enumerate(slots):
                for b in range(2):
                    for c in range(2):
                        for s in range(2):
                            cross[b, :, slot, pl.ds(c * NF + row, 16), s * CH : (s + 1) * CH] = res[
                                i, :, b, s, :, c * CH : (c + 1) * CH
                            ]
            return carry

        quarter = GROUPS // 4
        lax.fori_loop(quarter if part == 1 else 0, quarter if part == 0 else 2 * quarter, bins, 0, unroll=4)

    def receive(t, late):
        for way, d in pieces(t - 1):
            if (d >= 2) == bool(late):
                arrived(piece(t, way, d), ring_recv.at[way, t - 1, d])
                if t == 4:
                    pass_last(d).start()
                elif (way, d) in pieces(t):
                    ring_piece(t, way, d).start()

    slots = [[z], [down(1), up(1)], [down(2), up(2)], [down(3), up(3)], [up(4)]]
    done = sum(slots, [])
    for t in range(5):

        @pl.when(active)
        def _():
            if t == 0:
                for d, v in enumerate(ys):
                    arrived(gathered.at[z, v], gy_recv.at[v])
                    for way in range(2):
                        ring_piece(0, way, d + 1).start()
            else:
                if t == 1:
                    receive(t, 0)
                receive(t, 1)
            if t < 4:
                for slot in slots[t]:
                    pass_on(slot).start()

        @pl.when(win != core)
        def _():
            if t < 4:
                for slot in slots[t]:
                    arrived(gathered.at[slot], gc_recv.at[slot])
            else:
                for d in range(NY):
                    arrived(piece(4, 0, d), last_recv.at[d])

        if 0 < t < 4:
            correlate(slots[t], 0)

            @pl.when(active)
            def _():
                receive(t + 1, 0)

            correlate(slots[t], 1)
        else:
            correlate(slots[t])

    for copy in sent:
        copy.wait_send()

    @pl.when(win != core)
    def _():
        over().wait_send()

    @pl.when(active)
    def _():
        for copy in over_y() + [pass_on(slot) for slot in done[:7]] + [pass_last(d) for d in range(NY)]:
            copy.wait_send()
        for t in range(4):
            for way, d in pieces(t):
                ring_piece(t, way, d).wait_send()


def spread(plan, spectra):
    bf = jnp.bfloat16
    piece = (2, 16, NF)
    dma = pltpu.SemaphoreType.DMA
    natural = (2, NY, 16, 2 * NF)
    return pl.pallas_call(
        spread_kernel,
        out_shape=jax.ShapeDtypeStruct((2, NY, NZ, 2 * NF, 2 * CH), bf),
        in_specs=[pl.BlockSpec(memory_space=pltpu.HBM), pl.BlockSpec(memory_space=pltpu.HBM)],
        out_specs=pl.BlockSpec(memory_space=pltpu.VMEM),
        scratch_shapes=[
            pltpu.SMEM((2,), jnp.int32),
            pltpu.VMEM((8,) + natural, bf),
            pltpu.VMEM((8,) + natural, bf),
            pltpu.VMEM((NY, 8, 2, 16, 2 * NF), bf),
            pltpu.VMEM((4, 2, 16, 2 * NF), bf),
            pltpu.VMEM((4, 2, 16, 2 * NF), bf),
            pltpu.VMEM((2, 8, 16, 2 * NF), bf),
            pltpu.VMEM((2, 2, 8, 16, 2 * NF), bf),
            pltpu.VMEM((NZ, 2) + piece, bf),
            pltpu.VMEM((NZ, 2) + piece, bf),
            pltpu.VMEM(piece, bf),
            pltpu.VMEM((2, 2, GROUPS, CH), bf),
            pltpu.VMEM((2, 2, 2, 2, GROUPS, CH), bf),
            pltpu.VMEM((NZ, NY, 2, 2, GROUPS, 2 * CH), bf),
            pltpu.VMEM((4,) + natural, bf),
            pltpu.VMEM((4,) + natural, bf),
            pltpu.VMEM((GROUPS, 2 * CH, 2 * CH), bf),
            pltpu.VMEM((2, NY, 2, 2, GROUPS, 2 * CH), jnp.float32),
            dma((2,)), dma((4,)), dma((6,)), dma((2,)), dma((7,)), dma((NZ,)), dma((4,)), dma((2,)), dma((2, 2)),
            dma((3,)), dma((NY,)), dma((2, 4, NY)), dma((2, 4, NY)), dma((NZ,)), dma((NZ,)), dma((NY,)), dma((NY,)), dma((2,)),
            dma((8,)), dma((8,)), dma((8,)), dma((8,)),
        ],
        compiler_params=pltpu.CompilerParams(
            collective_id=0, has_side_effects=True, vmem_limit_bytes=28 * 1024 * 1024
        ),
    )(
        pltpu.with_memory_space_constraint(plan, pltpu.HBM),
        pltpu.with_memory_space_constraint(spectra.reshape((8,) + natural), pltpu.HBM),
    )


def lag_kernel(cross, mask_ref, table_ref, out_ref, stage, out_sems):
    half = HALF // 2

    def result(p):
        slot = lax.rem(p, BUFFERS)
        place = out_ref.at[p // half, pl.ds(2 * lax.rem(p, half), 2)]
        return pltpu.make_async_copy(stage.at[slot], place, out_sems.at[slot])

    def batch(i, drain):
        pairs = [BATCH * i + k for k in range(BATCH)]
        if drain:
            for p in pairs:
                result(p - BUFFERS).wait()
        for p in pairs:
            b, row = p // half, 2 * lax.rem(p, half)
            lagged = jnp.dot(table_ref[...], cross[b, lax.rem(p, half)], preferred_element_type=jnp.float32)
            for s in range(2):
                keep = mask_ref[b, pl.ds(row + s, 1), :].astype(jnp.float32)
                kept = (lagged[:, s * CH : (s + 1) * CH] * keep).astype(jnp.bfloat16)
                stage[lax.rem(p, BUFFERS), s] = kept.T
        for p in pairs:
            result(p).start()

    def first(i, carry):
        batch(i, False)
        return carry

    def rest(i, carry):
        batch(i, True)
        return carry

    lax.fori_loop(0, 2, first, 0)
    lax.fori_loop(2, HALF // BATCH, rest, 0)
    for k in range(BUFFERS):
        result(HALF - BUFFERS + k).wait()


def lags(cross, mask):
    vmem = pl.BlockSpec(memory_space=pltpu.VMEM)
    return pl.pallas_call(
        lag_kernel,
        out_shape=jax.ShapeDtypeStruct((2, HALF, CH, LAGS), jnp.bfloat16),
        in_specs=[vmem, vmem, vmem],
        out_specs=pl.BlockSpec(memory_space=pltpu.HBM),
        scratch_shapes=[
            pltpu.VMEM((BUFFERS, 2, CH, LAGS), jnp.bfloat16),
            pltpu.SemaphoreType.DMA((BUFFERS,)),
        ],
        compiler_params=pltpu.CompilerParams(vmem_limit_bytes=28 * 1024 * 1024),
    )(cross.reshape(2, HALF // 2, 2 * NF, 2 * CH), mask, jnp.asarray(table_transposed()))


def on_device(spectra, plan, mask):
    return lags(spread(plan, spectra), mask)


def solution(mesh):
    return jax.shard_map(
        on_device,
        mesh=mesh,
        in_specs=(P("win", "rx", None), P(), P(None, "win", "rx")),
        out_specs=P(None, "win", "rx", None),
        check_vma=False,
    )
```

```python
import math

import jax
import jax.numpy as jnp
import numpy as np
from jax import lax
from jax.experimental import pallas as pl
from jax.experimental.pallas import tpu as pltpu
from jax.sharding import PartitionSpec as P

LAGS = 256
SAMPLES = 15000
BIN0 = 12
NF = 256
WINDOWS = 16
CH = 128
HALF = 64
GROUPS = 32
MESH = pl.DeviceIdType.MESH
NY, NZ = 4, 8
BATCH = 16
BUFFERS = 2 * BATCH


def table_transposed():
    bins = BIN0 + np.arange(NF)
    shifts = np.arange(LAGS) - LAGS // 2
    theta = 2.0 * math.pi * np.mod(bins[:, None] * shifts[None, :], SAMPLES) / SAMPLES
    scale = 1.0 / math.sqrt(NF)
    table = np.concatenate([np.cos(theta) * scale, -np.sin(theta) * scale], 0)
    table = table.astype(np.float32).astype(jnp.bfloat16).astype(np.float32)
    return np.ascontiguousarray((table / WINDOWS).T).astype(jnp.bfloat16)


def owner_of(plan_ref, block):
    rx = plan_ref[block]
    return rx // 32, (rx // 16) % 2, (rx // 2) % NZ, rx % 2


def spread_kernel(
    plan_hbm, spec_ref, cross,
    plan_ref, near, far, from_y, relay_p, relay_m, to_z, from_z, relay_z, to_x, from_x,
    gathered, transit_p, transit_m, weights, sources,
    y_send, y_recv, relay_sems, core_sems, z_send, z_recv, zr_sems, x_send, x_recv,
    gy_send, gy_recv, ring_send, ring_recv, gc_send, gc_recv, last_send, last_recv, in_sems,
    hop1_send, hop1_recv, hop2_send, hop2_recv,
):
    rx, win = lax.axis_index("rx"), lax.axis_index("win")
    core, z, x_lo, y = rx % 2, (rx // 2) % NZ, (rx // 16) % 2, rx // 32

    def at(y_=y, x_=x_lo, z_=z, core_=core, win_=win):
        return {"rx": ((y_ * 2 + x_) * NZ + z_) * 2 + core_, "win": win_}

    def remote(src, dst, send, recv, device):
        return pltpu.make_async_remote_copy(
            src_ref=src, dst_ref=dst, send_sem=send, recv_sem=recv, device_id=device, device_id_type=MESH
        )

    def arrived(ref, recv):
        remote(ref, ref, recv, recv, at()).wait_recv()


    loads = [
        pltpu.make_async_copy(spec_ref, near, in_sems.at[0]),
        pltpu.make_async_copy(plan_hbm, plan_ref, in_sems.at[1]),
    ]
    for load in loads:
        load.start()

    plus = at(x_=1 - x_lo, win_=(win + x_lo) % 2)
    minus = at(x_=1 - x_lo, win_=(win + 1 - x_lo) % 2)
    ys = [(y + d) % NY for d in range(1, NY)]
    zs = [(z + d) % NZ for d in range(1, NZ)]
    peers = [at(y_=v) for v in ys] + [at(z_=v) for v in zs] + [at(core_=1 - core)]
    peers += [plus, minus, at(win_=1 - win), at(y_=ys[0], core_=1 - core), at(y_=ys[2], core_=1 - core)]
    barrier = pltpu.get_barrier_semaphore()
    for peer in peers:
        pl.semaphore_signal(barrier, inc=1, device_id=peer, device_id_type=MESH)
    pl.semaphore_wait(barrier, len(peers))

    sent = []

    def go(copy):
        copy.start()
        sent.append(copy)

    next_y, across, last_y = ys
    go(remote(spec_ref.at[0:4, :, across], relay_p, relay_sems.at[0], relay_sems.at[1], at(y_=next_y)))
    go(remote(spec_ref.at[4:8, :, across], relay_m, relay_sems.at[2], relay_sems.at[3], at(y_=last_y)))
    mine = from_y.at[y, core]
    for h in range(2):
        go(remote(spec_ref.at[:, h, next_y], mine, y_send.at[0, h], y_recv.at[0, core], at(y_=next_y, core_=h)))
        go(remote(spec_ref.at[:, h, last_y], mine, y_send.at[1, h], y_recv.at[1, core], at(y_=last_y, core_=h)))
    go(remote(spec_ref.at[:, 1 - core, y], mine, core_sems.at[0], core_sems.at[1], at(core_=1 - core)))
    for i in range(4):
        go(remote(spec_ref.at[i], transit_p.at[i], hop1_send.at[i], hop1_recv.at[i], plus))
        go(remote(spec_ref.at[4 + i], transit_m.at[i], hop1_send.at[4 + i], hop1_recv.at[4 + i], minus))

    def window_pair(ref, side):
        def body(i, carry):
            both = [
                ref[2 * i + k].reshape(CH, 2 * NF).astype(jnp.float32).T.reshape(2, GROUPS, 8, CH) for k in range(2)
            ]
            a = jnp.concatenate([both[0][0], both[1][0]], 1).astype(jnp.bfloat16)
            b = jnp.concatenate([both[0][1], both[1][1]], 1)
            minus_b = (-b).astype(jnp.bfloat16)
            b = b.astype(jnp.bfloat16)
            row = pl.multiple_of(side * CH + 16 * i, 16)
            weights[:, pl.ds(row, 16), :CH] = a
            weights[:, pl.ds(HALF + row, 16), :CH] = b
            weights[:, pl.ds(row, 16), CH:] = minus_b
            weights[:, pl.ds(HALF + row, 16), CH:] = a
            return carry

        lax.fori_loop(0, 4, body, 0)

    for load in loads:
        load.wait()
    from_y[y, core] = near[:, core, y]
    arrived(relay_p, relay_sems.at[1])
    place = from_y.at[last_y, core, 0:4]
    for h in range(2):
        go(remote(relay_p.at[:, h], place, y_send.at[2, h], y_recv.at[2, core], at(y_=next_y, core_=h)))
    arrived(relay_m, relay_sems.at[3])
    place = from_y.at[next_y, core, 4:8]
    for h in range(2):
        go(remote(relay_m.at[:, h], place, y_send.at[3, h], y_recv.at[3, core], at(y_=last_y, core_=h)))
    window_pair(near, win)

    def forward(i):
        arrived(transit_p.at[i], hop1_recv.at[i])
        go(remote(transit_p.at[i], far.at[i], hop2_send.at[i], hop2_recv.at[i], plus))
        arrived(transit_m.at[i], hop1_recv.at[4 + i])
        go(remote(transit_m.at[i], far.at[4 + i], hop2_send.at[4 + i], hop2_recv.at[4 + i], minus))

    for i in range(3):
        forward(i)
    arrived(from_y.at[y, 1 - core], core_sems.at[1])
    for k in range(2):
        arrived(from_y.at[last_y, k], y_recv.at[0, k])
        arrived(from_y.at[next_y, k], y_recv.at[1, k])
        arrived(from_y.at[across, k, 0:4], y_recv.at[2, k])
        arrived(from_y.at[across, k, 4:8], y_recv.at[3, k])
    for b in range(2):
        oy, _, _, oc = owner_of(plan_ref, b)
        picked = jnp.transpose(from_y[oy, oc].astype(jnp.float32), (1, 0, 2))
        picked = jnp.concatenate([picked[:, :, :NF], picked[:, :, NF:]], 1)
        to_z[:, b] = picked.astype(jnp.bfloat16).reshape(NZ, 2, 16, NF)

    opposite, three_down, one_down = zs[3], zs[4], zs[6]
    go(remote(to_z.at[opposite, :, 1], relay_z, zr_sems.at[0], zr_sems.at[1], at(z_=three_down)))
    go(remote(to_z.at[opposite, :, 0], from_z.at[z, :, 0], z_send.at[3], z_recv.at[z], at(z_=opposite)))
    for d, v in enumerate(zs):
        if d != 3:
            go(remote(to_z.at[v], from_z.at[z], z_send.at[d], z_recv.at[z], at(z_=v)))
    from_z[z] = to_z[z]
    forward(3)

    shape = (GROUPS * 16, NF)
    pick_group = (lax.broadcasted_iota(jnp.int32, shape, 1) >> 3) == (lax.broadcasted_iota(jnp.int32, shape, 0) >> 4)
    shape = (GROUPS * 16, CH)
    pick_row = (lax.broadcasted_iota(jnp.int32, shape, 1) >> 3) == (lax.broadcasted_iota(jnp.int32, shape, 0) & 15)
    f = lax.broadcasted_iota(jnp.int32, (NF, CH), 0)
    n = lax.broadcasted_iota(jnp.int32, (NF, CH), 1)
    same_place = ((f & 7) == (n & 7)).astype(jnp.float32).astype(jnp.bfloat16)
    out_row = lax.broadcasted_iota(jnp.int32, (GROUPS, GROUPS * 16), 0)
    in_row = lax.broadcasted_iota(jnp.int32, (GROUPS, GROUPS * 16), 1)
    same_group = ((in_row >> 4) == out_row).astype(jnp.float32).astype(jnp.bfloat16)

    arrived(relay_z, zr_sems.at[1])
    go(remote(relay_z, from_z.at[zs[2], :, 1], zr_sems.at[2], zr_sems.at[3], at(z_=one_down)))
    for d, v in enumerate(zs):
        if d != 3:
            arrived(from_z.at[v], z_recv.at[v])
    arrived(from_z.at[opposite, :, 0], z_recv.at[opposite])
    arrived(from_z.at[opposite, :, 1], zr_sems.at[3])

    def regroup(i, carry):
        b, e = i // 2, i % 2
        rows = from_z[owner_of(plan_ref, b)[2], b, e].astype(jnp.float32).reshape(1, 16, NF)
        rows = jnp.broadcast_to(rows, (GROUPS, 16, NF)).reshape(GROUPS * 16, NF)
        rows = jnp.where(pick_group, rows, 0.0).astype(jnp.bfloat16)
        moved = jnp.dot(rows, same_place, preferred_element_type=jnp.float32)
        moved = jnp.where(pick_row, moved, 0.0).astype(jnp.bfloat16)
        done = jnp.dot(same_group, moved, preferred_element_type=jnp.float32)
        to_x[b, e] = done.astype(jnp.bfloat16)
        return carry

    lax.fori_loop(0, 4, regroup, 0, unroll=2)

    active = win == core
    there = from_x.at[x_lo, win]
    go(remote(to_x, there, x_send.at[0], x_recv.at[x_lo, win], at(x_=1 - x_lo, win_=core)))

    def over():
        return remote(to_x, there, x_send.at[1], x_recv.at[x_lo, win], at(win_=core))

    @pl.when(win != core)
    def _():
        over().start()

    def down(t):
        return (z + NZ - t) % NZ

    def up(t):
        return (z + t) % NZ

    def pieces(t):
        return [(0, 0), (0, 1), (1, 2), (1, 3)] if t == 3 else [(way, d) for d in range(NY) for way in range(2)]

    def piece(t, way, d):
        return gathered.at[down(t) if way == 0 else up(t), (y + d) % NY]

    def ring_piece(t, way, d):
        ref = piece(t, way, d)
        return remote(ref, ref, ring_send.at[way, t, d], ring_recv.at[way, t, d], at(z_=up(1) if way == 0 else down(1)))

    def pass_on(slot):
        ref = gathered.at[slot]
        return remote(ref, ref, gc_send.at[slot], gc_recv.at[slot], at(core_=1 - core))

    def pass_last(d):
        ref = piece(4, 0, d)
        return remote(ref, ref, last_send.at[d], last_recv.at[d], at(core_=1 - core))

    own = gathered.at[z, y]

    def over_y():
        return [remote(own, own, gy_send.at[d], gy_recv.at[y], at(y_=v)) for d, v in enumerate(ys)]

    @pl.when(active)
    def _():
        from_x[x_lo, win] = to_x[...]
        arrived(from_x.at[1 - x_lo, win], x_recv.at[1 - x_lo, win])
        arrived(from_x.at[0, 1 - win], x_recv.at[0, 1 - win])
        arrived(from_x.at[1, 1 - win], x_recv.at[1, 1 - win])

        for b in range(2):
            ox = owner_of(plan_ref, b)[1]
            for w in range(2):
                gathered[z, y, b, :, :, w * CH : (w + 1) * CH] = from_x[ox, w, b]
        for copy in over_y():
            copy.start()
        for way in range(2):
            ring_piece(0, way, 0).start()

    for i in range(8):
        arrived(far.at[i], hop2_recv.at[i])
    window_pair(far, 1 - win)

    lane = lax.broadcasted_iota(jnp.int32, (1, 8, 2 * CH), 2)
    sub = lax.broadcasted_iota(jnp.int32, (1, 8, 2 * CH), 1)
    diagonal = (lane & 7) == sub

    def correlate(slots, part=None):
        count = len(slots)

        def unpack(v, carry):
            for i, slot in enumerate(slots):
                sources[i, v] = gathered[slot, v].astype(jnp.float32)
            return carry

        if part != 1:
            lax.fori_loop(0, NY, unpack, 0)

        def product(g):
            row = sources[:count, :, :, :, pl.ds(g, 1), :].reshape(count * 16, 1, 2 * CH)
            spread = jnp.where(diagonal, row, 0.0)
            spread = spread.reshape(count * 16 * 8, 2 * CH).astype(jnp.bfloat16)
            res = jnp.dot(spread, weights[g], preferred_element_type=jnp.float32)
            return res.reshape(count * 16, 8, 2 * CH)

        def bins(gg, carry):
            res = jnp.concatenate([product(2 * gg), product(2 * gg + 1)], 1)
            res = res.astype(jnp.bfloat16).reshape(count, NY, 2, 2, 16, 2 * CH)
            row = pl.multiple_of(gg * 16, 16)
            for i, slot in enumerate(slots):
                for b in range(2):
                    for c in range(2):
                        for s in range(2):
                            cross[b, :, slot, pl.ds(c * NF + row, 16), s * CH : (s + 1) * CH] = res[
                                i, :, b, s, :, c * CH : (c + 1) * CH
                            ]
            return carry

        quarter = GROUPS // 4
        lax.fori_loop(quarter if part == 1 else 0, quarter if part == 0 else 2 * quarter, bins, 0, unroll=4)

    def receive(t, late):
        for way, d in pieces(t - 1):
            if (d >= 2) == bool(late):
                arrived(piece(t, way, d), ring_recv.at[way, t - 1, d])
                if t == 4:
                    pass_last(d).start()
                elif (way, d) in pieces(t):
                    ring_piece(t, way, d).start()

    slots = [[z], [down(1), up(1)], [down(2), up(2)], [down(3), up(3)], [up(4)]]
    done = sum(slots, [])
    for t in range(5):

        @pl.when(active)
        def _():
            if t == 0:
                for d, v in enumerate(ys):
                    arrived(gathered.at[z, v], gy_recv.at[v])
                    for way in range(2):
                        ring_piece(0, way, d + 1).start()
            else:
                if t == 1:
                    receive(t, 0)
                receive(t, 1)
            if t < 4:
                for slot in slots[t]:
                    pass_on(slot).start()

        @pl.when(win != core)
        def _():
            if t < 4:
                for slot in slots[t]:
                    arrived(gathered.at[slot], gc_recv.at[slot])
            else:
                for d in range(NY):
                    arrived(piece(4, 0, d), last_recv.at[d])

        if 0 < t < 4:
            correlate(slots[t], 0)

            @pl.when(active)
            def _():
                receive(t + 1, 0)

            correlate(slots[t], 1)
        else:
            correlate(slots[t])

    for copy in sent:
        copy.wait_send()

    @pl.when(win != core)
    def _():
        over().wait_send()

    @pl.when(active)
    def _():
        for copy in over_y() + [pass_on(slot) for slot in done[:7]] + [pass_last(d) for d in range(NY)]:
            copy.wait_send()
        for t in range(4):
            for way, d in pieces(t):
                ring_piece(t, way, d).wait_send()


def spread(plan, spectra):
    bf = jnp.bfloat16
    piece = (2, 16, NF)
    dma = pltpu.SemaphoreType.DMA
    natural = (2, NY, 16, 2 * NF)
    return pl.pallas_call(
        spread_kernel,
        out_shape=jax.ShapeDtypeStruct((2, NY, NZ, 2 * NF, 2 * CH), bf),
        in_specs=[pl.BlockSpec(memory_space=pltpu.HBM), pl.BlockSpec(memory_space=pltpu.HBM)],
        out_specs=pl.BlockSpec(memory_space=pltpu.VMEM),
        scratch_shapes=[
            pltpu.SMEM((2,), jnp.int32),
            pltpu.VMEM((8,) + natural, bf),
            pltpu.VMEM((8,) + natural, bf),
            pltpu.VMEM((NY, 2, 8, 16, 2 * NF), bf),
            pltpu.VMEM((4, 2, 16, 2 * NF), bf),
            pltpu.VMEM((4, 2, 16, 2 * NF), bf),
            pltpu.VMEM((NZ, 2) + piece, bf),
            pltpu.VMEM((NZ, 2) + piece, bf),
            pltpu.VMEM(piece, bf),
            pltpu.VMEM((2, 2, GROUPS, CH), bf),
            pltpu.VMEM((2, 2, 2, 2, GROUPS, CH), bf),
            pltpu.VMEM((NZ, NY, 2, 2, GROUPS, 2 * CH), bf),
            pltpu.VMEM((4,) + natural, bf),
            pltpu.VMEM((4,) + natural, bf),
            pltpu.VMEM((GROUPS, 2 * CH, 2 * CH), bf),
            pltpu.VMEM((2, NY, 2, 2, GROUPS, 2 * CH), jnp.float32),
            dma((4, 2)), dma((4, 2)), dma((4,)), dma((2,)), dma((7,)), dma((NZ,)), dma((4,)), dma((2,)), dma((2, 2)),
            dma((3,)), dma((NY,)), dma((2, 4, NY)), dma((2, 4, NY)), dma((NZ,)), dma((NZ,)), dma((NY,)), dma((NY,)), dma((2,)),
            dma((8,)), dma((8,)), dma((8,)), dma((8,)),
        ],
        compiler_params=pltpu.CompilerParams(
            collective_id=0, has_side_effects=True, vmem_limit_bytes=28 * 1024 * 1024
        ),
    )(
        pltpu.with_memory_space_constraint(plan, pltpu.HBM),
        pltpu.with_memory_space_constraint(spectra.reshape((8,) + natural), pltpu.HBM),
    )


def lag_kernel(cross, mask_ref, table_ref, out_ref, stage, out_sems):
    half = HALF // 2

    def result(p):
        slot = lax.rem(p, BUFFERS)
        place = out_ref.at[p // half, pl.ds(2 * lax.rem(p, half), 2)]
        return pltpu.make_async_copy(stage.at[slot], place, out_sems.at[slot])

    def batch(i, drain):
        pairs = [BATCH * i + k for k in range(BATCH)]
        if drain:
            for p in pairs:
                result(p - BUFFERS).wait()
        for p in pairs:
            b, row = p // half, 2 * lax.rem(p, half)
            lagged = jnp.dot(table_ref[...], cross[b, lax.rem(p, half)], preferred_element_type=jnp.float32)
            for s in range(2):
                keep = mask_ref[b, pl.ds(row + s, 1), :].astype(jnp.float32)
                kept = (lagged[:, s * CH : (s + 1) * CH] * keep).astype(jnp.bfloat16)
                stage[lax.rem(p, BUFFERS), s] = kept.T
        for p in pairs:
            result(p).start()

    def first(i, carry):
        batch(i, False)
        return carry

    def rest(i, carry):
        batch(i, True)
        return carry

    lax.fori_loop(0, 2, first, 0)
    lax.fori_loop(2, HALF // BATCH, rest, 0)
    for k in range(BUFFERS):
        result(HALF - BUFFERS + k).wait()


def lags(cross, mask):
    vmem = pl.BlockSpec(memory_space=pltpu.VMEM)
    return pl.pallas_call(
        lag_kernel,
        out_shape=jax.ShapeDtypeStruct((2, HALF, CH, LAGS), jnp.bfloat16),
        in_specs=[vmem, vmem, vmem],
        out_specs=pl.BlockSpec(memory_space=pltpu.HBM),
        scratch_shapes=[
            pltpu.VMEM((BUFFERS, 2, CH, LAGS), jnp.bfloat16),
            pltpu.SemaphoreType.DMA((BUFFERS,)),
        ],
        compiler_params=pltpu.CompilerParams(vmem_limit_bytes=28 * 1024 * 1024),
    )(cross.reshape(2, HALF // 2, 2 * NF, 2 * CH), mask, jnp.asarray(table_transposed()))


def on_device(spectra, plan, mask):
    return lags(spread(plan, spectra), mask)


def solution(mesh):
    return jax.shard_map(
        on_device,
        mesh=mesh,
        in_specs=(P("win", "rx", None), P(), P(None, "win", "rx")),
        out_specs=P(None, "win", "rx", None),
        check_vma=False,
    )
```

```python
import math

import jax
import jax.numpy as jnp
import numpy as np
from jax import lax
from jax.experimental import pallas as pl
from jax.experimental.pallas import tpu as pltpu
from jax.sharding import PartitionSpec as P

LAGS = 256
SAMPLES = 15000
BIN0 = 12
NF = 256
WINDOWS = 16
CH = 128
HALF = 64
GROUPS = 32
MESH = pl.DeviceIdType.MESH
NY, NZ = 4, 8
BATCH = 16
BUFFERS = 2 * BATCH


def table_transposed():
    bins = BIN0 + np.arange(NF)
    shifts = np.arange(LAGS) - LAGS // 2
    theta = 2.0 * math.pi * np.mod(bins[:, None] * shifts[None, :], SAMPLES) / SAMPLES
    scale = 1.0 / math.sqrt(NF)
    table = np.concatenate([np.cos(theta) * scale, -np.sin(theta) * scale], 0)
    table = table.astype(np.float32).astype(jnp.bfloat16).astype(np.float32)
    return np.ascontiguousarray((table / WINDOWS).T).astype(jnp.bfloat16)


def owner_of(plan_ref, block):
    rx = plan_ref[block]
    return rx // 32, (rx // 16) % 2, (rx // 2) % NZ, rx % 2


def spread_kernel(
    plan_hbm, spec_ref, cross,
    plan_ref, near, far, from_y_real, from_y_imag, relay_p, relay_m, to_z, from_z, relay_z, to_x, from_x,
    gathered, transit_p, transit_m, weights, sources,
    y_send, y_recv, relay_sems, core_sems, z_send, z_recv, zr_sems, x_send, x_recv,
    gy_send, gy_recv, ring_send, ring_recv, gc_send, gc_recv, last_send, last_recv, in_sems,
    hop1_send, hop1_recv, hop2_send, hop2_recv,
):
    from_y = (from_y_real, from_y_imag)
    rx, win = lax.axis_index("rx"), lax.axis_index("win")
    core, z, x_lo, y = rx % 2, (rx // 2) % NZ, (rx // 16) % 2, rx // 32

    def at(y_=y, x_=x_lo, z_=z, core_=core, win_=win):
        return {"rx": ((y_ * 2 + x_) * NZ + z_) * 2 + core_, "win": win_}

    def remote(src, dst, send, recv, device):
        return pltpu.make_async_remote_copy(
            src_ref=src, dst_ref=dst, send_sem=send, recv_sem=recv, device_id=device, device_id_type=MESH
        )

    def arrived(ref, recv):
        remote(ref, ref, recv, recv, at()).wait_recv()


    loads = [
        pltpu.make_async_copy(spec_ref, near, in_sems.at[0]),
        pltpu.make_async_copy(plan_hbm, plan_ref, in_sems.at[1]),
    ]
    for load in loads:
        load.start()

    plus = at(x_=1 - x_lo, win_=(win + x_lo) % 2)
    minus = at(x_=1 - x_lo, win_=(win + 1 - x_lo) % 2)
    ys = [(y + d) % NY for d in range(1, NY)]
    zs = [(z + d) % NZ for d in range(1, NZ)]
    peers = [at(y_=v) for v in ys] + [at(z_=v) for v in zs] + [at(core_=1 - core)]
    peers += [plus, minus, at(win_=1 - win), at(y_=ys[0], core_=1 - core), at(y_=ys[2], core_=1 - core)]
    barrier = pltpu.get_barrier_semaphore()
    for peer in peers:
        pl.semaphore_signal(barrier, inc=1, device_id=peer, device_id_type=MESH)
    pl.semaphore_wait(barrier, len(peers))

    sent = []

    def go(copy):
        copy.start()
        sent.append(copy)

    next_y, across, last_y = ys

    def scatter_y(c):
        part = pl.ds(c * NF, NF)
        rs, ss, rr = relay_sems.at[c], y_send.at[c], y_recv.at[c]
        go(remote(spec_ref.at[0:4, :, across, :, part], relay_p.at[c], rs.at[0], rs.at[1], at(y_=next_y)))
        go(remote(spec_ref.at[4:8, :, across, :, part], relay_m.at[c], rs.at[2], rs.at[3], at(y_=last_y)))
        mine = from_y[c].at[y, core]
        for h in range(2):
            there = at(y_=next_y, core_=h)
            go(remote(spec_ref.at[:, h, next_y, :, part], mine, ss.at[0, h], rr.at[0, core], there))
            there = at(y_=last_y, core_=h)
            go(remote(spec_ref.at[:, h, last_y, :, part], mine, ss.at[1, h], rr.at[1, core], there))
        sibling = at(core_=1 - core)
        go(remote(spec_ref.at[:, 1 - core, y, :, part], mine, core_sems.at[c, 0], core_sems.at[c, 1], sibling))

    def relay_y(c):
        rs, ss, rr = relay_sems.at[c], y_send.at[c], y_recv.at[c]
        arrived(relay_p.at[c], rs.at[1])
        place = from_y[c].at[last_y, core, 0:4]
        for h in range(2):
            go(remote(relay_p.at[c, :, h], place, ss.at[2, h], rr.at[2, core], at(y_=next_y, core_=h)))
        arrived(relay_m.at[c], rs.at[3])
        place = from_y[c].at[next_y, core, 4:8]
        for h in range(2):
            go(remote(relay_m.at[c, :, h], place, ss.at[3, h], rr.at[3, core], at(y_=last_y, core_=h)))

    def gathered_y(c):
        arrived(from_y[c].at[y, 1 - core], core_sems.at[c, 1])
        for k in range(2):
            arrived(from_y[c].at[last_y, k], y_recv.at[c, 0, k])
            arrived(from_y[c].at[next_y, k], y_recv.at[c, 1, k])
            arrived(from_y[c].at[across, k, 0:4], y_recv.at[c, 2, k])
            arrived(from_y[c].at[across, k, 4:8], y_recv.at[c, 3, k])
        for b in range(2):
            oy, _, _, oc = owner_of(plan_ref, b)
            picked = jnp.transpose(from_y[c][oy, oc].astype(jnp.float32), (1, 0, 2))
            to_z[c, :, b] = picked.reshape(NZ, 16, NF).astype(jnp.bfloat16)

    scatter_y(0)
    for i in range(4):
        go(remote(spec_ref.at[i], transit_p.at[i], hop1_send.at[i], hop1_recv.at[i], plus))
        go(remote(spec_ref.at[4 + i], transit_m.at[i], hop1_send.at[4 + i], hop1_recv.at[4 + i], minus))

    def window_pair(ref, side):
        def body(i, carry):
            both = [
                ref[2 * i + k].reshape(CH, 2 * NF).astype(jnp.float32).T.reshape(2, GROUPS, 8, CH) for k in range(2)
            ]
            a = jnp.concatenate([both[0][0], both[1][0]], 1).astype(jnp.bfloat16)
            b = jnp.concatenate([both[0][1], both[1][1]], 1)
            minus_b = (-b).astype(jnp.bfloat16)
            b = b.astype(jnp.bfloat16)
            row = pl.multiple_of(side * CH + 16 * i, 16)
            weights[:, pl.ds(row, 16), :CH] = a
            weights[:, pl.ds(HALF + row, 16), :CH] = b
            weights[:, pl.ds(row, 16), CH:] = minus_b
            weights[:, pl.ds(HALF + row, 16), CH:] = a
            return carry

        lax.fori_loop(0, 4, body, 0)

    for load in loads:
        load.wait()
    for c in range(2):
        from_y[c][y, core] = near[:, core, y, :, c * NF : (c + 1) * NF]
    relay_y(0)
    scatter_y(1)
    window_pair(near, win)
    relay_y(1)

    opposite, three_down, one_down = zs[3], zs[4], zs[6]

    def scatter_z(c):
        gathered_y(c)
        rs, ss, rr = zr_sems.at[c], z_send.at[c], z_recv.at[c]
        go(remote(to_z.at[c, opposite, 1], relay_z.at[c], rs.at[0], rs.at[1], at(z_=three_down)))
        go(remote(to_z.at[c, opposite, 0], from_z.at[c, z, 0], ss.at[3], rr.at[z], at(z_=opposite)))
        for d, v in enumerate(zs):
            if d != 3:
                go(remote(to_z.at[c, v], from_z.at[c, z], ss.at[d], rr.at[z], at(z_=v)))
        from_z[c, z] = to_z[c, z]

    def relay_back(c):
        arrived(relay_z.at[c], zr_sems.at[c, 1])
        go(remote(relay_z.at[c], from_z.at[c, zs[2], 1], zr_sems.at[c, 2], zr_sems.at[c, 3], at(z_=one_down)))

    scatter_z(0)
    relay_back(0)
    scatter_z(1)
    for i in range(4):
        arrived(transit_p.at[i], hop1_recv.at[i])
        go(remote(transit_p.at[i], far.at[i], hop2_send.at[i], hop2_recv.at[i], plus))
        arrived(transit_m.at[i], hop1_recv.at[4 + i])
        go(remote(transit_m.at[i], far.at[4 + i], hop2_send.at[4 + i], hop2_recv.at[4 + i], minus))
    relay_back(1)

    shape = (GROUPS * 16, NF)
    pick_group = (lax.broadcasted_iota(jnp.int32, shape, 1) >> 3) == (lax.broadcasted_iota(jnp.int32, shape, 0) >> 4)
    shape = (GROUPS * 16, CH)
    pick_row = (lax.broadcasted_iota(jnp.int32, shape, 1) >> 3) == (lax.broadcasted_iota(jnp.int32, shape, 0) & 15)
    f = lax.broadcasted_iota(jnp.int32, (NF, CH), 0)
    n = lax.broadcasted_iota(jnp.int32, (NF, CH), 1)
    same_place = ((f & 7) == (n & 7)).astype(jnp.float32).astype(jnp.bfloat16)
    out_row = lax.broadcasted_iota(jnp.int32, (GROUPS, GROUPS * 16), 0)
    in_row = lax.broadcasted_iota(jnp.int32, (GROUPS, GROUPS * 16), 1)
    same_group = ((in_row >> 4) == out_row).astype(jnp.float32).astype(jnp.bfloat16)

    for c in range(2):
        for d, v in enumerate(zs):
            if d != 3:
                arrived(from_z.at[c, v], z_recv.at[c, v])
        arrived(from_z.at[c, opposite, 0], z_recv.at[c, opposite])
        arrived(from_z.at[c, opposite, 1], zr_sems.at[c, 3])

    def regroup(b, carry):
        oz = owner_of(plan_ref, b)[2]
        parts = [from_z[c, oz, b].astype(jnp.float32) for c in range(2)]
        for e in range(2):
            rows = jnp.concatenate([part[8 * e : 8 * e + 8] for part in parts], 0).reshape(1, 16, NF)
            rows = jnp.broadcast_to(rows, (GROUPS, 16, NF)).reshape(GROUPS * 16, NF)
            rows = jnp.where(pick_group, rows, 0.0).astype(jnp.bfloat16)
            moved = jnp.dot(rows, same_place, preferred_element_type=jnp.float32)
            moved = jnp.where(pick_row, moved, 0.0).astype(jnp.bfloat16)
            done = jnp.dot(same_group, moved, preferred_element_type=jnp.float32)
            to_x[b, e] = done.astype(jnp.bfloat16)
        return carry

    lax.fori_loop(0, 2, regroup, 0, unroll=2)

    active = win == core
    there = from_x.at[x_lo, win]
    go(remote(to_x, there, x_send.at[0], x_recv.at[x_lo, win], at(x_=1 - x_lo, win_=core)))

    def over():
        return remote(to_x, there, x_send.at[1], x_recv.at[x_lo, win], at(win_=core))

    @pl.when(win != core)
    def _():
        over().start()

    def down(t):
        return (z + NZ - t) % NZ

    def up(t):
        return (z + t) % NZ

    def pieces(t):
        return [(0, 0), (0, 1), (1, 2), (1, 3)] if t == 3 else [(way, d) for d in range(NY) for way in range(2)]

    def piece(t, way, d):
        return gathered.at[down(t) if way == 0 else up(t), (y + d) % NY]

    def ring_piece(t, way, d):
        ref = piece(t, way, d)
        return remote(ref, ref, ring_send.at[way, t, d], ring_recv.at[way, t, d], at(z_=up(1) if way == 0 else down(1)))

    def pass_on(slot):
        ref = gathered.at[slot]
        return remote(ref, ref, gc_send.at[slot], gc_recv.at[slot], at(core_=1 - core))

    def pass_last(d):
        ref = piece(4, 0, d)
        return remote(ref, ref, last_send.at[d], last_recv.at[d], at(core_=1 - core))

    own = gathered.at[z, y]

    def over_y():
        return [remote(own, own, gy_send.at[d], gy_recv.at[y], at(y_=v)) for d, v in enumerate(ys)]

    @pl.when(active)
    def _():
        from_x[x_lo, win] = to_x[...]
        arrived(from_x.at[1 - x_lo, win], x_recv.at[1 - x_lo, win])
        arrived(from_x.at[0, 1 - win], x_recv.at[0, 1 - win])
        arrived(from_x.at[1, 1 - win], x_recv.at[1, 1 - win])

        for b in range(2):
            ox = owner_of(plan_ref, b)[1]
            for w in range(2):
                gathered[z, y, b, :, :, w * CH : (w + 1) * CH] = from_x[ox, w, b]
        for copy in over_y():
            copy.start()
        for way in range(2):
            ring_piece(0, way, 0).start()

    for i in range(8):
        arrived(far.at[i], hop2_recv.at[i])
    window_pair(far, 1 - win)

    lane = lax.broadcasted_iota(jnp.int32, (1, 8, 2 * CH), 2)
    sub = lax.broadcasted_iota(jnp.int32, (1, 8, 2 * CH), 1)
    diagonal = (lane & 7) == sub

    def correlate(slots, part=None):
        count = len(slots)

        def unpack(v, carry):
            for i, slot in enumerate(slots):
                sources[i, v] = gathered[slot, v].astype(jnp.float32)
            return carry

        if part != 1:
            lax.fori_loop(0, NY, unpack, 0)

        def product(g):
            row = sources[:count, :, :, :, pl.ds(g, 1), :].reshape(count * 16, 1, 2 * CH)
            spread = jnp.where(diagonal, row, 0.0)
            spread = spread.reshape(count * 16 * 8, 2 * CH).astype(jnp.bfloat16)
            res = jnp.dot(spread, weights[g], preferred_element_type=jnp.float32)
            return res.reshape(count * 16, 8, 2 * CH)

        def bins(gg, carry):
            res = jnp.concatenate([product(2 * gg), product(2 * gg + 1)], 1)
            res = res.astype(jnp.bfloat16).reshape(count, NY, 2, 2, 16, 2 * CH)
            row = pl.multiple_of(gg * 16, 16)
            for i, slot in enumerate(slots):
                for b in range(2):
                    for c in range(2):
                        for s in range(2):
                            cross[b, :, slot, pl.ds(c * NF + row, 16), s * CH : (s + 1) * CH] = res[
                                i, :, b, s, :, c * CH : (c + 1) * CH
                            ]
            return carry

        quarter = GROUPS // 4
        lax.fori_loop(quarter if part == 1 else 0, quarter if part == 0 else 2 * quarter, bins, 0, unroll=4)

    def receive(t, late):
        for way, d in pieces(t - 1):
            if (d >= 2) == bool(late):
                arrived(piece(t, way, d), ring_recv.at[way, t - 1, d])
                if t == 4:
                    pass_last(d).start()
                elif (way, d) in pieces(t):
                    ring_piece(t, way, d).start()

    slots = [[z], [down(1), up(1)], [down(2), up(2)], [down(3), up(3)], [up(4)]]
    done = sum(slots, [])
    for t in range(5):

        @pl.when(active)
        def _():
            if t == 0:
                for d, v in enumerate(ys):
                    arrived(gathered.at[z, v], gy_recv.at[v])
                    for way in range(2):
                        ring_piece(0, way, d + 1).start()
            else:
                if t == 1:
                    receive(t, 0)
                receive(t, 1)
            if t < 4:
                for slot in slots[t]:
                    pass_on(slot).start()

        @pl.when(win != core)
        def _():
            if t < 4:
                for slot in slots[t]:
                    arrived(gathered.at[slot], gc_recv.at[slot])
            else:
                for d in range(NY):
                    arrived(piece(4, 0, d), last_recv.at[d])

        if 0 < t < 4:
            correlate(slots[t], 0)

            @pl.when(active)
            def _():
                receive(t + 1, 0)

            correlate(slots[t], 1)
        else:
            correlate(slots[t])

    for copy in sent:
        copy.wait_send()

    @pl.when(win != core)
    def _():
        over().wait_send()

    @pl.when(active)
    def _():
        for copy in over_y() + [pass_on(slot) for slot in done[:7]] + [pass_last(d) for d in range(NY)]:
            copy.wait_send()
        for t in range(4):
            for way, d in pieces(t):
                ring_piece(t, way, d).wait_send()


def spread(plan, spectra):
    bf = jnp.bfloat16
    dma = pltpu.SemaphoreType.DMA
    natural = (2, NY, 16, 2 * NF)
    return pl.pallas_call(
        spread_kernel,
        out_shape=jax.ShapeDtypeStruct((2, NY, NZ, 2 * NF, 2 * CH), bf),
        in_specs=[pl.BlockSpec(memory_space=pltpu.HBM), pl.BlockSpec(memory_space=pltpu.HBM)],
        out_specs=pl.BlockSpec(memory_space=pltpu.VMEM),
        scratch_shapes=[
            pltpu.SMEM((2,), jnp.int32),
            pltpu.VMEM((8,) + natural, bf),
            pltpu.VMEM((8,) + natural, bf),
            pltpu.VMEM((NY, 2, 8, 16, NF), bf),
            pltpu.VMEM((NY, 2, 8, 16, NF), bf),
            pltpu.VMEM((2, 4, 2, 16, NF), bf),
            pltpu.VMEM((2, 4, 2, 16, NF), bf),
            pltpu.VMEM((2, NZ, 2, 16, NF), bf),
            pltpu.VMEM((2, NZ, 2, 16, NF), bf),
            pltpu.VMEM((2, 16, NF), bf),
            pltpu.VMEM((2, 2, GROUPS, CH), bf),
            pltpu.VMEM((2, 2, 2, 2, GROUPS, CH), bf),
            pltpu.VMEM((NZ, NY, 2, 2, GROUPS, 2 * CH), bf),
            pltpu.VMEM((4,) + natural, bf),
            pltpu.VMEM((4,) + natural, bf),
            pltpu.VMEM((GROUPS, 2 * CH, 2 * CH), bf),
            pltpu.VMEM((2, NY, 2, 2, GROUPS, 2 * CH), jnp.float32),
            dma((2, 4, 2)), dma((2, 4, 2)), dma((2, 4)), dma((2, 2)), dma((2, 7)), dma((2, NZ)), dma((2, 4)),
            dma((2,)), dma((2, 2)),
            dma((3,)), dma((NY,)), dma((2, 4, NY)), dma((2, 4, NY)), dma((NZ,)), dma((NZ,)), dma((NY,)), dma((NY,)), dma((2,)),
            dma((8,)), dma((8,)), dma((8,)), dma((8,)),
        ],
        compiler_params=pltpu.CompilerParams(
            collective_id=0, has_side_effects=True, vmem_limit_bytes=28 * 1024 * 1024
        ),
    )(
        pltpu.with_memory_space_constraint(plan, pltpu.HBM),
        pltpu.with_memory_space_constraint(spectra.reshape((8,) + natural), pltpu.HBM),
    )


def lag_kernel(cross, mask_ref, table_ref, out_ref, stage, out_sems):
    half = HALF // 2

    def result(p):
        slot = lax.rem(p, BUFFERS)
        place = out_ref.at[p // half, pl.ds(2 * lax.rem(p, half), 2)]
        return pltpu.make_async_copy(stage.at[slot], place, out_sems.at[slot])

    def batch(i, drain):
        pairs = [BATCH * i + k for k in range(BATCH)]
        if drain:
            for p in pairs:
                result(p - BUFFERS).wait()
        for p in pairs:
            b, row = p // half, 2 * lax.rem(p, half)
            lagged = jnp.dot(table_ref[...], cross[b, lax.rem(p, half)], preferred_element_type=jnp.float32)
            for s in range(2):
                keep = mask_ref[b, pl.ds(row + s, 1), :].astype(jnp.float32)
                kept = (lagged[:, s * CH : (s + 1) * CH] * keep).astype(jnp.bfloat16)
                stage[lax.rem(p, BUFFERS), s] = kept.T
        for p in pairs:
            result(p).start()

    def first(i, carry):
        batch(i, False)
        return carry

    def rest(i, carry):
        batch(i, True)
        return carry

    lax.fori_loop(0, 2, first, 0)
    lax.fori_loop(2, HALF // BATCH, rest, 0)
    for k in range(BUFFERS):
        result(HALF - BUFFERS + k).wait()


def lags(cross, mask):
    vmem = pl.BlockSpec(memory_space=pltpu.VMEM)
    return pl.pallas_call(
        lag_kernel,
        out_shape=jax.ShapeDtypeStruct((2, HALF, CH, LAGS), jnp.bfloat16),
        in_specs=[vmem, vmem, vmem],
        out_specs=pl.BlockSpec(memory_space=pltpu.HBM),
        scratch_shapes=[
            pltpu.VMEM((BUFFERS, 2, CH, LAGS), jnp.bfloat16),
            pltpu.SemaphoreType.DMA((BUFFERS,)),
        ],
        compiler_params=pltpu.CompilerParams(vmem_limit_bytes=28 * 1024 * 1024),
    )(cross.reshape(2, HALF // 2, 2 * NF, 2 * CH), mask, jnp.asarray(table_transposed()))


def on_device(spectra, plan, mask):
    return lags(spread(plan, spectra), mask)


def solution(mesh):
    return jax.shard_map(
        on_device,
        mesh=mesh,
        in_specs=(P("win", "rx", None), P(), P(None, "win", "rx")),
        out_specs=P(None, "win", "rx", None),
        check_vma=False,
    )
```

```python
import math

import jax
import jax.numpy as jnp
import numpy as np
from jax import lax
from jax.experimental import pallas as pl
from jax.experimental.pallas import tpu as pltpu
from jax.sharding import PartitionSpec as P

LAGS = 256
SAMPLES = 15000
BIN0 = 12
NF = 256
WINDOWS = 16
CH = 128
HALF = 64
GROUPS = 32
MESH = pl.DeviceIdType.MESH
NY, NZ = 4, 8
BATCH = 16
BUFFERS = 2 * BATCH


def table_transposed():
    bins = BIN0 + np.arange(NF)
    shifts = np.arange(LAGS) - LAGS // 2
    theta = 2.0 * math.pi * np.mod(bins[:, None] * shifts[None, :], SAMPLES) / SAMPLES
    scale = 1.0 / math.sqrt(NF)
    table = np.concatenate([np.cos(theta) * scale, -np.sin(theta) * scale], 0)
    table = table.astype(np.float32).astype(jnp.bfloat16).astype(np.float32)
    return np.ascontiguousarray((table / WINDOWS).T).astype(jnp.bfloat16)


def owner_of(plan_ref, block):
    rx = plan_ref[block]
    return rx // 32, (rx // 16) % 2, (rx // 2) % NZ, rx % 2


def spread_kernel(
    plan_hbm, spec_ref, cross,
    plan_ref, near, far, from_y, relay_p, relay_m, to_z, from_z, relay_z, to_x, from_x,
    gathered, transit_p, transit_m, weights, sources,
    y_send, y_recv, relay_sems, core_sems, z_send, z_recv, zr_sems, x_send, x_recv,
    gy_send, gy_recv, ring_send, ring_recv, gc_send, gc_recv, last_send, last_recv, in_sems,
    hop1_send, hop1_recv, hop2_send, hop2_recv,
):
    rx, win = lax.axis_index("rx"), lax.axis_index("win")
    core, z, x_lo, y = rx % 2, (rx // 2) % NZ, (rx // 16) % 2, rx // 32

    def at(y_=y, x_=x_lo, z_=z, core_=core, win_=win):
        return {"rx": ((y_ * 2 + x_) * NZ + z_) * 2 + core_, "win": win_}

    def remote(src, dst, send, recv, device):
        return pltpu.make_async_remote_copy(
            src_ref=src, dst_ref=dst, send_sem=send, recv_sem=recv, device_id=device, device_id_type=MESH
        )

    def arrived(ref, recv):
        remote(ref, ref, recv, recv, at()).wait_recv()


    loads = [
        pltpu.make_async_copy(spec_ref, near, in_sems.at[0]),
        pltpu.make_async_copy(plan_hbm, plan_ref, in_sems.at[1]),
    ]
    for load in loads:
        load.start()

    plus = at(x_=1 - x_lo, win_=(win + x_lo) % 2)
    minus = at(x_=1 - x_lo, win_=(win + 1 - x_lo) % 2)
    ys = [(y + d) % NY for d in range(1, NY)]
    zs = [(z + d) % NZ for d in range(1, NZ)]
    peers = [at(y_=v) for v in ys] + [at(z_=v) for v in zs] + [at(core_=1 - core)]
    peers += [plus, minus, at(win_=1 - win), at(y_=ys[0], core_=1 - core), at(y_=ys[2], core_=1 - core)]
    barrier = pltpu.get_barrier_semaphore()
    for peer in peers:
        pl.semaphore_signal(barrier, inc=1, device_id=peer, device_id_type=MESH)
    pl.semaphore_wait(barrier, len(peers))

    sent = []

    def go(copy):
        copy.start()
        sent.append(copy)

    next_y, across, last_y = ys

    def hop1(i):
        go(remote(spec_ref.at[i], transit_p.at[i], hop1_send.at[i], hop1_recv.at[i], plus))
        go(remote(spec_ref.at[4 + i], transit_m.at[i], hop1_send.at[4 + i], hop1_recv.at[4 + i], minus))

    go(remote(spec_ref.at[0:4, :, across], relay_p, relay_sems.at[0], relay_sems.at[1], at(y_=next_y)))
    go(remote(spec_ref.at[4:8, :, across], relay_m, relay_sems.at[2], relay_sems.at[3], at(y_=last_y)))
    hop1(0)
    mine = from_y.at[y, core]
    for h in range(2):
        go(remote(spec_ref.at[:, h, next_y], mine, y_send.at[0, h], y_recv.at[0, core], at(y_=next_y, core_=h)))
        go(remote(spec_ref.at[:, h, last_y], mine, y_send.at[1, h], y_recv.at[1, core], at(y_=last_y, core_=h)))
    go(remote(spec_ref.at[:, 1 - core, y], mine, core_sems.at[0], core_sems.at[1], at(core_=1 - core)))
    for i in range(1, 4):
        hop1(i)

    def window_pair(ref, side, first):
        def body(i, carry):
            both = [
                ref[2 * i + k].reshape(CH, 2 * NF).astype(jnp.float32).T.reshape(2, GROUPS, 8, CH) for k in range(2)
            ]
            a = jnp.concatenate([both[0][0], both[1][0]], 1).astype(jnp.bfloat16)
            b = jnp.concatenate([both[0][1], both[1][1]], 1)
            minus_b = (-b).astype(jnp.bfloat16)
            b = b.astype(jnp.bfloat16)
            row = pl.multiple_of(side * CH + 16 * i, 16)
            weights[:, pl.ds(row, 16), :CH] = a
            weights[:, pl.ds(HALF + row, 16), :CH] = b
            weights[:, pl.ds(row, 16), CH:] = minus_b
            weights[:, pl.ds(HALF + row, 16), CH:] = a
            return carry

        lax.fori_loop(0, 2, lambda i, carry: body(first + 2 * i, carry), 0, unroll=2)

    for load in loads:
        load.wait()
    from_y[y, core] = near[:, core, y]
    def forward(i):
        arrived(transit_p.at[i], hop1_recv.at[i])
        go(remote(transit_p.at[i], far.at[i], hop2_send.at[i], hop2_recv.at[i], plus))
        arrived(transit_m.at[i], hop1_recv.at[4 + i])
        go(remote(transit_m.at[i], far.at[4 + i], hop2_send.at[4 + i], hop2_recv.at[4 + i], minus))

    arrived(relay_p, relay_sems.at[1])
    place = from_y.at[last_y, core, 0:4]
    for h in range(2):
        go(remote(relay_p.at[:, h], place, y_send.at[2, h], y_recv.at[2, core], at(y_=next_y, core_=h)))
    arrived(relay_m, relay_sems.at[3])
    place = from_y.at[next_y, core, 4:8]
    for h in range(2):
        go(remote(relay_m.at[:, h], place, y_send.at[3, h], y_recv.at[3, core], at(y_=last_y, core_=h)))
    forward(0)
    window_pair(near, win, 0)
    forward(1)
    window_pair(near, win, 1)

    forward(2)
    forward(3)
    arrived(from_y.at[y, 1 - core], core_sems.at[1])
    for k in range(2):
        arrived(from_y.at[last_y, k], y_recv.at[0, k])
        arrived(from_y.at[next_y, k], y_recv.at[1, k])
        arrived(from_y.at[across, k, 0:4], y_recv.at[2, k])
        arrived(from_y.at[across, k, 4:8], y_recv.at[3, k])
    for b in range(2):
        oy, _, _, oc = owner_of(plan_ref, b)
        picked = jnp.transpose(from_y[oy, oc].astype(jnp.float32), (1, 0, 2))
        picked = jnp.concatenate([picked[:, :, :NF], picked[:, :, NF:]], 1)
        to_z[:, b] = picked.astype(jnp.bfloat16).reshape(NZ, 2, 16, NF)

    opposite, three_down, one_down = zs[3], zs[4], zs[6]
    go(remote(to_z.at[opposite, :, 1], relay_z, zr_sems.at[0], zr_sems.at[1], at(z_=three_down)))
    go(remote(to_z.at[opposite, :, 0], from_z.at[z, :, 0], z_send.at[3], z_recv.at[z], at(z_=opposite)))
    for d, v in enumerate(zs):
        if d != 3:
            go(remote(to_z.at[v], from_z.at[z], z_send.at[d], z_recv.at[z], at(z_=v)))
    from_z[z] = to_z[z]

    shape = (GROUPS * 16, NF)
    pick_group = (lax.broadcasted_iota(jnp.int32, shape, 1) >> 3) == (lax.broadcasted_iota(jnp.int32, shape, 0) >> 4)
    shape = (GROUPS * 16, CH)
    pick_row = (lax.broadcasted_iota(jnp.int32, shape, 1) >> 3) == (lax.broadcasted_iota(jnp.int32, shape, 0) & 15)
    f = lax.broadcasted_iota(jnp.int32, (NF, CH), 0)
    n = lax.broadcasted_iota(jnp.int32, (NF, CH), 1)
    same_place = ((f & 7) == (n & 7)).astype(jnp.float32).astype(jnp.bfloat16)
    out_row = lax.broadcasted_iota(jnp.int32, (GROUPS, GROUPS * 16), 0)
    in_row = lax.broadcasted_iota(jnp.int32, (GROUPS, GROUPS * 16), 1)
    same_group = ((in_row >> 4) == out_row).astype(jnp.float32).astype(jnp.bfloat16)

    arrived(relay_z, zr_sems.at[1])
    go(remote(relay_z, from_z.at[zs[2], :, 1], zr_sems.at[2], zr_sems.at[3], at(z_=one_down)))
    for d, v in enumerate(zs):
        if d != 3:
            arrived(from_z.at[v], z_recv.at[v])
    arrived(from_z.at[opposite, :, 0], z_recv.at[opposite])
    arrived(from_z.at[opposite, :, 1], zr_sems.at[3])

    def regroup(i, carry):
        b, e = i // 2, i % 2
        rows = from_z[owner_of(plan_ref, b)[2], b, e].astype(jnp.float32).reshape(1, 16, NF)
        rows = jnp.broadcast_to(rows, (GROUPS, 16, NF)).reshape(GROUPS * 16, NF)
        rows = jnp.where(pick_group, rows, 0.0).astype(jnp.bfloat16)
        moved = jnp.dot(rows, same_place, preferred_element_type=jnp.float32)
        moved = jnp.where(pick_row, moved, 0.0).astype(jnp.bfloat16)
        done = jnp.dot(same_group, moved, preferred_element_type=jnp.float32)
        to_x[b, e] = done.astype(jnp.bfloat16)
        return carry

    lax.fori_loop(0, 4, regroup, 0, unroll=2)

    active = win == core
    there = from_x.at[x_lo, win]
    go(remote(to_x, there, x_send.at[0], x_recv.at[x_lo, win], at(x_=1 - x_lo, win_=core)))

    def over():
        return remote(to_x, there, x_send.at[1], x_recv.at[x_lo, win], at(win_=core))

    @pl.when(win != core)
    def _():
        over().start()

    def down(t):
        return (z + NZ - t) % NZ

    def up(t):
        return (z + t) % NZ

    def pieces(t):
        return [(0, 0), (0, 1), (1, 2), (1, 3)] if t == 3 else [(way, d) for d in range(NY) for way in range(2)]

    def piece(t, way, d):
        return gathered.at[down(t) if way == 0 else up(t), (y + d) % NY]

    def ring_piece(t, way, d):
        ref = piece(t, way, d)
        return remote(ref, ref, ring_send.at[way, t, d], ring_recv.at[way, t, d], at(z_=up(1) if way == 0 else down(1)))

    def pass_on(slot):
        ref = gathered.at[slot]
        return remote(ref, ref, gc_send.at[slot], gc_recv.at[slot], at(core_=1 - core))

    def pass_last(d):
        ref = piece(4, 0, d)
        return remote(ref, ref, last_send.at[d], last_recv.at[d], at(core_=1 - core))

    own = gathered.at[z, y]

    def over_y():
        return [remote(own, own, gy_send.at[d], gy_recv.at[y], at(y_=v)) for d, v in enumerate(ys)]

    @pl.when(active)
    def _():
        from_x[x_lo, win] = to_x[...]
        arrived(from_x.at[1 - x_lo, win], x_recv.at[1 - x_lo, win])
        arrived(from_x.at[0, 1 - win], x_recv.at[0, 1 - win])
        arrived(from_x.at[1, 1 - win], x_recv.at[1, 1 - win])

        for b in range(2):
            ox = owner_of(plan_ref, b)[1]
            for w in range(2):
                gathered[z, y, b, :, :, w * CH : (w + 1) * CH] = from_x[ox, w, b]
        for copy in over_y():
            copy.start()
        for way in range(2):
            ring_piece(0, way, 0).start()

    for first in range(2):
        for i in (2 * first, 2 * first + 1):
            arrived(far.at[i], hop2_recv.at[i])
            arrived(far.at[4 + i], hop2_recv.at[4 + i])
        window_pair(far, 1 - win, first)

    lane = lax.broadcasted_iota(jnp.int32, (1, 8, 2 * CH), 2)
    sub = lax.broadcasted_iota(jnp.int32, (1, 8, 2 * CH), 1)
    diagonal = (lane & 7) == sub

    def correlate(slots, part=None):
        count = len(slots)

        def unpack(v, carry):
            for i, slot in enumerate(slots):
                sources[i, v] = gathered[slot, v].astype(jnp.float32)
            return carry

        if part != 1:
            lax.fori_loop(0, NY, unpack, 0)

        def product(g):
            row = sources[:count, :, :, :, pl.ds(g, 1), :].reshape(count * 16, 1, 2 * CH)
            spread = jnp.where(diagonal, row, 0.0)
            spread = spread.reshape(count * 16 * 8, 2 * CH).astype(jnp.bfloat16)
            res = jnp.dot(spread, weights[g], preferred_element_type=jnp.float32)
            return res.reshape(count * 16, 8, 2 * CH)

        def bins(gg, carry):
            res = jnp.concatenate([product(2 * gg), product(2 * gg + 1)], 1)
            res = res.astype(jnp.bfloat16).reshape(count, NY, 2, 2, 16, 2 * CH)
            row = pl.multiple_of(gg * 16, 16)
            for i, slot in enumerate(slots):
                for b in range(2):
                    for c in range(2):
                        for s in range(2):
                            cross[b, :, slot, pl.ds(c * NF + row, 16), s * CH : (s + 1) * CH] = res[
                                i, :, b, s, :, c * CH : (c + 1) * CH
                            ]
            return carry

        quarter = GROUPS // 4
        lax.fori_loop(quarter if part == 1 else 0, quarter if part == 0 else 2 * quarter, bins, 0, unroll=4)

    def receive(t, late):
        for way, d in pieces(t - 1):
            if (d >= 2) == bool(late):
                arrived(piece(t, way, d), ring_recv.at[way, t - 1, d])
                if t == 4:
                    pass_last(d).start()
                elif (way, d) in pieces(t):
                    ring_piece(t, way, d).start()

    slots = [[z], [down(1), up(1)], [down(2), up(2)], [down(3), up(3)], [up(4)]]
    done = sum(slots, [])
    for t in range(5):

        @pl.when(active)
        def _():
            if t == 0:
                for d, v in enumerate(ys):
                    arrived(gathered.at[z, v], gy_recv.at[v])
                    for way in range(2):
                        ring_piece(0, way, d + 1).start()
            else:
                if t == 1:
                    receive(t, 0)
                receive(t, 1)
            if t < 4:
                for slot in slots[t]:
                    pass_on(slot).start()

        @pl.when(win != core)
        def _():
            if t < 4:
                for slot in slots[t]:
                    arrived(gathered.at[slot], gc_recv.at[slot])
            else:
                for d in range(NY):
                    arrived(piece(4, 0, d), last_recv.at[d])

        if 0 < t < 4:
            correlate(slots[t], 0)

            @pl.when(active)
            def _():
                receive(t + 1, 0)

            correlate(slots[t], 1)
        else:
            correlate(slots[t])

    for copy in sent:
        copy.wait_send()

    @pl.when(win != core)
    def _():
        over().wait_send()

    @pl.when(active)
    def _():
        for copy in over_y() + [pass_on(slot) for slot in done[:7]] + [pass_last(d) for d in range(NY)]:
            copy.wait_send()
        for t in range(4):
            for way, d in pieces(t):
                ring_piece(t, way, d).wait_send()


def spread(plan, spectra):
    bf = jnp.bfloat16
    piece = (2, 16, NF)
    dma = pltpu.SemaphoreType.DMA
    natural = (2, NY, 16, 2 * NF)
    return pl.pallas_call(
        spread_kernel,
        out_shape=jax.ShapeDtypeStruct((2, NY, NZ, 2 * NF, 2 * CH), bf),
        in_specs=[pl.BlockSpec(memory_space=pltpu.HBM), pl.BlockSpec(memory_space=pltpu.HBM)],
        out_specs=pl.BlockSpec(memory_space=pltpu.VMEM),
        scratch_shapes=[
            pltpu.SMEM((2,), jnp.int32),
            pltpu.VMEM((8,) + natural, bf),
            pltpu.VMEM((8,) + natural, bf),
            pltpu.VMEM((NY, 2, 8, 16, 2 * NF), bf),
            pltpu.VMEM((4, 2, 16, 2 * NF), bf),
            pltpu.VMEM((4, 2, 16, 2 * NF), bf),
            pltpu.VMEM((NZ, 2) + piece, bf),
            pltpu.VMEM((NZ, 2) + piece, bf),
            pltpu.VMEM(piece, bf),
            pltpu.VMEM((2, 2, GROUPS, CH), bf),
            pltpu.VMEM((2, 2, 2, 2, GROUPS, CH), bf),
            pltpu.VMEM((NZ, NY, 2, 2, GROUPS, 2 * CH), bf),
            pltpu.VMEM((4,) + natural, bf),
            pltpu.VMEM((4,) + natural, bf),
            pltpu.VMEM((GROUPS, 2 * CH, 2 * CH), bf),
            pltpu.VMEM((2, NY, 2, 2, GROUPS, 2 * CH), jnp.float32),
            dma((4, 2)), dma((4, 2)), dma((4,)), dma((2,)), dma((7,)), dma((NZ,)), dma((4,)), dma((2,)), dma((2, 2)),
            dma((3,)), dma((NY,)), dma((2, 4, NY)), dma((2, 4, NY)), dma((NZ,)), dma((NZ,)), dma((NY,)), dma((NY,)), dma((2,)),
            dma((8,)), dma((8,)), dma((8,)), dma((8,)),
        ],
        compiler_params=pltpu.CompilerParams(
            collective_id=0, has_side_effects=True, vmem_limit_bytes=28 * 1024 * 1024
        ),
    )(
        pltpu.with_memory_space_constraint(plan, pltpu.HBM),
        pltpu.with_memory_space_constraint(spectra.reshape((8,) + natural), pltpu.HBM),
    )


def lag_kernel(cross, mask_ref, table_ref, out_ref, stage, out_sems):
    half = HALF // 2

    def result(p):
        slot = lax.rem(p, BUFFERS)
        place = out_ref.at[p // half, pl.ds(2 * lax.rem(p, half), 2)]
        return pltpu.make_async_copy(stage.at[slot], place, out_sems.at[slot])

    def batch(i, drain):
        pairs = [BATCH * i + k for k in range(BATCH)]
        if drain:
            for p in pairs:
                result(p - BUFFERS).wait()
        for p in pairs:
            b, row = p // half, 2 * lax.rem(p, half)
            lagged = jnp.dot(table_ref[...], cross[b, lax.rem(p, half)], preferred_element_type=jnp.float32)
            for s in range(2):
                keep = mask_ref[b, pl.ds(row + s, 1), :].astype(jnp.float32)
                kept = (lagged[:, s * CH : (s + 1) * CH] * keep).astype(jnp.bfloat16)
                stage[lax.rem(p, BUFFERS), s] = kept.T
        for p in pairs:
            result(p).start()

    def first(i, carry):
        batch(i, False)
        return carry

    def rest(i, carry):
        batch(i, True)
        return carry

    lax.fori_loop(0, 2, first, 0)
    lax.fori_loop(2, HALF // BATCH, rest, 0)
    for k in range(BUFFERS):
        result(HALF - BUFFERS + k).wait()


def lags(cross, mask):
    vmem = pl.BlockSpec(memory_space=pltpu.VMEM)
    return pl.pallas_call(
        lag_kernel,
        out_shape=jax.ShapeDtypeStruct((2, HALF, CH, LAGS), jnp.bfloat16),
        in_specs=[vmem, vmem, vmem],
        out_specs=pl.BlockSpec(memory_space=pltpu.HBM),
        scratch_shapes=[
            pltpu.VMEM((BUFFERS, 2, CH, LAGS), jnp.bfloat16),
            pltpu.SemaphoreType.DMA((BUFFERS,)),
        ],
        compiler_params=pltpu.CompilerParams(vmem_limit_bytes=28 * 1024 * 1024),
    )(cross.reshape(2, HALF // 2, 2 * NF, 2 * CH), mask, jnp.asarray(table_transposed()))


def on_device(spectra, plan, mask):
    return lags(spread(plan, spectra), mask)


def solution(mesh):
    return jax.shard_map(
        on_device,
        mesh=mesh,
        in_specs=(P("win", "rx", None), P(), P(None, "win", "rx")),
        out_specs=P(None, "win", "rx", None),
        check_vma=False,
    )
```

```python
import math

import jax
import jax.numpy as jnp
import numpy as np
from jax import lax
from jax.experimental import pallas as pl
from jax.experimental.pallas import tpu as pltpu
from jax.sharding import PartitionSpec as P

LAGS = 256
SAMPLES = 15000
BIN0 = 12
NF = 256
WINDOWS = 16
CH = 128
HALF = 64
GROUPS = 32
MESH = pl.DeviceIdType.MESH
NY, NZ = 4, 8
BATCH = 16
BUFFERS = 2 * BATCH


def table_transposed():
    bins = BIN0 + np.arange(NF)
    shifts = np.arange(LAGS) - LAGS // 2
    theta = 2.0 * math.pi * np.mod(bins[:, None] * shifts[None, :], SAMPLES) / SAMPLES
    scale = 1.0 / math.sqrt(NF)
    table = np.concatenate([np.cos(theta) * scale, -np.sin(theta) * scale], 0)
    table = table.astype(np.float32).astype(jnp.bfloat16).astype(np.float32)
    return np.ascontiguousarray((table / WINDOWS).T).astype(jnp.bfloat16)


def owner_of(plan_ref, block):
    rx = plan_ref[block]
    return rx // 32, (rx // 16) % 2, (rx // 2) % NZ, rx % 2


def spread_kernel(
    plan_hbm, spec_ref, cross,
    plan_ref, near, far, from_y, relay_p, relay_m, to_z, from_z, relay_z, to_x, from_x,
    gathered, transit_p, transit_m, weights, sources,
    y_send, y_recv, relay_sems, core_sems, z_send, z_recv, zr_sems, x_send, x_recv,
    gy_send, gy_recv, ring_send, ring_recv, gc_send, gc_recv, in_sems,
    hop1_send, hop1_recv, hop2_send, hop2_recv,
):
    rx, win = lax.axis_index("rx"), lax.axis_index("win")
    core, z, x_lo, y = rx % 2, (rx // 2) % NZ, (rx // 16) % 2, rx // 32

    def at(y_=y, x_=x_lo, z_=z, core_=core, win_=win):
        return {"rx": ((y_ * 2 + x_) * NZ + z_) * 2 + core_, "win": win_}

    def remote(src, dst, send, recv, device):
        return pltpu.make_async_remote_copy(
            src_ref=src, dst_ref=dst, send_sem=send, recv_sem=recv, device_id=device, device_id_type=MESH
        )

    def arrived(ref, recv):
        remote(ref, ref, recv, recv, at()).wait_recv()


    loads = [
        pltpu.make_async_copy(spec_ref, near, in_sems.at[0]),
        pltpu.make_async_copy(plan_hbm, plan_ref, in_sems.at[1]),
    ]
    for load in loads:
        load.start()

    plus = at(x_=1 - x_lo, win_=(win + x_lo) % 2)
    minus = at(x_=1 - x_lo, win_=(win + 1 - x_lo) % 2)
    ys = [(y + d) % NY for d in range(1, NY)]
    zs = [(z + d) % NZ for d in range(1, NZ)]
    peers = [at(y_=v) for v in ys] + [at(z_=v) for v in zs] + [at(core_=1 - core)]
    peers += [plus, minus, at(win_=1 - win), at(y_=ys[0], core_=1 - core), at(y_=ys[2], core_=1 - core)]
    barrier = pltpu.get_barrier_semaphore()
    for peer in peers:
        pl.semaphore_signal(barrier, inc=1, device_id=peer, device_id_type=MESH)
    pl.semaphore_wait(barrier, len(peers))

    sent = []

    def go(copy):
        copy.start()
        sent.append(copy)

    next_y, across, last_y = ys

    def hop1(i):
        go(remote(spec_ref.at[i], transit_p.at[i], hop1_send.at[i], hop1_recv.at[i], plus))
        go(remote(spec_ref.at[4 + i], transit_m.at[i], hop1_send.at[4 + i], hop1_recv.at[4 + i], minus))

    go(remote(spec_ref.at[0:4, :, across], relay_p, relay_sems.at[0], relay_sems.at[1], at(y_=next_y)))
    go(remote(spec_ref.at[4:8, :, across], relay_m, relay_sems.at[2], relay_sems.at[3], at(y_=last_y)))
    hop1(0)
    mine = from_y.at[y, core]
    for h in range(2):
        go(remote(spec_ref.at[:, h, next_y], mine, y_send.at[0, h], y_recv.at[0, core], at(y_=next_y, core_=h)))
        go(remote(spec_ref.at[:, h, last_y], mine, y_send.at[1, h], y_recv.at[1, core], at(y_=last_y, core_=h)))
    go(remote(spec_ref.at[:, 1 - core, y], mine, core_sems.at[0], core_sems.at[1], at(core_=1 - core)))
    for i in range(1, 4):
        hop1(i)

    def window_pair(ref, side, first):
        def body(i, carry):
            both = [
                ref[2 * i + k].reshape(CH, 2 * NF).astype(jnp.float32).T.reshape(2, GROUPS, 8, CH) for k in range(2)
            ]
            a = jnp.concatenate([both[0][0], both[1][0]], 1).astype(jnp.bfloat16)
            b = jnp.concatenate([both[0][1], both[1][1]], 1)
            minus_b = (-b).astype(jnp.bfloat16)
            b = b.astype(jnp.bfloat16)
            row = pl.multiple_of(side * CH + 16 * i, 16)
            weights[:, pl.ds(row, 16), :CH] = a
            weights[:, pl.ds(HALF + row, 16), :CH] = b
            weights[:, pl.ds(row, 16), CH:] = minus_b
            weights[:, pl.ds(HALF + row, 16), CH:] = a
            return carry

        lax.fori_loop(0, 2, lambda i, carry: body(first + 2 * i, carry), 0, unroll=2)

    for load in loads:
        load.wait()
    from_y[y, core] = near[:, core, y]
    def forward(i):
        arrived(transit_p.at[i], hop1_recv.at[i])
        go(remote(transit_p.at[i], far.at[i], hop2_send.at[i], hop2_recv.at[i], plus))
        arrived(transit_m.at[i], hop1_recv.at[4 + i])
        go(remote(transit_m.at[i], far.at[4 + i], hop2_send.at[4 + i], hop2_recv.at[4 + i], minus))

    arrived(relay_p, relay_sems.at[1])
    place = from_y.at[last_y, core, 0:4]
    for h in range(2):
        go(remote(relay_p.at[:, h], place, y_send.at[2, h], y_recv.at[2, core], at(y_=next_y, core_=h)))
    arrived(relay_m, relay_sems.at[3])
    place = from_y.at[next_y, core, 4:8]
    for h in range(2):
        go(remote(relay_m.at[:, h], place, y_send.at[3, h], y_recv.at[3, core], at(y_=last_y, core_=h)))
    forward(0)
    window_pair(near, win, 0)
    forward(1)
    window_pair(near, win, 1)

    forward(2)
    forward(3)
    arrived(from_y.at[y, 1 - core], core_sems.at[1])
    for k in range(2):
        arrived(from_y.at[last_y, k], y_recv.at[0, k])
        arrived(from_y.at[next_y, k], y_recv.at[1, k])
        arrived(from_y.at[across, k, 0:4], y_recv.at[2, k])
        arrived(from_y.at[across, k, 4:8], y_recv.at[3, k])
    for b in range(2):
        oy, _, _, oc = owner_of(plan_ref, b)
        picked = jnp.transpose(from_y[oy, oc].astype(jnp.float32), (1, 0, 2))
        picked = jnp.concatenate([picked[:, :, :NF], picked[:, :, NF:]], 1)
        to_z[:, b] = picked.astype(jnp.bfloat16).reshape(NZ, 2, 16, NF)

    opposite, three_down, one_down = zs[3], zs[4], zs[6]
    go(remote(to_z.at[opposite, :, 1], relay_z, zr_sems.at[0], zr_sems.at[1], at(z_=three_down)))
    go(remote(to_z.at[opposite, :, 0], from_z.at[z, :, 0], z_send.at[3], z_recv.at[z], at(z_=opposite)))
    for d, v in enumerate(zs):
        if d != 3:
            go(remote(to_z.at[v], from_z.at[z], z_send.at[d], z_recv.at[z], at(z_=v)))
    from_z[z] = to_z[z]

    shape = (GROUPS * 16, NF)
    pick_group = (lax.broadcasted_iota(jnp.int32, shape, 1) >> 3) == (lax.broadcasted_iota(jnp.int32, shape, 0) >> 4)
    shape = (GROUPS * 16, CH)
    pick_row = (lax.broadcasted_iota(jnp.int32, shape, 1) >> 3) == (lax.broadcasted_iota(jnp.int32, shape, 0) & 15)
    f = lax.broadcasted_iota(jnp.int32, (NF, CH), 0)
    n = lax.broadcasted_iota(jnp.int32, (NF, CH), 1)
    same_place = ((f & 7) == (n & 7)).astype(jnp.float32).astype(jnp.bfloat16)
    out_row = lax.broadcasted_iota(jnp.int32, (GROUPS, GROUPS * 16), 0)
    in_row = lax.broadcasted_iota(jnp.int32, (GROUPS, GROUPS * 16), 1)
    same_group = ((in_row >> 4) == out_row).astype(jnp.float32).astype(jnp.bfloat16)

    arrived(relay_z, zr_sems.at[1])
    go(remote(relay_z, from_z.at[zs[2], :, 1], zr_sems.at[2], zr_sems.at[3], at(z_=one_down)))
    for d, v in enumerate(zs):
        if d != 3:
            arrived(from_z.at[v], z_recv.at[v])
    arrived(from_z.at[opposite, :, 0], z_recv.at[opposite])
    arrived(from_z.at[opposite, :, 1], zr_sems.at[3])

    def regroup(i, carry):
        b, e = i // 2, i % 2
        rows = from_z[owner_of(plan_ref, b)[2], b, e].astype(jnp.float32).reshape(1, 16, NF)
        rows = jnp.broadcast_to(rows, (GROUPS, 16, NF)).reshape(GROUPS * 16, NF)
        rows = jnp.where(pick_group, rows, 0.0).astype(jnp.bfloat16)
        moved = jnp.dot(rows, same_place, preferred_element_type=jnp.float32)
        moved = jnp.where(pick_row, moved, 0.0).astype(jnp.bfloat16)
        done = jnp.dot(same_group, moved, preferred_element_type=jnp.float32)
        to_x[b, e] = done.astype(jnp.bfloat16)
        return carry

    lax.fori_loop(0, 4, regroup, 0, unroll=2)

    active = win == core
    there = from_x.at[x_lo, win]
    go(remote(to_x, there, x_send.at[0], x_recv.at[x_lo, win], at(x_=1 - x_lo, win_=core)))

    def over():
        return remote(to_x, there, x_send.at[1], x_recv.at[x_lo, win], at(win_=core))

    @pl.when(win != core)
    def _():
        over().start()

    def down(t):
        return (z + NZ - t) % NZ

    def up(t):
        return (z + t) % NZ

    def pieces(t):
        return [(0, 0), (0, 1), (1, 2), (1, 3)] if t == 3 else [(way, d) for d in range(NY) for way in range(2)]

    def piece(t, way, d):
        return gathered.at[down(t) if way == 0 else up(t), (y + d) % NY]

    def ring_piece(t, way, d):
        ref = piece(t, way, d)
        return remote(ref, ref, ring_send.at[way, t, d], ring_recv.at[way, t, d], at(z_=up(1) if way == 0 else down(1)))

    def pass_on(t, way, d):
        ref = piece(t, way, d)
        slot = down(t) if way == 0 else up(t)
        return remote(ref, ref, gc_send.at[slot, d], gc_recv.at[slot, d], at(core_=1 - core))

    def passed(t):
        return [(0, d) for d in range(NY)] if t in (0, 4) else [(way, d) for d in range(NY) for way in range(2)]

    own = gathered.at[z, y]

    def over_y():
        return [remote(own, own, gy_send.at[d], gy_recv.at[y], at(y_=v)) for d, v in enumerate(ys)]

    @pl.when(active)
    def _():
        from_x[x_lo, win] = to_x[...]
        arrived(from_x.at[1 - x_lo, win], x_recv.at[1 - x_lo, win])
        arrived(from_x.at[0, 1 - win], x_recv.at[0, 1 - win])
        arrived(from_x.at[1, 1 - win], x_recv.at[1, 1 - win])

        for b in range(2):
            ox = owner_of(plan_ref, b)[1]
            for w in range(2):
                gathered[z, y, b, :, :, w * CH : (w + 1) * CH] = from_x[ox, w, b]
        for copy in over_y():
            copy.start()
        for way in range(2):
            ring_piece(0, way, 0).start()
        pass_on(0, 0, 0).start()

    for first in range(2):
        for i in (2 * first, 2 * first + 1):
            arrived(far.at[i], hop2_recv.at[i])
            arrived(far.at[4 + i], hop2_recv.at[4 + i])
        window_pair(far, 1 - win, first)

    lane = lax.broadcasted_iota(jnp.int32, (1, 8, 2 * CH), 2)
    sub = lax.broadcasted_iota(jnp.int32, (1, 8, 2 * CH), 1)
    diagonal = (lane & 7) == sub

    def correlate(slots, part=None):
        count = len(slots)

        def unpack(v, carry):
            for i, slot in enumerate(slots):
                sources[i, v] = gathered[slot, v].astype(jnp.float32)
            return carry

        if part != 1:
            lax.fori_loop(0, NY, unpack, 0)

        def product(g):
            row = sources[:count, :, :, :, pl.ds(g, 1), :].reshape(count * 16, 1, 2 * CH)
            spread = jnp.where(diagonal, row, 0.0)
            spread = spread.reshape(count * 16 * 8, 2 * CH).astype(jnp.bfloat16)
            res = jnp.dot(spread, weights[g], preferred_element_type=jnp.float32)
            return res.reshape(count * 16, 8, 2 * CH)

        def bins(gg, carry):
            res = jnp.concatenate([product(2 * gg), product(2 * gg + 1)], 1)
            res = res.astype(jnp.bfloat16).reshape(count, NY, 2, 2, 16, 2 * CH)
            row = pl.multiple_of(gg * 16, 16)
            for i, slot in enumerate(slots):
                for b in range(2):
                    for c in range(2):
                        for s in range(2):
                            cross[b, :, slot, pl.ds(c * NF + row, 16), s * CH : (s + 1) * CH] = res[
                                i, :, b, s, :, c * CH : (c + 1) * CH
                            ]
            return carry

        quarter = GROUPS // 4
        lax.fori_loop(quarter if part == 1 else 0, quarter if part == 0 else 2 * quarter, bins, 0, unroll=8)

    def receive(t, late):
        for way, d in pieces(t - 1):
            if (d >= 2) == bool(late):
                arrived(piece(t, way, d), ring_recv.at[way, t - 1, d])
                if t < 4 and (way, d) in pieces(t):
                    ring_piece(t, way, d).start()
                pass_on(t, way, d).start()

    slots = [[z], [down(1), up(1)], [down(2), up(2)], [down(3), up(3)], [up(4)]]
    for t in range(5):

        @pl.when(active)
        def _():
            if t == 0:
                for d, v in enumerate(ys):
                    arrived(gathered.at[z, v], gy_recv.at[v])
                    for way in range(2):
                        ring_piece(0, way, d + 1).start()
                    pass_on(0, 0, d + 1).start()
            else:
                if t == 1:
                    receive(t, 0)
                receive(t, 1)

        @pl.when(win != core)
        def _():
            for way, d in passed(t):
                slot = down(t) if way == 0 else up(t)
                arrived(piece(t, way, d), gc_recv.at[slot, d])

        if 0 < t < 4:
            correlate(slots[t], 0)

            @pl.when(active)
            def _():
                receive(t + 1, 0)

            correlate(slots[t], 1)
        else:
            correlate(slots[t])

    for copy in sent:
        copy.wait_send()

    @pl.when(win != core)
    def _():
        over().wait_send()

    @pl.when(active)
    def _():
        for copy in over_y() + [pass_on(t, way, d) for t in range(5) for way, d in passed(t)]:
            copy.wait_send()
        for t in range(4):
            for way, d in pieces(t):
                ring_piece(t, way, d).wait_send()


def spread(plan, spectra):
    bf = jnp.bfloat16
    piece = (2, 16, NF)
    dma = pltpu.SemaphoreType.DMA
    natural = (2, NY, 16, 2 * NF)
    return pl.pallas_call(
        spread_kernel,
        out_shape=jax.ShapeDtypeStruct((2, NY, NZ, 2 * NF, 2 * CH), bf),
        in_specs=[pl.BlockSpec(memory_space=pltpu.HBM), pl.BlockSpec(memory_space=pltpu.HBM)],
        out_specs=pl.BlockSpec(memory_space=pltpu.VMEM),
        scratch_shapes=[
            pltpu.SMEM((2,), jnp.int32),
            pltpu.VMEM((8,) + natural, bf),
            pltpu.VMEM((8,) + natural, bf),
            pltpu.VMEM((NY, 2, 8, 16, 2 * NF), bf),
            pltpu.VMEM((4, 2, 16, 2 * NF), bf),
            pltpu.VMEM((4, 2, 16, 2 * NF), bf),
            pltpu.VMEM((NZ, 2) + piece, bf),
            pltpu.VMEM((NZ, 2) + piece, bf),
            pltpu.VMEM(piece, bf),
            pltpu.VMEM((2, 2, GROUPS, CH), bf),
            pltpu.VMEM((2, 2, 2, 2, GROUPS, CH), bf),
            pltpu.VMEM((NZ, NY, 2, 2, GROUPS, 2 * CH), bf),
            pltpu.VMEM((4,) + natural, bf),
            pltpu.VMEM((4,) + natural, bf),
            pltpu.VMEM((GROUPS, 2 * CH, 2 * CH), bf),
            pltpu.VMEM((2, NY, 2, 2, GROUPS, 2 * CH), jnp.float32),
            dma((4, 2)), dma((4, 2)), dma((4,)), dma((2,)), dma((7,)), dma((NZ,)), dma((4,)), dma((2,)), dma((2, 2)),
            dma((3,)), dma((NY,)), dma((2, 4, NY)), dma((2, 4, NY)), dma((NZ, NY)), dma((NZ, NY)), dma((2,)),
            dma((8,)), dma((8,)), dma((8,)), dma((8,)),
        ],
        compiler_params=pltpu.CompilerParams(
            collective_id=0, has_side_effects=True, vmem_limit_bytes=28 * 1024 * 1024
        ),
    )(
        pltpu.with_memory_space_constraint(plan, pltpu.HBM),
        pltpu.with_memory_space_constraint(spectra.reshape((8,) + natural), pltpu.HBM),
    )


def lag_kernel(cross, mask_ref, table_ref, out_ref, stage, out_sems):
    half = HALF // 2

    def result(p):
        slot = lax.rem(p, BUFFERS)
        place = out_ref.at[p // half, pl.ds(2 * lax.rem(p, half), 2)]
        return pltpu.make_async_copy(stage.at[slot], place, out_sems.at[slot])

    def batch(i, drain):
        pairs = [BATCH * i + k for k in range(BATCH)]
        if drain:
            for p in pairs:
                result(p - BUFFERS).wait()
        for p in pairs:
            b, row = p // half, 2 * lax.rem(p, half)
            lagged = jnp.dot(table_ref[...], cross[b, lax.rem(p, half)], preferred_element_type=jnp.float32)
            for s in range(2):
                keep = mask_ref[b, pl.ds(row + s, 1), :].astype(jnp.float32)
                kept = (lagged[:, s * CH : (s + 1) * CH] * keep).astype(jnp.bfloat16)
                stage[lax.rem(p, BUFFERS), s] = kept.T
        for p in pairs:
            result(p).start()

    def first(i, carry):
        batch(i, False)
        return carry

    def rest(i, carry):
        batch(i, True)
        return carry

    lax.fori_loop(0, 2, first, 0)
    lax.fori_loop(2, HALF // BATCH, rest, 0)
    for k in range(BUFFERS):
        result(HALF - BUFFERS + k).wait()


def lags(cross, mask):
    vmem = pl.BlockSpec(memory_space=pltpu.VMEM)
    return pl.pallas_call(
        lag_kernel,
        out_shape=jax.ShapeDtypeStruct((2, HALF, CH, LAGS), jnp.bfloat16),
        in_specs=[vmem, vmem, vmem],
        out_specs=pl.BlockSpec(memory_space=pltpu.HBM),
        scratch_shapes=[
            pltpu.VMEM((BUFFERS, 2, CH, LAGS), jnp.bfloat16),
            pltpu.SemaphoreType.DMA((BUFFERS,)),
        ],
        compiler_params=pltpu.CompilerParams(vmem_limit_bytes=28 * 1024 * 1024),
    )(cross.reshape(2, HALF // 2, 2 * NF, 2 * CH), mask, jnp.asarray(table_transposed()))


def on_device(spectra, plan, mask):
    return lags(spread(plan, spectra), mask)


def solution(mesh):
    return jax.shard_map(
        on_device,
        mesh=mesh,
        in_specs=(P("win", "rx", None), P(), P(None, "win", "rx")),
        out_specs=P(None, "win", "rx", None),
        check_vma=False,
    )
```

```python
import math

import jax
import jax.numpy as jnp
import numpy as np
from jax import lax
from jax.experimental import pallas as pl
from jax.experimental.pallas import tpu as pltpu
from jax.sharding import PartitionSpec as P

LAGS = 256
SAMPLES = 15000
BIN0 = 12
NF = 256
WINDOWS = 16
CH = 128
HALF = 64
GROUPS = 32
MESH = pl.DeviceIdType.MESH
NY, NZ = 4, 8
BATCH = 16
BUFFERS = 2 * BATCH


def table_transposed():
    bins = BIN0 + np.arange(NF)
    shifts = np.arange(LAGS) - LAGS // 2
    theta = 2.0 * math.pi * np.mod(bins[:, None] * shifts[None, :], SAMPLES) / SAMPLES
    scale = 1.0 / math.sqrt(NF)
    table = np.concatenate([np.cos(theta) * scale, -np.sin(theta) * scale], 0)
    table = table.astype(np.float32).astype(jnp.bfloat16).astype(np.float32)
    return np.ascontiguousarray((table / WINDOWS).T).astype(jnp.bfloat16)


def owner_of(plan_ref, block):
    rx = plan_ref[block]
    return rx // 32, (rx // 16) % 2, (rx // 2) % NZ, rx % 2


def spread_kernel(
    plan_hbm, spec_ref, cross,
    plan_ref, near, far, from_y, relay_p, relay_m, to_z, from_z, relay_z, to_x, from_x,
    gathered, transit_p, transit_m, weights, sources,
    y_send, y_recv, relay_sems, core_sems, z_send, z_recv, zr_sems, x_send, x_recv,
    gy_send, gy_recv, ring_send, ring_recv, gc_send, gc_recv, in_sems,
    hop1_send, hop1_recv, hop2_send, hop2_recv,
):
    rx, win = lax.axis_index("rx"), lax.axis_index("win")
    core, z, x_lo, y = rx % 2, (rx // 2) % NZ, (rx // 16) % 2, rx // 32

    def at(y_=y, x_=x_lo, z_=z, core_=core, win_=win):
        return {"rx": ((y_ * 2 + x_) * NZ + z_) * 2 + core_, "win": win_}

    def remote(src, dst, send, recv, device):
        return pltpu.make_async_remote_copy(
            src_ref=src, dst_ref=dst, send_sem=send, recv_sem=recv, device_id=device, device_id_type=MESH
        )

    def arrived(ref, recv):
        remote(ref, ref, recv, recv, at()).wait_recv()


    loads = [
        pltpu.make_async_copy(spec_ref, near, in_sems.at[0]),
        pltpu.make_async_copy(plan_hbm, plan_ref, in_sems.at[1]),
    ]
    for load in loads:
        load.start()

    plus = at(x_=1 - x_lo, win_=(win + x_lo) % 2)
    minus = at(x_=1 - x_lo, win_=(win + 1 - x_lo) % 2)
    ys = [(y + d) % NY for d in range(1, NY)]
    zs = [(z + d) % NZ for d in range(1, NZ)]
    peers = [at(y_=v) for v in ys] + [at(z_=v) for v in zs] + [at(core_=1 - core)]
    peers += [plus, minus, at(win_=1 - win), at(y_=ys[0], core_=1 - core), at(y_=ys[2], core_=1 - core)]
    barrier = pltpu.get_barrier_semaphore()
    for peer in peers:
        pl.semaphore_signal(barrier, inc=1, device_id=peer, device_id_type=MESH)
    pl.semaphore_wait(barrier, len(peers))

    sent = []

    def go(copy):
        copy.start()
        sent.append(copy)

    next_y, across, last_y = ys

    def hop1(i):
        go(remote(spec_ref.at[i], transit_p.at[i], hop1_send.at[i], hop1_recv.at[i], plus))
        go(remote(spec_ref.at[4 + i], transit_m.at[i], hop1_send.at[4 + i], hop1_recv.at[4 + i], minus))

    go(remote(spec_ref.at[0:4, :, across], relay_p, relay_sems.at[0], relay_sems.at[1], at(y_=next_y)))
    go(remote(spec_ref.at[4:8, :, across], relay_m, relay_sems.at[2], relay_sems.at[3], at(y_=last_y)))
    hop1(0)
    mine = from_y.at[y, core]
    for h in range(2):
        go(remote(spec_ref.at[:, h, next_y], mine, y_send.at[0, h], y_recv.at[0, core], at(y_=next_y, core_=h)))
        go(remote(spec_ref.at[:, h, last_y], mine, y_send.at[1, h], y_recv.at[1, core], at(y_=last_y, core_=h)))
    go(remote(spec_ref.at[:, 1 - core, y], mine, core_sems.at[0], core_sems.at[1], at(core_=1 - core)))
    hop1(1)

    def window_pair(ref, side, first):
        def body(i, carry):
            both = [
                ref[2 * i + k].reshape(CH, 2 * NF).astype(jnp.float32).T.reshape(2, GROUPS, 8, CH) for k in range(2)
            ]
            a = jnp.concatenate([both[0][0], both[1][0]], 1).astype(jnp.bfloat16)
            b = jnp.concatenate([both[0][1], both[1][1]], 1)
            minus_b = (-b).astype(jnp.bfloat16)
            b = b.astype(jnp.bfloat16)
            row = pl.multiple_of(side * CH + 16 * i, 16)
            weights[:, pl.ds(row, 16), :CH] = a
            weights[:, pl.ds(HALF + row, 16), :CH] = b
            weights[:, pl.ds(row, 16), CH:] = minus_b
            weights[:, pl.ds(HALF + row, 16), CH:] = a
            return carry

        lax.fori_loop(0, 2, lambda i, carry: body(first + 2 * i, carry), 0, unroll=2)

    for load in loads:
        load.wait()
    from_y[y, core] = near[:, core, y]
    def forward(i):
        arrived(transit_p.at[i], hop1_recv.at[i])
        go(remote(transit_p.at[i], far.at[i], hop2_send.at[i], hop2_recv.at[i], plus))
        arrived(transit_m.at[i], hop1_recv.at[4 + i])
        go(remote(transit_m.at[i], far.at[4 + i], hop2_send.at[4 + i], hop2_recv.at[4 + i], minus))

    arrived(relay_p, relay_sems.at[1])
    place = from_y.at[last_y, core, 0:4]
    for h in range(2):
        go(remote(relay_p.at[:, h], place, y_send.at[2, h], y_recv.at[2, core], at(y_=next_y, core_=h)))
    arrived(relay_m, relay_sems.at[3])
    place = from_y.at[next_y, core, 4:8]
    for h in range(2):
        go(remote(relay_m.at[:, h], place, y_send.at[3, h], y_recv.at[3, core], at(y_=last_y, core_=h)))
    hop1(2)
    window_pair(near, win, 0)
    hop1(3)
    window_pair(near, win, 1)
    forward(0)
    forward(1)
    forward(2)
    arrived(from_y.at[y, 1 - core], core_sems.at[1])
    for k in range(2):
        arrived(from_y.at[last_y, k], y_recv.at[0, k])
        arrived(from_y.at[next_y, k], y_recv.at[1, k])
        arrived(from_y.at[across, k, 0:4], y_recv.at[2, k])
        arrived(from_y.at[across, k, 4:8], y_recv.at[3, k])
    for b in range(2):
        oy, _, _, oc = owner_of(plan_ref, b)
        picked = jnp.transpose(from_y[oy, oc].astype(jnp.float32), (1, 0, 2))
        picked = jnp.concatenate([picked[:, :, :NF], picked[:, :, NF:]], 1)
        to_z[:, b] = picked.astype(jnp.bfloat16).reshape(NZ, 2, 16, NF)

    opposite, three_down, one_down = zs[3], zs[4], zs[6]
    go(remote(to_z.at[opposite, :, 1], relay_z, zr_sems.at[0], zr_sems.at[1], at(z_=three_down)))
    go(remote(to_z.at[opposite, :, 0], from_z.at[z, :, 0], z_send.at[3], z_recv.at[z], at(z_=opposite)))
    for d, v in enumerate(zs):
        if d != 3:
            go(remote(to_z.at[v], from_z.at[z], z_send.at[d], z_recv.at[z], at(z_=v)))
    from_z[z] = to_z[z]
    forward(3)

    shape = (GROUPS * 16, NF)
    pick_group = (lax.broadcasted_iota(jnp.int32, shape, 1) >> 3) == (lax.broadcasted_iota(jnp.int32, shape, 0) >> 4)
    shape = (GROUPS * 16, CH)
    pick_row = (lax.broadcasted_iota(jnp.int32, shape, 1) >> 3) == (lax.broadcasted_iota(jnp.int32, shape, 0) & 15)
    f = lax.broadcasted_iota(jnp.int32, (NF, CH), 0)
    n = lax.broadcasted_iota(jnp.int32, (NF, CH), 1)
    same_place = ((f & 7) == (n & 7)).astype(jnp.float32).astype(jnp.bfloat16)
    out_row = lax.broadcasted_iota(jnp.int32, (GROUPS, GROUPS * 16), 0)
    in_row = lax.broadcasted_iota(jnp.int32, (GROUPS, GROUPS * 16), 1)
    same_group = ((in_row >> 4) == out_row).astype(jnp.float32).astype(jnp.bfloat16)

    arrived(relay_z, zr_sems.at[1])
    go(remote(relay_z, from_z.at[zs[2], :, 1], zr_sems.at[2], zr_sems.at[3], at(z_=one_down)))
    for d, v in enumerate(zs):
        if d != 3:
            arrived(from_z.at[v], z_recv.at[v])
    arrived(from_z.at[opposite, :, 0], z_recv.at[opposite])
    arrived(from_z.at[opposite, :, 1], zr_sems.at[3])

    def regroup(i, carry):
        b, e = i // 2, i % 2
        rows = from_z[owner_of(plan_ref, b)[2], b, e].astype(jnp.float32).reshape(1, 16, NF)
        rows = jnp.broadcast_to(rows, (GROUPS, 16, NF)).reshape(GROUPS * 16, NF)
        rows = jnp.where(pick_group, rows, 0.0).astype(jnp.bfloat16)
        moved = jnp.dot(rows, same_place, preferred_element_type=jnp.float32)
        moved = jnp.where(pick_row, moved, 0.0).astype(jnp.bfloat16)
        done = jnp.dot(same_group, moved, preferred_element_type=jnp.float32)
        to_x[b, e] = done.astype(jnp.bfloat16)
        return carry

    lax.fori_loop(0, 4, regroup, 0, unroll=2)

    active = win == core
    there = from_x.at[x_lo, win]
    go(remote(to_x, there, x_send.at[0], x_recv.at[x_lo, win], at(x_=1 - x_lo, win_=core)))

    def over():
        return remote(to_x, there, x_send.at[1], x_recv.at[x_lo, win], at(win_=core))

    @pl.when(win != core)
    def _():
        over().start()

    def down(t):
        return (z + NZ - t) % NZ

    def up(t):
        return (z + t) % NZ

    def pieces(t):
        return [(0, 0), (0, 1), (1, 2), (1, 3)] if t == 3 else [(way, d) for d in range(NY) for way in range(2)]

    def piece(t, way, d):
        return gathered.at[down(t) if way == 0 else up(t), (y + d) % NY]

    def ring_piece(t, way, d):
        ref = piece(t, way, d)
        return remote(ref, ref, ring_send.at[way, t, d], ring_recv.at[way, t, d], at(z_=up(1) if way == 0 else down(1)))

    def pass_on(t, way, d):
        ref = piece(t, way, d)
        slot = down(t) if way == 0 else up(t)
        return remote(ref, ref, gc_send.at[slot, d], gc_recv.at[slot, d], at(core_=1 - core))

    def passed(t):
        return [(0, d) for d in range(NY)] if t in (0, 4) else [(way, d) for d in range(NY) for way in range(2)]

    own = gathered.at[z, y]

    def over_y():
        return [remote(own, own, gy_send.at[d], gy_recv.at[y], at(y_=v)) for d, v in enumerate(ys)]

    @pl.when(active)
    def _():
        from_x[x_lo, win] = to_x[...]
        arrived(from_x.at[1 - x_lo, win], x_recv.at[1 - x_lo, win])
        arrived(from_x.at[0, 1 - win], x_recv.at[0, 1 - win])
        arrived(from_x.at[1, 1 - win], x_recv.at[1, 1 - win])

        for b in range(2):
            ox = owner_of(plan_ref, b)[1]
            for w in range(2):
                gathered[z, y, b, :, :, w * CH : (w + 1) * CH] = from_x[ox, w, b]
        for copy in over_y():
            copy.start()
        for way in range(2):
            ring_piece(0, way, 0).start()
        pass_on(0, 0, 0).start()

    def far_weights(first):
        for i in (2 * first, 2 * first + 1):
            arrived(far.at[i], hop2_recv.at[i])
            arrived(far.at[4 + i], hop2_recv.at[4 + i])
        window_pair(far, 1 - win, first)

    far_weights(0)

    @pl.when(active)
    def _():
        for d, v in enumerate(ys):
            arrived(gathered.at[z, v], gy_recv.at[v])
            for way in range(2):
                ring_piece(0, way, d + 1).start()
            pass_on(0, 0, d + 1).start()

    far_weights(1)

    lane = lax.broadcasted_iota(jnp.int32, (1, 8, 2 * CH), 2)
    sub = lax.broadcasted_iota(jnp.int32, (1, 8, 2 * CH), 1)
    diagonal = (lane & 7) == sub

    def correlate(slots, part=None):
        count = len(slots)

        def unpack(v, carry):
            for i, slot in enumerate(slots):
                sources[i, v] = gathered[slot, v].astype(jnp.float32)
            return carry

        if part != 1:
            lax.fori_loop(0, NY, unpack, 0)

        def product(g):
            row = sources[:count, :, :, :, pl.ds(g, 1), :].reshape(count * 16, 1, 2 * CH)
            spread = jnp.where(diagonal, row, 0.0)
            spread = spread.reshape(count * 16 * 8, 2 * CH).astype(jnp.bfloat16)
            res = jnp.dot(spread, weights[g], preferred_element_type=jnp.float32)
            return res.reshape(count * 16, 8, 2 * CH)

        def bins(gg, carry):
            res = jnp.concatenate([product(2 * gg), product(2 * gg + 1)], 1)
            res = res.astype(jnp.bfloat16).reshape(count, NY, 2, 2, 16, 2 * CH)
            row = pl.multiple_of(gg * 16, 16)
            for i, slot in enumerate(slots):
                for b in range(2):
                    for c in range(2):
                        for s in range(2):
                            cross[b, :, slot, pl.ds(c * NF + row, 16), s * CH : (s + 1) * CH] = res[
                                i, :, b, s, :, c * CH : (c + 1) * CH
                            ]
            return carry

        quarter = GROUPS // 4
        lax.fori_loop(quarter if part == 1 else 0, quarter if part == 0 else 2 * quarter, bins, 0, unroll=8)

    def receive(t, late):
        for way, d in pieces(t - 1):
            if (d >= 2) == bool(late):
                arrived(piece(t, way, d), ring_recv.at[way, t - 1, d])
                if t < 4 and (way, d) in pieces(t):
                    ring_piece(t, way, d).start()
                pass_on(t, way, d).start()

    slots = [[z], [down(1), up(1)], [down(2), up(2)], [down(3), up(3)], [up(4)]]
    for t in range(5):

        @pl.when(active)
        def _():
            if t == 1:
                receive(t, 0)
            if t > 0:
                receive(t, 1)

        @pl.when(win != core)
        def _():
            for way, d in passed(t):
                slot = down(t) if way == 0 else up(t)
                arrived(piece(t, way, d), gc_recv.at[slot, d])

        if 0 < t < 4:
            correlate(slots[t], 0)

            @pl.when(active)
            def _():
                receive(t + 1, 0)

            correlate(slots[t], 1)
        else:
            correlate(slots[t])

    for copy in sent:
        copy.wait_send()

    @pl.when(win != core)
    def _():
        over().wait_send()

    @pl.when(active)
    def _():
        for copy in over_y() + [pass_on(t, way, d) for t in range(5) for way, d in passed(t)]:
            copy.wait_send()
        for t in range(4):
            for way, d in pieces(t):
                ring_piece(t, way, d).wait_send()


def spread(plan, spectra):
    bf = jnp.bfloat16
    piece = (2, 16, NF)
    dma = pltpu.SemaphoreType.DMA
    natural = (2, NY, 16, 2 * NF)
    return pl.pallas_call(
        spread_kernel,
        out_shape=jax.ShapeDtypeStruct((2, NY, NZ, 2 * NF, 2 * CH), bf),
        in_specs=[pl.BlockSpec(memory_space=pltpu.HBM), pl.BlockSpec(memory_space=pltpu.HBM)],
        out_specs=pl.BlockSpec(memory_space=pltpu.VMEM),
        scratch_shapes=[
            pltpu.SMEM((2,), jnp.int32),
            pltpu.VMEM((8,) + natural, bf),
            pltpu.VMEM((8,) + natural, bf),
            pltpu.VMEM((NY, 2, 8, 16, 2 * NF), bf),
            pltpu.VMEM((4, 2, 16, 2 * NF), bf),
            pltpu.VMEM((4, 2, 16, 2 * NF), bf),
            pltpu.VMEM((NZ, 2) + piece, bf),
            pltpu.VMEM((NZ, 2) + piece, bf),
            pltpu.VMEM(piece, bf),
            pltpu.VMEM((2, 2, GROUPS, CH), bf),
            pltpu.VMEM((2, 2, 2, 2, GROUPS, CH), bf),
            pltpu.VMEM((NZ, NY, 2, 2, GROUPS, 2 * CH), bf),
            pltpu.VMEM((4,) + natural, bf),
            pltpu.VMEM((4,) + natural, bf),
            pltpu.VMEM((GROUPS, 2 * CH, 2 * CH), bf),
            pltpu.VMEM((2, NY, 2, 2, GROUPS, 2 * CH), jnp.float32),
            dma((4, 2)), dma((4, 2)), dma((4,)), dma((2,)), dma((7,)), dma((NZ,)), dma((4,)), dma((2,)), dma((2, 2)),
            dma((3,)), dma((NY,)), dma((2, 4, NY)), dma((2, 4, NY)), dma((NZ, NY)), dma((NZ, NY)), dma((2,)),
            dma((8,)), dma((8,)), dma((8,)), dma((8,)),
        ],
        compiler_params=pltpu.CompilerParams(
            collective_id=0, has_side_effects=True, vmem_limit_bytes=28 * 1024 * 1024
        ),
    )(
        pltpu.with_memory_space_constraint(plan, pltpu.HBM),
        pltpu.with_memory_space_constraint(spectra.reshape((8,) + natural), pltpu.HBM),
    )


def lag_kernel(cross, mask_ref, table_ref, out_ref, stage, out_sems):
    half = HALF // 2

    def result(p):
        slot = lax.rem(p, BUFFERS)
        place = out_ref.at[p // half, pl.ds(2 * lax.rem(p, half), 2)]
        return pltpu.make_async_copy(stage.at[slot], place, out_sems.at[slot])

    def batch(i, drain):
        pairs = [BATCH * i + k for k in range(BATCH)]
        if drain:
            for p in pairs:
                result(p - BUFFERS).wait()
        for p in pairs:
            b, row = p // half, 2 * lax.rem(p, half)
            lagged = jnp.dot(table_ref[...], cross[b, lax.rem(p, half)], preferred_element_type=jnp.float32)
            for s in range(2):
                keep = mask_ref[b, pl.ds(row + s, 1), :].astype(jnp.float32)
                kept = (lagged[:, s * CH : (s + 1) * CH] * keep).astype(jnp.bfloat16)
                stage[lax.rem(p, BUFFERS), s] = kept.T
        for p in pairs:
            result(p).start()

    def first(i, carry):
        batch(i, False)
        return carry

    def rest(i, carry):
        batch(i, True)
        return carry

    lax.fori_loop(0, 2, first, 0)
    lax.fori_loop(2, HALF // BATCH, rest, 0)
    for k in range(BUFFERS):
        result(HALF - BUFFERS + k).wait()


def lags(cross, mask):
    vmem = pl.BlockSpec(memory_space=pltpu.VMEM)
    return pl.pallas_call(
        lag_kernel,
        out_shape=jax.ShapeDtypeStruct((2, HALF, CH, LAGS), jnp.bfloat16),
        in_specs=[vmem, vmem, vmem],
        out_specs=pl.BlockSpec(memory_space=pltpu.HBM),
        scratch_shapes=[
            pltpu.VMEM((BUFFERS, 2, CH, LAGS), jnp.bfloat16),
            pltpu.SemaphoreType.DMA((BUFFERS,)),
        ],
        compiler_params=pltpu.CompilerParams(vmem_limit_bytes=28 * 1024 * 1024),
    )(cross.reshape(2, HALF // 2, 2 * NF, 2 * CH), mask, jnp.asarray(table_transposed()))


def on_device(spectra, plan, mask):
    return lags(spread(plan, spectra), mask)


def solution(mesh):
    return jax.shard_map(
        on_device,
        mesh=mesh,
        in_specs=(P("win", "rx", None), P(), P(None, "win", "rx")),
        out_specs=P(None, "win", "rx", None),
        check_vma=False,
    )
```

```python
import math

import jax
import jax.numpy as jnp
import numpy as np
from jax import lax
from jax.experimental import pallas as pl
from jax.experimental.pallas import tpu as pltpu
from jax.sharding import PartitionSpec as P

LAGS = 256
SAMPLES = 15000
BIN0 = 12
NF = 256
WINDOWS = 16
CH = 128
HALF = 64
GROUPS = 32
MESH = pl.DeviceIdType.MESH
NY, NZ = 4, 8
BATCH = 16
BUFFERS = 2 * BATCH


def table_transposed():
    bins = BIN0 + np.arange(NF)
    shifts = np.arange(LAGS) - LAGS // 2
    theta = 2.0 * math.pi * np.mod(bins[:, None] * shifts[None, :], SAMPLES) / SAMPLES
    scale = 1.0 / math.sqrt(NF)
    table = np.concatenate([np.cos(theta) * scale, -np.sin(theta) * scale], 0)
    table = table.astype(np.float32).astype(jnp.bfloat16).astype(np.float32)
    return np.ascontiguousarray((table / WINDOWS).T).astype(jnp.bfloat16)


def owner_of(plan_ref, block):
    rx = plan_ref[block]
    return rx // 32, (rx // 16) % 2, (rx // 2) % NZ, rx % 2


def spread_kernel(
    plan_hbm, spec_ref, cross,
    plan_ref, near, far, from_y, relay_p, relay_m, to_z, from_z, relay_z, to_x, from_x,
    gathered, transit_p, transit_m, weights, sources,
    y_send, y_recv, relay_sems, core_sems, z_send, z_recv, zr_sems, x_send, x_recv,
    gy_send, gy_recv, ring_send, ring_recv, gc_send, gc_recv, in_sems,
    hop1_send, hop1_recv, hop2_send, hop2_recv,
):
    rx, win = lax.axis_index("rx"), lax.axis_index("win")
    core, z, x_lo, y = rx % 2, (rx // 2) % NZ, (rx // 16) % 2, rx // 32

    def at(y_=y, x_=x_lo, z_=z, core_=core, win_=win):
        return {"rx": ((y_ * 2 + x_) * NZ + z_) * 2 + core_, "win": win_}

    def remote(src, dst, send, recv, device):
        return pltpu.make_async_remote_copy(
            src_ref=src, dst_ref=dst, send_sem=send, recv_sem=recv, device_id=device, device_id_type=MESH
        )

    def arrived(ref, recv):
        remote(ref, ref, recv, recv, at()).wait_recv()


    loads = [
        pltpu.make_async_copy(spec_ref, near, in_sems.at[0]),
        pltpu.make_async_copy(plan_hbm, plan_ref, in_sems.at[1]),
    ]
    for load in loads:
        load.start()

    plus = at(x_=1 - x_lo, win_=(win + x_lo) % 2)
    minus = at(x_=1 - x_lo, win_=(win + 1 - x_lo) % 2)
    ys = [(y + d) % NY for d in range(1, NY)]
    zs = [(z + d) % NZ for d in range(1, NZ)]
    peers = [at(y_=v) for v in ys] + [at(z_=v) for v in zs] + [at(core_=1 - core)]
    peers += [plus, minus, at(win_=1 - win), at(y_=ys[0], core_=1 - core), at(y_=ys[2], core_=1 - core)]
    barrier = pltpu.get_barrier_semaphore()
    for peer in peers:
        pl.semaphore_signal(barrier, inc=1, device_id=peer, device_id_type=MESH)
    pl.semaphore_wait(barrier, len(peers))

    sent = []

    def go(copy):
        copy.start()
        sent.append(copy)

    next_y, across, last_y = ys

    def hop1(i):
        go(remote(spec_ref.at[i], transit_p.at[i], hop1_send.at[i], hop1_recv.at[i], plus))
        go(remote(spec_ref.at[4 + i], transit_m.at[i], hop1_send.at[4 + i], hop1_recv.at[4 + i], minus))

    go(remote(spec_ref.at[0:4, :, across], relay_p, relay_sems.at[0], relay_sems.at[1], at(y_=next_y)))
    go(remote(spec_ref.at[4:8, :, across], relay_m, relay_sems.at[2], relay_sems.at[3], at(y_=last_y)))
    hop1(0)
    mine = from_y.at[y, core]
    for h in range(2):
        go(remote(spec_ref.at[:, h, next_y], mine, y_send.at[0, h], y_recv.at[0, core], at(y_=next_y, core_=h)))
        go(remote(spec_ref.at[:, h, last_y], mine, y_send.at[1, h], y_recv.at[1, core], at(y_=last_y, core_=h)))
    go(remote(spec_ref.at[:, 1 - core, y], mine, core_sems.at[0], core_sems.at[1], at(core_=1 - core)))
    hop1(1)

    def window_pair(ref, side, first):
        def body(i, carry):
            both = [
                ref[2 * i + k].reshape(CH, 2 * NF).astype(jnp.float32).T.reshape(2, GROUPS, 8, CH) for k in range(2)
            ]
            a = jnp.concatenate([both[0][0], both[1][0]], 1).astype(jnp.bfloat16)
            b = jnp.concatenate([both[0][1], both[1][1]], 1)
            minus_b = (-b).astype(jnp.bfloat16)
            b = b.astype(jnp.bfloat16)
            row = pl.multiple_of(side * CH + 16 * i, 16)
            weights[:, pl.ds(row, 16), :CH] = a
            weights[:, pl.ds(HALF + row, 16), :CH] = b
            weights[:, pl.ds(row, 16), CH:] = minus_b
            weights[:, pl.ds(HALF + row, 16), CH:] = a
            return carry

        lax.fori_loop(0, 2, lambda i, carry: body(first + 2 * i, carry), 0, unroll=2)

    for load in loads:
        load.wait()
    from_y[y, core] = near[:, core, y]
    def forward(i):
        arrived(transit_p.at[i], hop1_recv.at[i])
        go(remote(transit_p.at[i], far.at[i], hop2_send.at[i], hop2_recv.at[i], plus))
        arrived(transit_m.at[i], hop1_recv.at[4 + i])
        go(remote(transit_m.at[i], far.at[4 + i], hop2_send.at[4 + i], hop2_recv.at[4 + i], minus))

    arrived(relay_p, relay_sems.at[1])
    place = from_y.at[last_y, core, 0:4]
    for h in range(2):
        go(remote(relay_p.at[:, h], place, y_send.at[2, h], y_recv.at[2, core], at(y_=next_y, core_=h)))
    arrived(relay_m, relay_sems.at[3])
    place = from_y.at[next_y, core, 4:8]
    for h in range(2):
        go(remote(relay_m.at[:, h], place, y_send.at[3, h], y_recv.at[3, core], at(y_=last_y, core_=h)))
    hop1(2)
    window_pair(near, win, 0)
    hop1(3)
    window_pair(near, win, 1)
    forward(0)
    forward(1)
    forward(2)
    arrived(from_y.at[y, 1 - core], core_sems.at[1])
    for k in range(2):
        arrived(from_y.at[last_y, k], y_recv.at[0, k])
        arrived(from_y.at[next_y, k], y_recv.at[1, k])
        arrived(from_y.at[across, k, 0:4], y_recv.at[2, k])
        arrived(from_y.at[across, k, 4:8], y_recv.at[3, k])
    for b in range(2):
        oy, _, _, oc = owner_of(plan_ref, b)
        picked = jnp.transpose(from_y[oy, oc].astype(jnp.float32), (1, 0, 2))
        picked = jnp.concatenate([picked[:, :, :NF], picked[:, :, NF:]], 1)
        to_z[:, b] = picked.astype(jnp.bfloat16).reshape(NZ, 2, 16, NF)

    opposite, three_down, one_down = zs[3], zs[4], zs[6]
    go(remote(to_z.at[opposite, :, 1], relay_z, zr_sems.at[0], zr_sems.at[1], at(z_=three_down)))
    go(remote(to_z.at[opposite, :, 0], from_z.at[z, :, 0], z_send.at[3], z_recv.at[z], at(z_=opposite)))
    for d, v in enumerate(zs):
        if d != 3:
            go(remote(to_z.at[v], from_z.at[z], z_send.at[d], z_recv.at[z], at(z_=v)))
    from_z[z] = to_z[z]
    forward(3)

    shape = (GROUPS * 16, NF)
    pick_group = (lax.broadcasted_iota(jnp.int32, shape, 1) >> 3) == (lax.broadcasted_iota(jnp.int32, shape, 0) >> 4)
    shape = (GROUPS * 16, CH)
    pick_row = (lax.broadcasted_iota(jnp.int32, shape, 1) >> 3) == (lax.broadcasted_iota(jnp.int32, shape, 0) & 15)
    f = lax.broadcasted_iota(jnp.int32, (NF, CH), 0)
    n = lax.broadcasted_iota(jnp.int32, (NF, CH), 1)
    same_place = ((f & 7) == (n & 7)).astype(jnp.float32).astype(jnp.bfloat16)
    out_row = lax.broadcasted_iota(jnp.int32, (GROUPS, GROUPS * 16), 0)
    in_row = lax.broadcasted_iota(jnp.int32, (GROUPS, GROUPS * 16), 1)
    same_group = ((in_row >> 4) == out_row).astype(jnp.float32).astype(jnp.bfloat16)

    arrived(relay_z, zr_sems.at[1])
    go(remote(relay_z, from_z.at[zs[2], :, 1], zr_sems.at[2], zr_sems.at[3], at(z_=one_down)))
    for d, v in enumerate(zs):
        if d != 3:
            arrived(from_z.at[v], z_recv.at[v])
    arrived(from_z.at[opposite, :, 0], z_recv.at[opposite])
    arrived(from_z.at[opposite, :, 1], zr_sems.at[3])

    def regroup(i, carry):
        b, e = i // 2, i % 2
        rows = from_z[owner_of(plan_ref, b)[2], b, e].astype(jnp.float32).reshape(1, 16, NF)
        rows = jnp.broadcast_to(rows, (GROUPS, 16, NF)).reshape(GROUPS * 16, NF)
        rows = jnp.where(pick_group, rows, 0.0).astype(jnp.bfloat16)
        moved = jnp.dot(rows, same_place, preferred_element_type=jnp.float32)
        moved = jnp.where(pick_row, moved, 0.0).astype(jnp.bfloat16)
        done = jnp.dot(same_group, moved, preferred_element_type=jnp.float32)
        to_x[b, e] = done.astype(jnp.bfloat16)
        return carry

    lax.fori_loop(0, 4, regroup, 0, unroll=2)

    active = win == core
    there = from_x.at[x_lo, win]
    go(remote(to_x, there, x_send.at[0], x_recv.at[x_lo, win], at(x_=1 - x_lo, win_=core)))

    def over():
        return remote(to_x, there, x_send.at[1], x_recv.at[x_lo, win], at(win_=core))

    @pl.when(win != core)
    def _():
        over().start()

    def down(t):
        return (z + NZ - t) % NZ

    def up(t):
        return (z + t) % NZ

    def pieces(t):
        return [(0, 0), (0, 1), (1, 2), (1, 3)] if t == 3 else [(way, d) for d in range(NY) for way in range(2)]

    def piece(t, way, d):
        return gathered.at[down(t) if way == 0 else up(t), (y + d) % NY]

    def ring_piece(t, way, d):
        ref = piece(t, way, d)
        return remote(ref, ref, ring_send.at[way, t, d], ring_recv.at[way, t, d], at(z_=up(1) if way == 0 else down(1)))

    def pass_on(t, way, d):
        ref = piece(t, way, d)
        slot = down(t) if way == 0 else up(t)
        return remote(ref, ref, gc_send.at[slot, d], gc_recv.at[slot, d], at(core_=1 - core))

    def passed(t):
        return [(0, d) for d in range(NY)] if t in (0, 4) else [(way, d) for d in range(NY) for way in range(2)]

    own = gathered.at[z, y]

    def over_y():
        return [remote(own, own, gy_send.at[d], gy_recv.at[y], at(y_=v)) for d, v in enumerate(ys)]

    @pl.when(active)
    def _():
        from_x[x_lo, win] = to_x[...]
        arrived(from_x.at[1 - x_lo, win], x_recv.at[1 - x_lo, win])
        arrived(from_x.at[0, 1 - win], x_recv.at[0, 1 - win])
        arrived(from_x.at[1, 1 - win], x_recv.at[1, 1 - win])

        for b in range(2):
            ox = owner_of(plan_ref, b)[1]
            for w in range(2):
                gathered[z, y, b, :, :, w * CH : (w + 1) * CH] = from_x[ox, w, b]
        for copy in over_y():
            copy.start()
        for way in range(2):
            ring_piece(0, way, 0).start()
        pass_on(0, 0, 0).start()

    def far_weights(first):
        for i in (2 * first, 2 * first + 1):
            arrived(far.at[i], hop2_recv.at[i])
            arrived(far.at[4 + i], hop2_recv.at[4 + i])
        window_pair(far, 1 - win, first)

    far_weights(0)

    @pl.when(active)
    def _():
        for d, v in enumerate(ys):
            arrived(gathered.at[z, v], gy_recv.at[v])
            for way in range(2):
                ring_piece(0, way, d + 1).start()
            pass_on(0, 0, d + 1).start()

    far_weights(1)

    lane = lax.broadcasted_iota(jnp.int32, (1, 8, 2 * CH), 2)
    sub = lax.broadcasted_iota(jnp.int32, (1, 8, 2 * CH), 1)
    diagonal = (lane & 7) == sub

    def correlate(slots, part=None):
        count = len(slots)

        def unpack(v, carry):
            for i, slot in enumerate(slots):
                sources[i, v] = gathered[slot, v].astype(jnp.float32)
            return carry

        if part != 1:
            lax.fori_loop(0, NY, unpack, 0)

        def product(g, row):
            spread = jnp.where(diagonal, row, 0.0)
            spread = spread.reshape(count * 16 * 8, 2 * CH).astype(jnp.bfloat16)
            res = jnp.dot(spread, weights[g], preferred_element_type=jnp.float32)
            return res.reshape(count * 16, 8, 2 * CH)

        def bins(block, carry):
            start = pl.multiple_of(8 * block, 8)
            rows = sources[:count, :, :, :, pl.ds(start, 8), :].reshape(count * 16, 8, 2 * CH)
            for k in range(0, 8, 2):
                res = jnp.concatenate([product(start + k + m, rows[:, k + m : k + m + 1]) for m in range(2)], 1)
                res = res.astype(jnp.bfloat16).reshape(count, NY, 2, 2, 16, 2 * CH)
                row = pl.multiple_of(block * 64 + 8 * k, 16)
                for i, slot in enumerate(slots):
                    for b in range(2):
                        for c in range(2):
                            for s in range(2):
                                cross[b, :, slot, pl.ds(c * NF + row, 16), s * CH : (s + 1) * CH] = res[
                                    i, :, b, s, :, c * CH : (c + 1) * CH
                                ]
            return carry

        lax.fori_loop(2 if part == 1 else 0, 2 if part == 0 else 4, bins, 0)

    def receive(t, late):
        for way, d in pieces(t - 1):
            if (d >= 2) == bool(late):
                arrived(piece(t, way, d), ring_recv.at[way, t - 1, d])
                if t < 4 and (way, d) in pieces(t):
                    ring_piece(t, way, d).start()
                pass_on(t, way, d).start()

    slots = [[z], [down(1), up(1)], [down(2), up(2)], [down(3), up(3)], [up(4)]]
    for t in range(5):

        @pl.when(active)
        def _():
            if t == 1:
                receive(t, 0)
            if t > 0:
                receive(t, 1)

        @pl.when(win != core)
        def _():
            for way, d in passed(t):
                slot = down(t) if way == 0 else up(t)
                arrived(piece(t, way, d), gc_recv.at[slot, d])

        if 0 < t < 4:
            correlate(slots[t], 0)

            @pl.when(active)
            def _():
                receive(t + 1, 0)

            correlate(slots[t], 1)
        else:
            correlate(slots[t])

    for copy in sent:
        copy.wait_send()

    @pl.when(win != core)
    def _():
        over().wait_send()

    @pl.when(active)
    def _():
        for copy in over_y() + [pass_on(t, way, d) for t in range(5) for way, d in passed(t)]:
            copy.wait_send()
        for t in range(4):
            for way, d in pieces(t):
                ring_piece(t, way, d).wait_send()


def spread(plan, spectra):
    bf = jnp.bfloat16
    piece = (2, 16, NF)
    dma = pltpu.SemaphoreType.DMA
    natural = (2, NY, 16, 2 * NF)
    return pl.pallas_call(
        spread_kernel,
        out_shape=jax.ShapeDtypeStruct((2, NY, NZ, 2 * NF, 2 * CH), bf),
        in_specs=[pl.BlockSpec(memory_space=pltpu.HBM), pl.BlockSpec(memory_space=pltpu.HBM)],
        out_specs=pl.BlockSpec(memory_space=pltpu.VMEM),
        scratch_shapes=[
            pltpu.SMEM((2,), jnp.int32),
            pltpu.VMEM((8,) + natural, bf),
            pltpu.VMEM((8,) + natural, bf),
            pltpu.VMEM((NY, 2, 8, 16, 2 * NF), bf),
            pltpu.VMEM((4, 2, 16, 2 * NF), bf),
            pltpu.VMEM((4, 2, 16, 2 * NF), bf),
            pltpu.VMEM((NZ, 2) + piece, bf),
            pltpu.VMEM((NZ, 2) + piece, bf),
            pltpu.VMEM(piece, bf),
            pltpu.VMEM((2, 2, GROUPS, CH), bf),
            pltpu.VMEM((2, 2, 2, 2, GROUPS, CH), bf),
            pltpu.VMEM((NZ, NY, 2, 2, GROUPS, 2 * CH), bf),
            pltpu.VMEM((4,) + natural, bf),
            pltpu.VMEM((4,) + natural, bf),
            pltpu.VMEM((GROUPS, 2 * CH, 2 * CH), bf),
            pltpu.VMEM((2, NY, 2, 2, GROUPS, 2 * CH), jnp.float32),
            dma((4, 2)), dma((4, 2)), dma((4,)), dma((2,)), dma((7,)), dma((NZ,)), dma((4,)), dma((2,)), dma((2, 2)),
            dma((3,)), dma((NY,)), dma((2, 4, NY)), dma((2, 4, NY)), dma((NZ, NY)), dma((NZ, NY)), dma((2,)),
            dma((8,)), dma((8,)), dma((8,)), dma((8,)),
        ],
        compiler_params=pltpu.CompilerParams(
            collective_id=0, has_side_effects=True, vmem_limit_bytes=28 * 1024 * 1024
        ),
    )(
        pltpu.with_memory_space_constraint(plan, pltpu.HBM),
        pltpu.with_memory_space_constraint(spectra.reshape((8,) + natural), pltpu.HBM),
    )


def lag_kernel(cross, mask_ref, table_ref, out_ref, stage, out_sems):
    half = HALF // 2

    def result(p):
        slot = lax.rem(p, BUFFERS)
        place = out_ref.at[p // half, pl.ds(2 * lax.rem(p, half), 2)]
        return pltpu.make_async_copy(stage.at[slot], place, out_sems.at[slot])

    def batch(i, drain):
        pairs = [BATCH * i + k for k in range(BATCH)]
        if drain:
            for p in pairs:
                result(p - BUFFERS).wait()
        for p in pairs:
            b, row = p // half, 2 * lax.rem(p, half)
            lagged = jnp.dot(table_ref[...], cross[b, lax.rem(p, half)], preferred_element_type=jnp.float32)
            for s in range(2):
                keep = mask_ref[b, pl.ds(row + s, 1), :].astype(jnp.float32)
                kept = (lagged[:, s * CH : (s + 1) * CH] * keep).astype(jnp.bfloat16)
                stage[lax.rem(p, BUFFERS), s] = kept.T
        for p in pairs:
            result(p).start()

    def first(i, carry):
        batch(i, False)
        return carry

    def rest(i, carry):
        batch(i, True)
        return carry

    lax.fori_loop(0, 2, first, 0)
    lax.fori_loop(2, HALF // BATCH, rest, 0)
    for k in range(BUFFERS):
        result(HALF - BUFFERS + k).wait()


def lags(cross, mask):
    vmem = pl.BlockSpec(memory_space=pltpu.VMEM)
    return pl.pallas_call(
        lag_kernel,
        out_shape=jax.ShapeDtypeStruct((2, HALF, CH, LAGS), jnp.bfloat16),
        in_specs=[vmem, vmem, vmem],
        out_specs=pl.BlockSpec(memory_space=pltpu.HBM),
        scratch_shapes=[
            pltpu.VMEM((BUFFERS, 2, CH, LAGS), jnp.bfloat16),
            pltpu.SemaphoreType.DMA((BUFFERS,)),
        ],
        compiler_params=pltpu.CompilerParams(vmem_limit_bytes=28 * 1024 * 1024),
    )(cross.reshape(2, HALF // 2, 2 * NF, 2 * CH), mask, jnp.asarray(table_transposed()))


def on_device(spectra, plan, mask):
    return lags(spread(plan, spectra), mask)


def solution(mesh):
    return jax.shard_map(
        on_device,
        mesh=mesh,
        in_specs=(P("win", "rx", None), P(), P(None, "win", "rx")),
        out_specs=P(None, "win", "rx", None),
        check_vma=False,
    )
```

```python
import math

import jax
import jax.numpy as jnp
import numpy as np
from jax import lax
from jax.experimental import pallas as pl
from jax.experimental.pallas import tpu as pltpu
from jax.sharding import PartitionSpec as P

LAGS = 256
SAMPLES = 15000
BIN0 = 12
NF = 256
WINDOWS = 16
CH = 128
HALF = 64
GROUPS = 32
MESH = pl.DeviceIdType.MESH
NY, NZ = 4, 8
BATCH = 16
BUFFERS = 2 * BATCH


def table_transposed():
    bins = BIN0 + np.arange(NF)
    shifts = np.arange(LAGS) - LAGS // 2
    theta = 2.0 * math.pi * np.mod(bins[:, None] * shifts[None, :], SAMPLES) / SAMPLES
    scale = 1.0 / math.sqrt(NF)
    table = np.concatenate([np.cos(theta) * scale, -np.sin(theta) * scale], 0)
    table = table.astype(np.float32).astype(jnp.bfloat16).astype(np.float32)
    return np.ascontiguousarray((table / WINDOWS).T).astype(jnp.bfloat16)


def owner_of(plan_ref, block):
    rx = plan_ref[block]
    return rx // 32, (rx // 16) % 2, (rx // 2) % NZ, rx % 2


def spread_kernel(
    plan_hbm, spec_ref, cross,
    plan_ref, near, far, from_y, relay_p, relay_m, to_z, from_z, relay_z, to_x, from_x,
    gathered, transit_p, transit_m, weights, sources,
    y_send, y_recv, relay_sems, core_sems, z_send, z_recv, zr_sems, x_send, x_recv,
    gy_send, gy_recv, ring_send, ring_recv, gc_send, gc_recv, in_sems,
    hop1_send, hop1_recv, hop2_send, hop2_recv,
):
    rx, win = lax.axis_index("rx"), lax.axis_index("win")
    core, z, x_lo, y = rx % 2, (rx // 2) % NZ, (rx // 16) % 2, rx // 32

    def at(y_=y, x_=x_lo, z_=z, core_=core, win_=win):
        return {"rx": ((y_ * 2 + x_) * NZ + z_) * 2 + core_, "win": win_}

    def remote(src, dst, send, recv, device):
        return pltpu.make_async_remote_copy(
            src_ref=src, dst_ref=dst, send_sem=send, recv_sem=recv, device_id=device, device_id_type=MESH
        )

    def arrived(ref, recv):
        remote(ref, ref, recv, recv, at()).wait_recv()


    loads = [
        pltpu.make_async_copy(spec_ref, near, in_sems.at[0]),
        pltpu.make_async_copy(plan_hbm, plan_ref, in_sems.at[1]),
    ]
    for load in loads:
        load.start()

    plus = at(x_=1 - x_lo, win_=(win + x_lo) % 2)
    minus = at(x_=1 - x_lo, win_=(win + 1 - x_lo) % 2)
    ys = [(y + d) % NY for d in range(1, NY)]
    zs = [(z + d) % NZ for d in range(1, NZ)]
    peers = [at(y_=v) for v in ys] + [at(z_=v) for v in zs] + [at(core_=1 - core)]
    peers += [plus, minus, at(win_=1 - win), at(y_=ys[0], core_=1 - core), at(y_=ys[2], core_=1 - core)]
    barrier = pltpu.get_barrier_semaphore()
    for peer in peers:
        pl.semaphore_signal(barrier, inc=1, device_id=peer, device_id_type=MESH)
    pl.semaphore_wait(barrier, len(peers))

    sent = []

    def go(copy):
        copy.start()
        sent.append(copy)

    next_y, across, last_y = ys

    def hop1(i):
        go(remote(spec_ref.at[i], transit_p.at[i], hop1_send.at[i], hop1_recv.at[i], plus))
        go(remote(spec_ref.at[4 + i], transit_m.at[i], hop1_send.at[4 + i], hop1_recv.at[4 + i], minus))

    go(remote(spec_ref.at[0:4, :, across], relay_p, relay_sems.at[0], relay_sems.at[1], at(y_=next_y)))
    go(remote(spec_ref.at[4:8, :, across], relay_m, relay_sems.at[2], relay_sems.at[3], at(y_=last_y)))
    hop1(0)
    mine = from_y.at[y, core]
    for h in range(2):
        go(remote(spec_ref.at[:, h, next_y], mine, y_send.at[0, h], y_recv.at[0, core], at(y_=next_y, core_=h)))
        go(remote(spec_ref.at[:, h, last_y], mine, y_send.at[1, h], y_recv.at[1, core], at(y_=last_y, core_=h)))
    go(remote(spec_ref.at[:, 1 - core, y], mine, core_sems.at[0], core_sems.at[1], at(core_=1 - core)))
    for i in range(1, 4):
        hop1(i)

    def window_pair(ref, side, first):
        def body(i, carry):
            both = [
                ref[2 * i + k].reshape(CH, 2 * NF).astype(jnp.float32).T.reshape(2, GROUPS, 8, CH) for k in range(2)
            ]
            a = jnp.concatenate([both[0][0], both[1][0]], 1).astype(jnp.bfloat16)
            b = jnp.concatenate([both[0][1], both[1][1]], 1)
            minus_b = (-b).astype(jnp.bfloat16)
            b = b.astype(jnp.bfloat16)
            row = pl.multiple_of(side * CH + 16 * i, 16)
            weights[:, pl.ds(row, 16), :CH] = a
            weights[:, pl.ds(HALF + row, 16), :CH] = b
            weights[:, pl.ds(row, 16), CH:] = minus_b
            weights[:, pl.ds(HALF + row, 16), CH:] = a
            return carry

        lax.fori_loop(0, 2, lambda i, carry: body(first + 2 * i, carry), 0, unroll=2)

    for load in loads:
        load.wait()
    from_y[y, core] = near[:, core, y]
    def forward(i):
        arrived(transit_p.at[i], hop1_recv.at[i])
        go(remote(transit_p.at[i], far.at[i], hop2_send.at[i], hop2_recv.at[i], plus))
        arrived(transit_m.at[i], hop1_recv.at[4 + i])
        go(remote(transit_m.at[i], far.at[4 + i], hop2_send.at[4 + i], hop2_recv.at[4 + i], minus))

    arrived(relay_p, relay_sems.at[1])
    place = from_y.at[last_y, core, 0:4]
    for h in range(2):
        go(remote(relay_p.at[:, h], place, y_send.at[2, h], y_recv.at[2, core], at(y_=next_y, core_=h)))
    arrived(relay_m, relay_sems.at[3])
    place = from_y.at[next_y, core, 4:8]
    for h in range(2):
        go(remote(relay_m.at[:, h], place, y_send.at[3, h], y_recv.at[3, core], at(y_=last_y, core_=h)))
    forward(0)
    window_pair(near, win, 0)
    forward(1)
    window_pair(near, win, 1)

    forward(2)
    forward(3)
    arrived(from_y.at[y, 1 - core], core_sems.at[1])
    for k in range(2):
        arrived(from_y.at[last_y, k], y_recv.at[0, k])
        arrived(from_y.at[next_y, k], y_recv.at[1, k])
        arrived(from_y.at[across, k, 0:4], y_recv.at[2, k])
        arrived(from_y.at[across, k, 4:8], y_recv.at[3, k])
    for b in range(2):
        oy, _, _, oc = owner_of(plan_ref, b)
        picked = jnp.transpose(from_y[oy, oc].astype(jnp.float32), (1, 0, 2))
        picked = jnp.concatenate([picked[:, :, :NF], picked[:, :, NF:]], 1)
        to_z[:, b] = picked.astype(jnp.bfloat16).reshape(NZ, 2, 16, NF)

    opposite, three_down, one_down = zs[3], zs[4], zs[6]
    go(remote(to_z.at[opposite, :, 1], relay_z, zr_sems.at[0], zr_sems.at[1], at(z_=three_down)))
    go(remote(to_z.at[opposite, :, 0], from_z.at[z, :, 0], z_send.at[3], z_recv.at[z], at(z_=opposite)))
    for d, v in enumerate(zs):
        if d != 3:
            go(remote(to_z.at[v], from_z.at[z], z_send.at[d], z_recv.at[z], at(z_=v)))
    from_z[z] = to_z[z]

    shape = (GROUPS * 16, NF)
    pick_group = (lax.broadcasted_iota(jnp.int32, shape, 1) >> 3) == (lax.broadcasted_iota(jnp.int32, shape, 0) >> 4)
    shape = (GROUPS * 16, CH)
    pick_row = (lax.broadcasted_iota(jnp.int32, shape, 1) >> 3) == (lax.broadcasted_iota(jnp.int32, shape, 0) & 15)
    f = lax.broadcasted_iota(jnp.int32, (NF, CH), 0)
    n = lax.broadcasted_iota(jnp.int32, (NF, CH), 1)
    same_place = ((f & 7) == (n & 7)).astype(jnp.float32).astype(jnp.bfloat16)
    out_row = lax.broadcasted_iota(jnp.int32, (GROUPS, GROUPS * 16), 0)
    in_row = lax.broadcasted_iota(jnp.int32, (GROUPS, GROUPS * 16), 1)
    same_group = ((in_row >> 4) == out_row).astype(jnp.float32).astype(jnp.bfloat16)

    arrived(relay_z, zr_sems.at[1])
    go(remote(relay_z, from_z.at[zs[2], :, 1], zr_sems.at[2], zr_sems.at[3], at(z_=one_down)))
    for d, v in enumerate(zs):
        if d != 3:
            arrived(from_z.at[v], z_recv.at[v])
    arrived(from_z.at[opposite, :, 0], z_recv.at[opposite])
    arrived(from_z.at[opposite, :, 1], zr_sems.at[3])

    def regroup(i, carry):
        b, e = i // 2, i % 2
        rows = from_z[owner_of(plan_ref, b)[2], b, e].astype(jnp.float32).reshape(1, 16, NF)
        rows = jnp.broadcast_to(rows, (GROUPS, 16, NF)).reshape(GROUPS * 16, NF)
        rows = jnp.where(pick_group, rows, 0.0).astype(jnp.bfloat16)
        moved = jnp.dot(rows, same_place, preferred_element_type=jnp.float32)
        moved = jnp.where(pick_row, moved, 0.0).astype(jnp.bfloat16)
        done = jnp.dot(same_group, moved, preferred_element_type=jnp.float32)
        to_x[b, e] = done.astype(jnp.bfloat16)
        return carry

    lax.fori_loop(0, 4, regroup, 0, unroll=2)

    active = win == core
    there = from_x.at[x_lo, win]
    go(remote(to_x, there, x_send.at[0], x_recv.at[x_lo, win], at(x_=1 - x_lo, win_=core)))

    def over():
        return remote(to_x, there, x_send.at[1], x_recv.at[x_lo, win], at(win_=core))

    @pl.when(win != core)
    def _():
        over().start()

    def down(t):
        return (z + NZ - t) % NZ

    def up(t):
        return (z + t) % NZ

    def pieces(t):
        return [(0, 0), (0, 1), (1, 3), (1, 2)] if t == 3 else [(way, d) for d in (0, 1, 3, 2) for way in range(2)]

    def piece(t, way, d):
        return gathered.at[down(t) if way == 0 else up(t), (y + d) % NY]

    def ring_piece(t, way, d):
        ref = piece(t, way, d)
        return remote(ref, ref, ring_send.at[way, t, d], ring_recv.at[way, t, d], at(z_=up(1) if way == 0 else down(1)))

    def pass_on(t, way, d):
        ref = piece(t, way, d)
        slot = down(t) if way == 0 else up(t)
        return remote(ref, ref, gc_send.at[slot, d], gc_recv.at[slot, d], at(core_=1 - core))

    def passed(t):
        return [(0, d) for d in (0, 1, 3, 2)] if t in (0, 4) else [(way, d) for d in (0, 1, 3, 2) for way in range(2)]

    own = gathered.at[z, y]

    def over_y():
        return [remote(own, own, gy_send.at[d], gy_recv.at[y], at(y_=v)) for d, v in enumerate(ys)]

    @pl.when(active)
    def _():
        from_x[x_lo, win] = to_x[...]
        arrived(from_x.at[1 - x_lo, win], x_recv.at[1 - x_lo, win])
        arrived(from_x.at[0, 1 - win], x_recv.at[0, 1 - win])
        arrived(from_x.at[1, 1 - win], x_recv.at[1, 1 - win])

        for b in range(2):
            ox = owner_of(plan_ref, b)[1]
            for w in range(2):
                gathered[z, y, b, :, :, w * CH : (w + 1) * CH] = from_x[ox, w, b]
        for copy in over_y():
            copy.start()
        for way in range(2):
            ring_piece(0, way, 0).start()
        pass_on(0, 0, 0).start()

    for first in range(2):
        for i in (2 * first, 2 * first + 1):
            arrived(far.at[i], hop2_recv.at[i])
            arrived(far.at[4 + i], hop2_recv.at[4 + i])
        window_pair(far, 1 - win, first)

    lane = lax.broadcasted_iota(jnp.int32, (1, 8, 2 * CH), 2)
    sub = lax.broadcasted_iota(jnp.int32, (1, 8, 2 * CH), 1)
    diagonal = (lane & 7) == sub

    def correlate(slots, part=None):
        count = len(slots)

        def unpack(v, carry):
            for i, slot in enumerate(slots):
                sources[i, v] = gathered[slot, v].astype(jnp.float32)
            return carry

        if part != 1:
            lax.fori_loop(0, NY, unpack, 0)

        def product(g):
            row = sources[:count, :, :, :, pl.ds(g, 1), :].reshape(count * 16, 1, 2 * CH)
            spread = jnp.where(diagonal, row, 0.0)
            spread = spread.reshape(count * 16 * 8, 2 * CH).astype(jnp.bfloat16)
            res = jnp.dot(spread, weights[g], preferred_element_type=jnp.float32)
            return res.reshape(count * 16, 8, 2 * CH)

        def bins(gg, carry):
            res = jnp.concatenate([product(2 * gg), product(2 * gg + 1)], 1)
            res = res.astype(jnp.bfloat16).reshape(count, NY, 2, 2, 16, 2 * CH)
            row = pl.multiple_of(gg * 16, 16)
            for i, slot in enumerate(slots):
                for b in range(2):
                    for c in range(2):
                        for s in range(2):
                            cross[b, :, slot, pl.ds(c * NF + row, 16), s * CH : (s + 1) * CH] = res[
                                i, :, b, s, :, c * CH : (c + 1) * CH
                            ]
            return carry

        quarter = GROUPS // 4
        lax.fori_loop(quarter if part == 1 else 0, quarter if part == 0 else 2 * quarter, bins, 0, unroll=8)

    def receive(t, late):
        for way, d in pieces(t - 1):
            if (d >= 2) == bool(late):
                arrived(piece(t, way, d), ring_recv.at[way, t - 1, d])
                if t < 4 and (way, d) in pieces(t):
                    ring_piece(t, way, d).start()
                pass_on(t, way, d).start()

    slots = [[z], [down(1), up(1)], [down(2), up(2)], [down(3), up(3)], [up(4)]]
    for t in range(5):

        @pl.when(active)
        def _():
            if t == 0:
                for d in (1, 3, 2):
                    arrived(piece(0, 0, d), gy_recv.at[(y + d) % NY])
                    for way in range(2):
                        ring_piece(0, way, d).start()
                    pass_on(0, 0, d).start()
            else:
                if t == 1:
                    receive(t, 0)
                receive(t, 1)

        @pl.when(win != core)
        def _():
            for way, d in passed(t):
                slot = down(t) if way == 0 else up(t)
                arrived(piece(t, way, d), gc_recv.at[slot, d])

        if 0 < t < 4:
            correlate(slots[t], 0)

            @pl.when(active)
            def _():
                receive(t + 1, 0)

            correlate(slots[t], 1)
        else:
            correlate(slots[t])

    for copy in sent:
        copy.wait_send()

    @pl.when(win != core)
    def _():
        over().wait_send()

    @pl.when(active)
    def _():
        for copy in over_y() + [pass_on(t, way, d) for t in range(5) for way, d in passed(t)]:
            copy.wait_send()
        for t in range(4):
            for way, d in pieces(t):
                ring_piece(t, way, d).wait_send()


def spread(plan, spectra):
    bf = jnp.bfloat16
    piece = (2, 16, NF)
    dma = pltpu.SemaphoreType.DMA
    natural = (2, NY, 16, 2 * NF)
    return pl.pallas_call(
        spread_kernel,
        out_shape=jax.ShapeDtypeStruct((2, NY, NZ, 2 * NF, 2 * CH), bf),
        in_specs=[pl.BlockSpec(memory_space=pltpu.HBM), pl.BlockSpec(memory_space=pltpu.HBM)],
        out_specs=pl.BlockSpec(memory_space=pltpu.VMEM),
        scratch_shapes=[
            pltpu.SMEM((2,), jnp.int32),
            pltpu.VMEM((8,) + natural, bf),
            pltpu.VMEM((8,) + natural, bf),
            pltpu.VMEM((NY, 2, 8, 16, 2 * NF), bf),
            pltpu.VMEM((4, 2, 16, 2 * NF), bf),
            pltpu.VMEM((4, 2, 16, 2 * NF), bf),
            pltpu.VMEM((NZ, 2) + piece, bf),
            pltpu.VMEM((NZ, 2) + piece, bf),
            pltpu.VMEM(piece, bf),
            pltpu.VMEM((2, 2, GROUPS, CH), bf),
            pltpu.VMEM((2, 2, 2, 2, GROUPS, CH), bf),
            pltpu.VMEM((NZ, NY, 2, 2, GROUPS, 2 * CH), bf),
            pltpu.VMEM((4,) + natural, bf),
            pltpu.VMEM((4,) + natural, bf),
            pltpu.VMEM((GROUPS, 2 * CH, 2 * CH), bf),
            pltpu.VMEM((2, NY, 2, 2, GROUPS, 2 * CH), jnp.float32),
            dma((4, 2)), dma((4, 2)), dma((4,)), dma((2,)), dma((7,)), dma((NZ,)), dma((4,)), dma((2,)), dma((2, 2)),
            dma((3,)), dma((NY,)), dma((2, 4, NY)), dma((2, 4, NY)), dma((NZ, NY)), dma((NZ, NY)), dma((2,)),
            dma((8,)), dma((8,)), dma((8,)), dma((8,)),
        ],
        compiler_params=pltpu.CompilerParams(
            collective_id=0, has_side_effects=True, vmem_limit_bytes=28 * 1024 * 1024
        ),
    )(
        pltpu.with_memory_space_constraint(plan, pltpu.HBM),
        pltpu.with_memory_space_constraint(spectra.reshape((8,) + natural), pltpu.HBM),
    )


def lag_kernel(cross, mask_ref, table_ref, out_ref, stage, out_sems):
    half = HALF // 2

    def result(p):
        slot = lax.rem(p, BUFFERS)
        place = out_ref.at[p // half, pl.ds(2 * lax.rem(p, half), 2)]
        return pltpu.make_async_copy(stage.at[slot], place, out_sems.at[slot])

    def batch(i, drain):
        pairs = [BATCH * i + k for k in range(BATCH)]
        if drain:
            for p in pairs:
                result(p - BUFFERS).wait()
        for p in pairs:
            b, row = p // half, 2 * lax.rem(p, half)
            lagged = jnp.dot(table_ref[...], cross[b, lax.rem(p, half)], preferred_element_type=jnp.float32)
            for s in range(2):
                keep = mask_ref[b, pl.ds(row + s, 1), :].astype(jnp.float32)
                kept = (lagged[:, s * CH : (s + 1) * CH] * keep).astype(jnp.bfloat16)
                stage[lax.rem(p, BUFFERS), s] = kept.T
        for p in pairs:
            result(p).start()

    def first(i, carry):
        batch(i, False)
        return carry

    def rest(i, carry):
        batch(i, True)
        return carry

    lax.fori_loop(0, 2, first, 0)
    lax.fori_loop(2, HALF // BATCH, rest, 0)
    for k in range(BUFFERS):
        result(HALF - BUFFERS + k).wait()


def lags(cross, mask):
    vmem = pl.BlockSpec(memory_space=pltpu.VMEM)
    return pl.pallas_call(
        lag_kernel,
        out_shape=jax.ShapeDtypeStruct((2, HALF, CH, LAGS), jnp.bfloat16),
        in_specs=[vmem, vmem, vmem],
        out_specs=pl.BlockSpec(memory_space=pltpu.HBM),
        scratch_shapes=[
            pltpu.VMEM((BUFFERS, 2, CH, LAGS), jnp.bfloat16),
            pltpu.SemaphoreType.DMA((BUFFERS,)),
        ],
        compiler_params=pltpu.CompilerParams(vmem_limit_bytes=28 * 1024 * 1024),
    )(cross.reshape(2, HALF // 2, 2 * NF, 2 * CH), mask, jnp.asarray(table_transposed()))


def on_device(spectra, plan, mask):
    return lags(spread(plan, spectra), mask)


def solution(mesh):
    return jax.shard_map(
        on_device,
        mesh=mesh,
        in_specs=(P("win", "rx", None), P(), P(None, "win", "rx")),
        out_specs=P(None, "win", "rx", None),
        check_vma=False,
    )
```

```python
import math

import jax
import jax.numpy as jnp
import numpy as np
from jax import lax
from jax.experimental import pallas as pl
from jax.experimental.pallas import tpu as pltpu
from jax.sharding import PartitionSpec as P

LAGS = 256
SAMPLES = 15000
BIN0 = 12
NF = 256
WINDOWS = 16
CH = 128
HALF = 64
GROUPS = 32
MESH = pl.DeviceIdType.MESH
NY, NZ = 4, 8
BATCH = 32
BUFFERS = 2 * BATCH


def table_transposed():
    bins = BIN0 + np.arange(NF)
    shifts = np.arange(LAGS) - LAGS // 2
    theta = 2.0 * math.pi * np.mod(bins[:, None] * shifts[None, :], SAMPLES) / SAMPLES
    scale = 1.0 / math.sqrt(NF)
    table = np.concatenate([np.cos(theta) * scale, -np.sin(theta) * scale], 0)
    table = table.astype(np.float32).astype(jnp.bfloat16).astype(np.float32)
    return np.ascontiguousarray((table / WINDOWS).T).astype(jnp.bfloat16)


def owner_of(plan_ref, block):
    rx = plan_ref[block]
    return rx // 32, (rx // 16) % 2, (rx // 2) % NZ, rx % 2


def spread_kernel(
    plan_hbm, spec_ref, cross,
    plan_ref, near, far, from_y, relay_p, relay_m, to_z, from_z, relay_z, to_x, from_x,
    gathered, transit_p, transit_m, weights, sources,
    y_send, y_recv, relay_sems, core_sems, z_send, z_recv, zr_sems, x_send, x_recv,
    gy_send, gy_recv, ring_send, ring_recv, gc_send, gc_recv, in_sems,
    hop1_send, hop1_recv, hop2_send, hop2_recv,
):
    rx, win = lax.axis_index("rx"), lax.axis_index("win")
    core, z, x_lo, y = rx % 2, (rx // 2) % NZ, (rx // 16) % 2, rx // 32

    def at(y_=y, x_=x_lo, z_=z, core_=core, win_=win):
        return {"rx": ((y_ * 2 + x_) * NZ + z_) * 2 + core_, "win": win_}

    def remote(src, dst, send, recv, device):
        return pltpu.make_async_remote_copy(
            src_ref=src, dst_ref=dst, send_sem=send, recv_sem=recv, device_id=device, device_id_type=MESH
        )

    def arrived(ref, recv):
        remote(ref, ref, recv, recv, at()).wait_recv()


    loads = [
        pltpu.make_async_copy(spec_ref, near, in_sems.at[0]),
        pltpu.make_async_copy(plan_hbm, plan_ref, in_sems.at[1]),
    ]
    for load in loads:
        load.start()

    plus = at(x_=1 - x_lo, win_=(win + x_lo) % 2)
    minus = at(x_=1 - x_lo, win_=(win + 1 - x_lo) % 2)
    ys = [(y + d) % NY for d in range(1, NY)]
    zs = [(z + d) % NZ for d in range(1, NZ)]
    peers = [at(y_=v) for v in ys] + [at(z_=v) for v in zs] + [at(core_=1 - core)]
    peers += [plus, minus, at(win_=1 - win), at(y_=ys[0], core_=1 - core), at(y_=ys[2], core_=1 - core)]
    barrier = pltpu.get_barrier_semaphore()
    for peer in peers:
        pl.semaphore_signal(barrier, inc=1, device_id=peer, device_id_type=MESH)
    pl.semaphore_wait(barrier, len(peers))

    sent = []

    def go(copy):
        copy.start()
        sent.append(copy)

    next_y, across, last_y = ys

    def hop1(i):
        go(remote(spec_ref.at[i], transit_p.at[i], hop1_send.at[i], hop1_recv.at[i], plus))
        go(remote(spec_ref.at[4 + i], transit_m.at[i], hop1_send.at[4 + i], hop1_recv.at[4 + i], minus))

    go(remote(spec_ref.at[0:4, :, across], relay_p, relay_sems.at[0], relay_sems.at[1], at(y_=next_y)))
    go(remote(spec_ref.at[4:8, :, across], relay_m, relay_sems.at[2], relay_sems.at[3], at(y_=last_y)))
    hop1(0)
    mine = from_y.at[y, core]
    for h in range(2):
        go(remote(spec_ref.at[:, h, next_y], mine, y_send.at[0, h], y_recv.at[0, core], at(y_=next_y, core_=h)))
        go(remote(spec_ref.at[:, h, last_y], mine, y_send.at[1, h], y_recv.at[1, core], at(y_=last_y, core_=h)))
    go(remote(spec_ref.at[:, 1 - core, y], mine, core_sems.at[0], core_sems.at[1], at(core_=1 - core)))
    for i in range(1, 4):
        hop1(i)

    def window_pair(ref, side, first):
        def body(i, carry):
            both = [
                ref[2 * i + k].reshape(CH, 2 * NF).astype(jnp.float32).T.reshape(2, GROUPS, 8, CH) for k in range(2)
            ]
            a = jnp.concatenate([both[0][0], both[1][0]], 1).astype(jnp.bfloat16)
            b = jnp.concatenate([both[0][1], both[1][1]], 1)
            minus_b = (-b).astype(jnp.bfloat16)
            b = b.astype(jnp.bfloat16)
            row = pl.multiple_of(side * CH + 16 * i, 16)
            weights[:, pl.ds(row, 16), :CH] = a
            weights[:, pl.ds(HALF + row, 16), :CH] = b
            weights[:, pl.ds(row, 16), CH:] = minus_b
            weights[:, pl.ds(HALF + row, 16), CH:] = a
            return carry

        lax.fori_loop(0, 2, lambda i, carry: body(first + 2 * i, carry), 0, unroll=2)

    for load in loads:
        load.wait()
    from_y[y, core] = near[:, core, y]
    def forward(i):
        arrived(transit_p.at[i], hop1_recv.at[i])
        go(remote(transit_p.at[i], far.at[i], hop2_send.at[i], hop2_recv.at[i], plus))
        arrived(transit_m.at[i], hop1_recv.at[4 + i])
        go(remote(transit_m.at[i], far.at[4 + i], hop2_send.at[4 + i], hop2_recv.at[4 + i], minus))

    arrived(relay_p, relay_sems.at[1])
    place = from_y.at[last_y, core, 0:4]
    for h in range(2):
        go(remote(relay_p.at[:, h], place, y_send.at[2, h], y_recv.at[2, core], at(y_=next_y, core_=h)))
    arrived(relay_m, relay_sems.at[3])
    place = from_y.at[next_y, core, 4:8]
    for h in range(2):
        go(remote(relay_m.at[:, h], place, y_send.at[3, h], y_recv.at[3, core], at(y_=last_y, core_=h)))
    forward(0)
    window_pair(near, win, 0)
    forward(1)
    window_pair(near, win, 1)

    forward(2)
    forward(3)
    arrived(from_y.at[y, 1 - core], core_sems.at[1])
    for k in range(2):
        arrived(from_y.at[last_y, k], y_recv.at[0, k])
        arrived(from_y.at[next_y, k], y_recv.at[1, k])
        arrived(from_y.at[across, k, 0:4], y_recv.at[2, k])
        arrived(from_y.at[across, k, 4:8], y_recv.at[3, k])
    for b in range(2):
        oy, _, _, oc = owner_of(plan_ref, b)
        picked = jnp.transpose(from_y[oy, oc].astype(jnp.float32), (1, 0, 2))
        picked = jnp.concatenate([picked[:, :, :NF], picked[:, :, NF:]], 1)
        to_z[:, b] = picked.astype(jnp.bfloat16).reshape(NZ, 2, 16, NF)

    opposite, three_down, one_down = zs[3], zs[4], zs[6]
    go(remote(to_z.at[opposite, :, 1], relay_z, zr_sems.at[0], zr_sems.at[1], at(z_=three_down)))
    go(remote(to_z.at[opposite, :, 0], from_z.at[z, :, 0], z_send.at[3], z_recv.at[z], at(z_=opposite)))
    for d, v in enumerate(zs):
        if d != 3:
            go(remote(to_z.at[v], from_z.at[z], z_send.at[d], z_recv.at[z], at(z_=v)))
    from_z[z] = to_z[z]

    shape = (GROUPS * 16, NF)
    pick_group = (lax.broadcasted_iota(jnp.int32, shape, 1) >> 3) == (lax.broadcasted_iota(jnp.int32, shape, 0) >> 4)
    shape = (GROUPS * 16, CH)
    pick_row = (lax.broadcasted_iota(jnp.int32, shape, 1) >> 3) == (lax.broadcasted_iota(jnp.int32, shape, 0) & 15)
    f = lax.broadcasted_iota(jnp.int32, (NF, CH), 0)
    n = lax.broadcasted_iota(jnp.int32, (NF, CH), 1)
    same_place = ((f & 7) == (n & 7)).astype(jnp.float32).astype(jnp.bfloat16)
    out_row = lax.broadcasted_iota(jnp.int32, (GROUPS, GROUPS * 16), 0)
    in_row = lax.broadcasted_iota(jnp.int32, (GROUPS, GROUPS * 16), 1)
    same_group = ((in_row >> 4) == out_row).astype(jnp.float32).astype(jnp.bfloat16)

    arrived(relay_z, zr_sems.at[1])
    go(remote(relay_z, from_z.at[zs[2], :, 1], zr_sems.at[2], zr_sems.at[3], at(z_=one_down)))
    for d, v in enumerate(zs):
        if d != 3:
            arrived(from_z.at[v], z_recv.at[v])
    arrived(from_z.at[opposite, :, 0], z_recv.at[opposite])
    arrived(from_z.at[opposite, :, 1], zr_sems.at[3])

    def regroup(i, carry):
        b, e = i // 2, i % 2
        rows = from_z[owner_of(plan_ref, b)[2], b, e].astype(jnp.float32).reshape(1, 16, NF)
        rows = jnp.broadcast_to(rows, (GROUPS, 16, NF)).reshape(GROUPS * 16, NF)
        rows = jnp.where(pick_group, rows, 0.0).astype(jnp.bfloat16)
        moved = jnp.dot(rows, same_place, preferred_element_type=jnp.float32)
        moved = jnp.where(pick_row, moved, 0.0).astype(jnp.bfloat16)
        done = jnp.dot(same_group, moved, preferred_element_type=jnp.float32)
        to_x[b, e] = done.astype(jnp.bfloat16)
        return carry

    lax.fori_loop(0, 4, regroup, 0, unroll=2)

    active = win == core
    there = from_x.at[x_lo, win]
    go(remote(to_x, there, x_send.at[0], x_recv.at[x_lo, win], at(x_=1 - x_lo, win_=core)))

    def over():
        return remote(to_x, there, x_send.at[1], x_recv.at[x_lo, win], at(win_=core))

    @pl.when(win != core)
    def _():
        over().start()

    def down(t):
        return (z + NZ - t) % NZ

    def up(t):
        return (z + t) % NZ

    def pieces(t):
        return [(0, 0), (0, 1), (1, 3), (1, 2)] if t == 3 else [(way, d) for d in (0, 1, 3, 2) for way in range(2)]

    def piece(t, way, d):
        return gathered.at[down(t) if way == 0 else up(t), (y + d) % NY]

    def ring_piece(t, way, d):
        ref = piece(t, way, d)
        return remote(ref, ref, ring_send.at[way, t, d], ring_recv.at[way, t, d], at(z_=up(1) if way == 0 else down(1)))

    def pass_on(t, way, d):
        ref = piece(t, way, d)
        slot = down(t) if way == 0 else up(t)
        return remote(ref, ref, gc_send.at[slot, d], gc_recv.at[slot, d], at(core_=1 - core))

    def passed(t):
        return [(0, d) for d in (0, 1, 3, 2)] if t in (0, 4) else [(way, d) for d in (0, 1, 3, 2) for way in range(2)]

    own = gathered.at[z, y]

    def over_y():
        return [remote(own, own, gy_send.at[d], gy_recv.at[y], at(y_=v)) for d, v in enumerate(ys)]

    @pl.when(active)
    def _():
        from_x[x_lo, win] = to_x[...]
        arrived(from_x.at[1 - x_lo, win], x_recv.at[1 - x_lo, win])
        arrived(from_x.at[0, 1 - win], x_recv.at[0, 1 - win])
        arrived(from_x.at[1, 1 - win], x_recv.at[1, 1 - win])

        for b in range(2):
            ox = owner_of(plan_ref, b)[1]
            for w in range(2):
                gathered[z, y, b, :, :, w * CH : (w + 1) * CH] = from_x[ox, w, b]
        for copy in over_y():
            copy.start()
        for way in range(2):
            ring_piece(0, way, 0).start()
        pass_on(0, 0, 0).start()

    for first in range(2):
        for i in (2 * first, 2 * first + 1):
            arrived(far.at[i], hop2_recv.at[i])
            arrived(far.at[4 + i], hop2_recv.at[4 + i])
        window_pair(far, 1 - win, first)

    lane = lax.broadcasted_iota(jnp.int32, (1, 8, 2 * CH), 2)
    sub = lax.broadcasted_iota(jnp.int32, (1, 8, 2 * CH), 1)
    diagonal = (lane & 7) == sub

    def correlate(slots, part=None):
        count = len(slots)

        def unpack(v, carry):
            for i, slot in enumerate(slots):
                sources[i, v] = gathered[slot, v].astype(jnp.float32)
            return carry

        if part != 1:
            lax.fori_loop(0, NY, unpack, 0)

        def product(g):
            row = sources[:count, :, :, :, pl.ds(g, 1), :].reshape(count * 16, 1, 2 * CH)
            spread = jnp.where(diagonal, row, 0.0)
            spread = spread.reshape(count * 16 * 8, 2 * CH).astype(jnp.bfloat16)
            res = jnp.dot(spread, weights[g], preferred_element_type=jnp.float32)
            return res.reshape(count * 16, 8, 2 * CH)

        def bins(gg, carry):
            res = jnp.concatenate([product(2 * gg), product(2 * gg + 1)], 1)
            res = res.astype(jnp.bfloat16).reshape(count, NY, 2, 2, 16, 2 * CH)
            row = pl.multiple_of(gg * 16, 16)
            for i, slot in enumerate(slots):
                for b in range(2):
                    for c in range(2):
                        for s in range(2):
                            cross[b, :, slot, pl.ds(c * NF + row, 16), s * CH : (s + 1) * CH] = res[
                                i, :, b, s, :, c * CH : (c + 1) * CH
                            ]
            return carry

        quarter = GROUPS // 4
        lax.fori_loop(quarter if part == 1 else 0, quarter if part == 0 else 2 * quarter, bins, 0, unroll=4)

    def receive(t, late):
        for way, d in pieces(t - 1):
            if (d >= 2) == bool(late):
                arrived(piece(t, way, d), ring_recv.at[way, t - 1, d])
                if t < 4 and (way, d) in pieces(t):
                    ring_piece(t, way, d).start()
                pass_on(t, way, d).start()

    slots = [[z], [down(1), up(1)], [down(2), up(2)], [down(3), up(3)], [up(4)]]
    for t in range(5):

        @pl.when(active)
        def _():
            if t == 0:
                for d in (1, 3, 2):
                    arrived(piece(0, 0, d), gy_recv.at[(y + d) % NY])
                    for way in range(2):
                        ring_piece(0, way, d).start()
                    pass_on(0, 0, d).start()
            else:
                if t == 1:
                    receive(t, 0)
                receive(t, 1)

        @pl.when(win != core)
        def _():
            for way, d in passed(t):
                slot = down(t) if way == 0 else up(t)
                arrived(piece(t, way, d), gc_recv.at[slot, d])

        if 0 < t < 4:
            correlate(slots[t], 0)

            @pl.when(active)
            def _():
                receive(t + 1, 0)

            correlate(slots[t], 1)
        else:
            correlate(slots[t])

    for copy in sent:
        copy.wait_send()

    @pl.when(win != core)
    def _():
        over().wait_send()

    @pl.when(active)
    def _():
        for copy in over_y() + [pass_on(t, way, d) for t in range(5) for way, d in passed(t)]:
            copy.wait_send()
        for t in range(4):
            for way, d in pieces(t):
                ring_piece(t, way, d).wait_send()


def spread(plan, spectra):
    bf = jnp.bfloat16
    piece = (2, 16, NF)
    dma = pltpu.SemaphoreType.DMA
    natural = (2, NY, 16, 2 * NF)
    return pl.pallas_call(
        spread_kernel,
        out_shape=jax.ShapeDtypeStruct((2, NY, NZ, 2 * NF, 2 * CH), bf),
        in_specs=[pl.BlockSpec(memory_space=pltpu.HBM), pl.BlockSpec(memory_space=pltpu.HBM)],
        out_specs=pl.BlockSpec(memory_space=pltpu.VMEM),
        scratch_shapes=[
            pltpu.SMEM((2,), jnp.int32),
            pltpu.VMEM((8,) + natural, bf),
            pltpu.VMEM((8,) + natural, bf),
            pltpu.VMEM((NY, 2, 8, 16, 2 * NF), bf),
            pltpu.VMEM((4, 2, 16, 2 * NF), bf),
            pltpu.VMEM((4, 2, 16, 2 * NF), bf),
            pltpu.VMEM((NZ, 2) + piece, bf),
            pltpu.VMEM((NZ, 2) + piece, bf),
            pltpu.VMEM(piece, bf),
            pltpu.VMEM((2, 2, GROUPS, CH), bf),
            pltpu.VMEM((2, 2, 2, 2, GROUPS, CH), bf),
            pltpu.VMEM((NZ, NY, 2, 2, GROUPS, 2 * CH), bf),
            pltpu.VMEM((4,) + natural, bf),
            pltpu.VMEM((4,) + natural, bf),
            pltpu.VMEM((GROUPS, 2 * CH, 2 * CH), bf),
            pltpu.VMEM((2, NY, 2, 2, GROUPS, 2 * CH), jnp.float32),
            dma((4, 2)), dma((4, 2)), dma((4,)), dma((2,)), dma((7,)), dma((NZ,)), dma((4,)), dma((2,)), dma((2, 2)),
            dma((3,)), dma((NY,)), dma((2, 4, NY)), dma((2, 4, NY)), dma((NZ, NY)), dma((NZ, NY)), dma((2,)),
            dma((8,)), dma((8,)), dma((8,)), dma((8,)),
        ],
        compiler_params=pltpu.CompilerParams(
            collective_id=0, has_side_effects=True, vmem_limit_bytes=28 * 1024 * 1024
        ),
    )(
        pltpu.with_memory_space_constraint(plan, pltpu.HBM),
        pltpu.with_memory_space_constraint(spectra.reshape((8,) + natural), pltpu.HBM),
    )


def lag_kernel(cross, mask_ref, table_ref, out_ref, stage, out_sems):
    half = HALF // 2

    def result(p):
        slot = lax.rem(p, BUFFERS)
        place = out_ref.at[p // half, pl.ds(2 * lax.rem(p, half), 2)]
        return pltpu.make_async_copy(stage.at[slot], place, out_sems.at[slot])

    def batch(i, drain):
        pairs = [BATCH * i + k for k in range(BATCH)]
        if drain:
            for p in pairs:
                result(p - BUFFERS).wait()
        for p in pairs:
            b, row = p // half, 2 * lax.rem(p, half)
            lagged = jnp.dot(table_ref[...], cross[b, lax.rem(p, half)], preferred_element_type=jnp.float32)
            for s in range(2):
                keep = mask_ref[b, pl.ds(row + s, 1), :].astype(jnp.float32)
                kept = (lagged[:, s * CH : (s + 1) * CH] * keep).astype(jnp.bfloat16)
                stage[lax.rem(p, BUFFERS), s] = kept.T
        for p in pairs:
            result(p).start()

    def first(i, carry):
        batch(i, False)
        return carry

    def rest(i, carry):
        batch(i, True)
        return carry

    lax.fori_loop(0, 2, first, 0)
    lax.fori_loop(2, HALF // BATCH, rest, 0)
    for k in range(BUFFERS):
        result(HALF - BUFFERS + k).wait()


def lags(cross, mask):
    vmem = pl.BlockSpec(memory_space=pltpu.VMEM)
    return pl.pallas_call(
        lag_kernel,
        out_shape=jax.ShapeDtypeStruct((2, HALF, CH, LAGS), jnp.bfloat16),
        in_specs=[vmem, vmem, vmem],
        out_specs=pl.BlockSpec(memory_space=pltpu.HBM),
        scratch_shapes=[
            pltpu.VMEM((BUFFERS, 2, CH, LAGS), jnp.bfloat16),
            pltpu.SemaphoreType.DMA((BUFFERS,)),
        ],
        compiler_params=pltpu.CompilerParams(vmem_limit_bytes=28 * 1024 * 1024),
    )(cross.reshape(2, HALF // 2, 2 * NF, 2 * CH), mask, jnp.asarray(table_transposed()))


def on_device(spectra, plan, mask):
    return lags(spread(plan, spectra), mask)


def solution(mesh):
    return jax.shard_map(
        on_device,
        mesh=mesh,
        in_specs=(P("win", "rx", None), P(), P(None, "win", "rx")),
        out_specs=P(None, "win", "rx", None),
        check_vma=False,
    )
```
